256 devices in a mesh: pipe: 2 (over y_hi), ctx: 16 (over z, core), exp: 8 (over y_lo, x).
Axes of the slice: x: 4, y: 4 (y_hi: 2, y_lo: 2; y = y_hi * 2 + y_lo), z: 8, core: 2. Of those that a mesh axis runs over, the one named last changes fastest.
Arguments:
- queries: bfloat16 [2, 2048, 64, 576], P('pipe', 'ctx', 'exp'), may hold values from -24 to 24
- latent_rows: bfloat16 [2, 2048, 576], P('pipe', 'ctx'), may hold values from -4 to 4
- doc_ids: int32 [2, 2048], P('pipe', 'ctx'), may hold values from 0 to 2, never falling along the last dimension, each value on 1 to 1024 neighbouring positions
- value_up: bfloat16 [2, 64, 512, 128], P('pipe', 'exp'), may hold values from -0.25 to 0.25
- out_proj: bfloat16 [2, 8192, 7168], P('pipe', 'exp', 'ctx'), may hold values from -0.0625 to 0.0625
- residual_in: bfloat16 [2, 2048, 7168], P('pipe', ('ctx', 'exp')), may hold values from -6 to 6
- norm_gain: float32 [2, 7168], P('pipe'), may hold values from 0.1 to 1.9
- expert_ids: int32 [2, 2048, 2], P('pipe', ('ctx', 'exp')), may hold values from 0 to 7, all different within a row; in each aligned block of 16 rows (0 to 15, 16 to 31, ..., all dimensions but the last counted through in order) at most 5 rows name the same one
- gate_weights: float32 [2, 2048, 2], P('pipe', ('ctx', 'exp')), may hold values from 0.1 to 1
- gate_proj: bfloat16 [2, 8, 7168, 2048], P('pipe', 'exp', None, 'ctx'), may hold values from -0.0625 to 0.0625
- up_proj: bfloat16 [2, 8, 7168, 2048], P('pipe', 'exp', None, 'ctx'), may hold values from -0.0625 to 0.0625
- down_proj: bfloat16 [2, 8, 2048, 7168], P('pipe', 'exp', 'ctx'), may hold values from -0.125 to 0.125
Outputs:
- handed: bfloat16 [2, 2048, 7168], P('pipe', ('ctx', 'exp'))
The draws below stay inside these ranges and needn't reach their ends.
Inputs may be any that keep to these rules, and one draw needn't show every extreme that they name: `doc_ids`: within each section the ids never fall; each of the 3 documents holds 1 to 1024 positions, and one holds exactly 1024. `expert_ids`: each token names 2 different experts. Among the 16 tokens of one device no expert is named by more than 5 tokens, a bound that some block reaches.
All inputs are finite; a program needn't handle non-finite values.
Results may differ from the reference program's by a relative error of at most 0.02.
Values may be sent and summed in bfloat16 or wider, within the bound.
A program may use at most 64 MiB of HBM per device.

```python
import math
import jax
import jax.numpy as jnp
import numpy as np
from jax import lax

D = 7168
H = 64
HD = 128
ROPE = 64
LAT = 512
FF = 2048
TOP = 2
DOCS = 3
KV = 576
SECTIONS = 2
SEQ = 2048
TOK_DEV = 16
EXPERTS = 8
CAP = 5
N_CTX = 16


def latent_law(key, pick_rate):
    base_key = jax.random.fold_in(key, 5)
    normal_part = jnp.clip(jax.random.normal(jax.random.fold_in(base_key, 1), (SECTIONS, SEQ, KV), jnp.float32), -4.0, 4.0)
    values = normal_part
    chosen = jax.random.uniform(jax.random.fold_in(base_key, 3), (SECTIONS, SEQ), jnp.float32) < pick_rate
    chosen = chosen & (jnp.arange(SEQ)[None, :] >= 1)
    following = jnp.roll(values, -1, axis=1)
    chosen_next = jnp.roll(chosen, -1, axis=1)
    values = jnp.where(chosen_next[:, :, None], jnp.clip(following, -4.0, 4.0), values)
    return (values, chosen)


def draw_latent_rows(key, part):
    values, chosen = latent_law(key, 0.0)
    return values.astype(jnp.bfloat16)


def draw_queries(key, part):
    values, chosen = latent_law(key, 0.0)
    key = jax.random.fold_in(key, 31)
    drawn_rows = 2.0 * jnp.clip(jax.random.normal(jax.random.fold_in(key, 1), (SECTIONS, SEQ, H, KV), jnp.float32), -4.0, 4.0)
    strength = jax.random.uniform(jax.random.fold_in(key, 2), (SECTIONS, 1, H, 1), jnp.float32, 3.0, 6.0)
    aligned = strength * values[:, :, None, :]
    return jnp.where(chosen[:, :, None, None], aligned, drawn_rows).astype(jnp.bfloat16)


def shard_levels(key, shape, pieces, low, top_value):
    def one(position, parts):
        heights = jax.random.uniform(jax.random.fold_in(jax.random.fold_in(key, 6), position), (parts,), jnp.float32, low / len(pieces), top_value / len(pieces))
        return jnp.repeat(jnp.exp(heights), shape[position] // parts).reshape((-1,) + (1,) * (len(shape) - position - 1))

    loudness = one(*pieces[0])
    for cut in pieces[1:]:
        loudness = loudness * one(*cut)
    return loudness


def profile(amount, total, limit, slope):
    portions = [(1 << 20) // math.isqrt(rank ** slope) + 1 for rank in range(2, amount + 1)]
    surplus, given = total - limit - (amount - 1), [1] * (amount - 1)
    while surplus > 0:
        movable = [i for i in range(amount - 1) if given[i] < limit]
        pool, remaining = sum([portions[i] for i in movable]), surplus
        for i in movable:
            extra = min(limit - given[i], max(1, remaining * portions[i] // pool), surplus)
            given[i] = given[i] + extra
            surplus = surplus - extra
    return np.array([limit] + given)


def uneven_parts(key, amount, total, most, skew):
    if amount == 2:
        one = jax.random.randint(key, (), max(1, total - most), min(most, total - 1) + 1)
        return jnp.stack([one, total - one])
    sizes = jnp.asarray(profile(amount, total, most, skew), jnp.int32)
    twos = (amount - 1) // 2
    source_of, taker = sizes[1:1 + 2 * twos:2], sizes[2:2 + 2 * twos:2]
    room = jnp.minimum(source_of - 1, most - taker)
    shifted = jax.random.randint(jax.random.fold_in(key, 1), (twos,), 0, 1 << 20) % (room + 1)
    sizes = sizes.at[1:1 + 2 * twos:2].set(source_of - shifted).at[2:2 + 2 * twos:2].set(taker + shifted)
    return sizes[jax.random.permutation(jax.random.fold_in(key, 2), amount)]


def deal_out(stream_key, own, number, rows, number_of, top, most, slope):
    ranking = jax.random.permutation(stream_key, number_of)
    heavy_load, common = portions_of(number_of, rows * top, most, slope, True), portions_of(number_of, rows * top, most, slope, False)
    places = jnp.arange(number_of)

    def named(sizes, rotation):
        used = int((sizes > 0).sum())
        fixed = max(1, used // 4)
        shifted = fixed + (places - fixed + rotation * (used - fixed)) % max(1, number_of - fixed)
        return jnp.zeros((number_of,), jnp.int32).at[ranking[jnp.where(places < fixed, places, shifted)]].set(jnp.asarray(sizes, jnp.int32))

    sizes = jnp.where(number % 4 == 0, named(heavy_load, number // 4), named(common, number - number // 4 - 1))
    mixed = jax.random.permutation(jax.random.fold_in(own, 3), number_of)
    giver, taker = mixed[0:number_of // 2 * 2:2], mixed[1:number_of // 2 * 2:2]
    room = jnp.minimum(sizes[giver] - 1, most - sizes[taker]) // 2
    room = jnp.where((giver == ranking[0]) | (taker == ranking[0]) | (sizes[taker] == 0), 0, jnp.maximum(room, 0))
    shifted = jax.random.randint(jax.random.fold_in(own, 4), (number_of // 2,), 0, 1 << 20) % (room + 1)
    sizes = sizes.at[giver].add(-shifted).at[taker].add(shifted)
    members = jnp.searchsorted(jnp.cumsum(sizes), jnp.arange(rows * top), side="right").astype(jnp.int32)
    listing = members.reshape(top, rows).T
    listing = listing[jax.random.permutation(jax.random.fold_in(own, 1), rows)]
    rotation = jax.random.randint(jax.random.fold_in(own, 2), (rows, 1), 0, top)
    return jnp.take_along_axis(listing, (jnp.arange(top)[None, :] + rotation) % top, axis=1)


def portions_of(count, total, reach, lean, full):
    weights = [(1 << 20) // math.isqrt(standing ** lean) + 1 for standing in range(1, count + 1)]
    largest = reach if full else min(reach, max(-(-total // count), total * weights[0] // sum(weights)))
    least = 1 if total - largest >= count - 1 else 0
    given, spare = [largest] + [least] * (count - 1), total - largest - least * (count - 1)
    while spare > 0:
        candidates = [i for i in range(1, count) if given[i] < largest] or [i for i in range(1, count) if given[i] < reach]
        pool, budget = sum([weights[i] for i in candidates]), spare
        for i in candidates:
            more = min(reach - given[i], max(1, budget * weights[i] // pool), spare)
            given[i] = given[i] + more
            spare = spare - more
    return np.array(given)


def bell_draw(stream_key, shape, deviation, most, cuts=(), kind=jnp.bfloat16):
    array = jax.random.normal(stream_key, shape, jnp.float32) * deviation
    if len(cuts) > 0:
        array = shard_levels(stream_key, shape, cuts, -0.22, 0.18) * array
    return jnp.clip(array, min=-most, max=most).astype(kind)


def setup_inputs(seed: int = 0) -> dict:
    key_of = jax.random.split(jax.random.key(seed), 13)
    queries = draw_queries(jax.random.fold_in(key_of[12], 71), 0)
    latent_rows = draw_latent_rows(jax.random.fold_in(key_of[12], 71), 0)
    doc_ids = jax.vmap(lambda own: jnp.searchsorted(jnp.cumsum(uneven_parts(own, DOCS, SEQ, SEQ // 2, 0)), jnp.arange(SEQ), side="right"))(jax.random.split(key_of[2], SECTIONS)).reshape((SECTIONS, SEQ)).astype(jnp.int32)
    value_up = bell_draw(key_of[3], (SECTIONS, H, LAT, HD), LAT ** -0.5, 0.25, ((0, 2), (1, 8)))
    out_proj = bell_draw(key_of[4], (SECTIONS, H * HD, D), (H * HD) ** -0.5, 0.0625, ((0, 2), (1, 8), (2, 16)))
    residual_in = bell_draw(key_of[5], (SECTIONS, SEQ, D), 1.0, 6.0, ((0, 2), (1, 128)))
    norm_gain = jnp.clip(1.0 + 0.18 * jax.random.normal(key_of[6], (SECTIONS, D), jnp.float32), 0.1, 1.9)
    expert_ids_keys = jax.random.split(jax.random.fold_in(key_of[7], 1), SECTIONS * SEQ // TOK_DEV)
    expert_ids_turns = jax.random.permutation(jax.random.fold_in(key_of[7], 3), SECTIONS * SEQ // TOK_DEV)
    expert_ids = jax.vmap(lambda own, number: deal_out(jax.random.fold_in(key_of[7], 2), own, number, TOK_DEV, EXPERTS, TOP, CAP, 2))(expert_ids_keys, expert_ids_turns).reshape((SECTIONS, SEQ, TOP))
    gate_weights = jnp.clip(0.1 + 0.9 * jax.random.uniform(key_of[8], (SECTIONS, SEQ, TOP), jnp.float32) ** shard_levels(key_of[8], (SECTIONS, SEQ, TOP), ((0, 2), (1, 128)), -0.2, 0.2), 0.1, 1.0)
    gate_proj = bell_draw(key_of[9], (SECTIONS, EXPERTS, D, FF), D ** -0.5, 0.0625, ((0, 2), (1, 8), (3, 16)))
    up_proj = bell_draw(key_of[10], (SECTIONS, EXPERTS, D, FF), D ** -0.5, 0.0625, ((0, 2), (1, 8), (3, 16)))
    down_proj = bell_draw(key_of[11], (SECTIONS, EXPERTS, FF, D), FF ** -0.5, 0.125, ((0, 2), (1, 8), (2, 16)))
    return {"queries": queries, "latent_rows": latent_rows, "doc_ids": doc_ids, "value_up": value_up, "out_proj": out_proj, "residual_in": residual_in, "norm_gain": norm_gain, "expert_ids": expert_ids, "gate_weights": gate_weights, "gate_proj": gate_proj, "up_proj": up_proj, "down_proj": down_proj}


epsilon = 1e-06
masked_score = -1e+30

def section_layer(queries, latent_rows, doc_ids, value_up, out_proj, residual_in, norm_gain, expert_ids, gate_weights, gate_proj, up_proj, down_proj):
    positions = jnp.arange(SEQ, dtype=jnp.int32)
    allowed = (positions[None, :] <= positions[:, None]) & (doc_ids[None, :] == doc_ids[:, None])
    score_scale = 1.0 / math.sqrt(HD + ROPE)

    def one_head(head_args):
        query_head, up_head = head_args
        scores = jnp.dot(query_head, latent_rows.T, preferred_element_type=jnp.float32) * score_scale
        scores = jnp.where(allowed, scores, masked_score)
        highest = lax.optimization_barrier(jnp.max(scores, axis=1, keepdims=True))
        weights_now = jnp.where(allowed, jnp.exp(scores - highest), 0.0)
        totals = lax.optimization_barrier(jnp.sum(weights_now, axis=1, keepdims=True))
        mixed = jnp.dot(weights_now.astype(jnp.bfloat16), latent_rows[:, :LAT], preferred_element_type=jnp.float32)
        latent_out = (mixed / totals).astype(jnp.bfloat16)
        return jnp.dot(latent_out, up_head, preferred_element_type=jnp.float32).astype(jnp.bfloat16)
    heads = lax.map(one_head, (jnp.swapaxes(queries, 0, 1), value_up))
    heads = jnp.swapaxes(heads, 0, 1).reshape(SEQ, H * HD)
    attention = jnp.dot(heads, out_proj, preferred_element_type=jnp.float32).astype(jnp.bfloat16)
    stream = (residual_in.astype(jnp.float32) + attention.astype(jnp.float32)).astype(jnp.bfloat16)
    stream = lax.optimization_barrier(stream)
    stream_wide = stream.astype(jnp.float32)
    mean_square = lax.optimization_barrier(jnp.mean(stream_wide * stream_wide, axis=1, keepdims=True))
    normed = (stream_wide * lax.rsqrt(mean_square + epsilon) * norm_gain[None, :]).astype(jnp.bfloat16)
    block_count = SEQ // TOK_DEV
    grouped = expert_ids.reshape(block_count, TOK_DEV * TOP)
    matches = (grouped[:, :, None] == jnp.arange(EXPERTS, dtype=jnp.int32)[None, None, :]).astype(jnp.int32)
    running_count = jnp.cumsum(matches, axis=1).astype(jnp.int32)
    earlier = lax.optimization_barrier(jnp.sum((running_count - matches) * matches, axis=2)).astype(jnp.int32)
    slot_index = (jnp.arange(block_count, dtype=jnp.int32)[:, None] * CAP + earlier).astype(jnp.int32).reshape(SEQ, TOP)
    buffer_rows = jnp.zeros((EXPERTS, block_count * CAP, D), jnp.bfloat16)
    buffer_rows = buffer_rows.at[expert_ids.reshape(-1), slot_index.reshape(-1)].set(jnp.repeat(normed, TOP, axis=0))

    def one_expert(expert_args):
        rows_in, gate_cols, up_cols, down_rows = expert_args
        gate_value = jnp.dot(rows_in, gate_cols, preferred_element_type=jnp.float32)
        up_value = jnp.dot(rows_in, up_cols, preferred_element_type=jnp.float32)
        hidden = (jax.nn.silu(gate_value) * up_value).astype(jnp.bfloat16)
        share = FF // N_CTX
        hidden_blocks = jnp.swapaxes(hidden.reshape(hidden.shape[0], N_CTX, share), 0, 1)
        down_blocks = down_rows.reshape(N_CTX, share, D)

        def add_block(running, block_args):
            hidden_block, down_block = block_args
            partial_out = jnp.dot(hidden_block, down_block, preferred_element_type=jnp.float32).astype(jnp.bfloat16)
            partial_out = lax.optimization_barrier(partial_out)
            return (running + partial_out.astype(jnp.float32), None)
        summed, unused = lax.scan(add_block, jnp.zeros((hidden.shape[0], D), jnp.float32), (hidden_blocks, down_blocks))
        return summed.astype(jnp.bfloat16)
    expert_out = lax.map(one_expert, (buffer_rows, gate_proj, up_proj, down_proj))
    picked = expert_out[expert_ids, slot_index]
    combined = lax.optimization_barrier(jnp.sum(gate_weights[:, :, None] * picked.astype(jnp.float32), axis=1))
    return (stream_wide + combined).astype(jnp.bfloat16)

def reference(queries, latent_rows, doc_ids, value_up, out_proj, residual_in, norm_gain, expert_ids, gate_weights, gate_proj, up_proj, down_proj):
    outputs = []
    for section_num in range(SECTIONS):
        outputs.append(section_layer(queries[section_num], latent_rows[section_num], doc_ids[section_num], value_up[section_num], out_proj[section_num], residual_in[section_num], norm_gain[section_num], expert_ids[section_num], gate_weights[section_num], gate_proj[section_num], up_proj[section_num], down_proj[section_num]))
    layer_out = jnp.stack(outputs)
    return jnp.roll(layer_out, 1, axis=0)
```

```python
import math

import jax
import jax.numpy as jnp
import numpy as np
from jax import lax
from jax.experimental import pallas as pl
from jax.experimental.pallas import tpu as pltpu
from jax.sharding import PartitionSpec as P

D = 7168
HD = 128
ROPE = 64
LAT = 512
TOP = 2


epsilon = 1e-06
masked_score = -1e30
HALF = D // 2
MESH = pl.DeviceIdType.MESH


def remote(src, dst, send_sem, recv_sem, **device):
    return pltpu.make_async_remote_copy(
        src_ref=src,
        dst_ref=dst,
        send_sem=send_sem,
        recv_sem=recv_sem,
        device_id=device,
        device_id_type=MESH,
    )


def meet(peers):
    barrier = pltpu.get_barrier_semaphore()
    for device in peers:
        pl.semaphore_signal(barrier, 1, device_id=device, device_id_type=MESH)
    pl.semaphore_wait(barrier, len(peers))


def squeeze_map(rows, groups, group, dtype=jnp.bfloat16):
    row = lax.broadcasted_iota(jnp.int32, (80, 8 * rows), 0).astype(jnp.float32)
    col = lax.broadcasted_iota(jnp.int32, (80, 8 * rows), 1).astype(jnp.float32)
    source = jnp.floor((row + 0.5) * 0.1)
    want = source * rows + (row - source * 10) + group * 10
    return jnp.where(col == want, 1.0, 0.0).astype(dtype)


def spread_map(rows, groups, group, dtype=jnp.bfloat16):
    row = lax.broadcasted_iota(jnp.int32, (8 * rows, 80), 0).astype(jnp.float32)
    col = lax.broadcasted_iota(jnp.int32, (8 * rows, 80), 1).astype(jnp.float32)
    source = jnp.floor((col + 0.5) * 0.1)
    want = source * rows + (col - source * 10) + group * 10
    return jnp.where(row == want, 1.0, 0.0).astype(dtype)


PARTS = ((0, 4, 48), (4, 3, 32))
PIECES = ((0, 1024), (1024, 1024), (2048, 768), (2816, 768))
SUBS = ((0, 896), (896, 896), (1792, 896), (2688, 896))


def expert_kernel(
    stream_ref, gain_ref, sel0, sel1, mix0, mix1, gate_ref, up_ref, down_ref, out_ref,
    normed, pn, ps, xg0, xg1, sg0, sg1, outbox0, outbox1, inbox0, inbox1, w_in, w_down,
    rows, half, half_other, total, arrived, summed, ret0, ret1, back0, back1, ready, landed,
    pair_s, pair_r, loc, box_s, box_r, ag_s, ag_r, half_s, half_r, rs_s, rs_r, back_s, back_r, fin_s, fin_r,
):
    p, c, e = lax.axis_index("pipe"), lax.axis_index("ctx"), lax.axis_index("exp")
    k = lax.rem(c, 2)
    z = lax.div(c, 2)
    kk = 1 - k
    other = 2 * z + kk
    right = 2 * lax.rem(z + 1, 8) + k
    left = 2 * lax.rem(z + 7, 8) + k
    over = 1 - p
    mine = pl.multiple_of(k * HALF, 128)
    theirs = pl.multiple_of(kk * HALF, 128)
    my_lane = pl.multiple_of(k * 128, 128)
    up_lane = pl.multiple_of(256 + k * 128, 128)

    local = [
        pltpu.make_async_copy(gate_ref.at[pl.ds(mine, HALF), :], w_in.at[:, pl.ds(my_lane, 128)], loc.at[0]),
        pltpu.make_async_copy(up_ref.at[pl.ds(mine, HALF), :], w_in.at[:, pl.ds(up_lane, 128)], loc.at[1]),
        pltpu.make_async_copy(down_ref.at[:, pl.ds(mine, HALF)], w_down.at[pl.ds(my_lane, 128), :], loc.at[2]),
    ]
    for copy in local:
        copy.start()

    wide = stream_ref[...].astype(jnp.float32)
    mean_square = jnp.mean(wide * wide, axis=1, keepdims=True)
    normed[...] = (wide * lax.rsqrt(mean_square + epsilon) * gain_ref[...]).astype(jnp.bfloat16)

    meet(
        [{"ctx": other}, {"ctx": right}, {"ctx": left}]
        + [{"exp": lax.rem(e + i, 8)} for i in range(1, 8)]
        + [{"pipe": over}, {"pipe": over, "ctx": other}]
    )
    pair = [
        remote(normed.at[:, pl.ds(theirs, HALF)], pn, pair_s.at[0], pair_r.at[0], ctx=other),
        remote(stream_ref.at[:, pl.ds(theirs, HALF)], ps, pair_s.at[1], pair_r.at[1], ctx=other),
        remote(gate_ref.at[pl.ds(theirs, HALF), :], w_in.at[:, pl.ds(my_lane, 128)], pair_s.at[2], pair_r.at[2], ctx=other),
        remote(up_ref.at[pl.ds(theirs, HALF), :], w_in.at[:, pl.ds(up_lane, 128)], pair_s.at[3], pair_r.at[3], ctx=other),
        remote(down_ref.at[:, pl.ds(theirs, HALF)], w_down.at[pl.ds(my_lane, 128), :], pair_s.at[4], pair_r.at[4], ctx=other),
    ]
    for copy in pair:
        copy.start()
    my_rows = [pl.multiple_of(g * 32 + k * 16, 16) for g in range(4)]
    their_rows = [pl.multiple_of(g * 32 + kk * 16, 16) for g in range(4)]
    xgs, sgs = (xg0, xg1), (sg0, sg1)
    for part, (first, groups, _) in enumerate(PARTS):
        for g in range(groups):
            lanes = pl.ds(pl.multiple_of(mine + (first + g) * 512, 128), 512)
            xgs[part][pl.ds(my_rows[g], 16), :] = normed[:, lanes]
            sgs[part][pl.ds(my_rows[g], 16), :] = stream_ref[:, lanes]
    pair[0].wait_recv()
    outboxes, inboxes, sels = (outbox0, outbox1), (inbox0, inbox1), (sel0, sel1)

    def box(part, i):
        return remote(
            outboxes[part].at[lax.rem(e + i, 8)], inboxes[part].at[e], box_s.at[part, i], box_r.at[part, i],
            exp=lax.rem(e + i, 8),
        )

    def box_in(part, i):
        source = lax.rem(e + 8 - i, 8)
        return remote(outboxes[part].at[source], inboxes[part].at[source], box_s.at[part, i], box_r.at[part, i], exp=source)

    for part, (first, groups, height) in enumerate(PARTS):
        for g in range(groups):
            lanes = slice((first + g) * 512, (first + g + 1) * 512)
            xgs[part][pl.ds(their_rows[g], 16), :] = pn[:, lanes]
        chosen = jnp.dot(sels[part][...], xgs[part][...], preferred_element_type=jnp.float32).astype(jnp.bfloat16)
        outboxes[part][...] = chosen.reshape(8, height, 512)
        for i in range(1, 8):
            box(part, i).start()
        inboxes[part][pl.ds(e, 1)] = outboxes[part][pl.ds(e, 1)]

    pair[1].wait_recv()
    for part, (first, groups, _) in enumerate(PARTS):
        for g in range(groups):
            lanes = slice((first + g) * 512, (first + g + 1) * 512)
            sgs[part][pl.ds(their_rows[g], 16), :] = ps[:, lanes]

    def gather(d, q, r):
        columns = pl.ds(PIECES[q][0], PIECES[q][1])
        if d == 0:
            return remote(rows.at[r - 1, :, columns], rows.at[r, :, columns], ag_s.at[d, q, r], ag_r.at[d, q, r], ctx=right)
        return remote(
            rows.at[lax.rem(9 - r, 8), :, columns], rows.at[8 - r, :, columns], ag_s.at[d, q, r], ag_r.at[d, q, r], ctx=left
        )

    def reach(d, q):
        return 4 if (q % 2 == 0) == (d == 0) else 3

    for part, (first, groups, height) in enumerate(PARTS):
        for i in range(1, 8):
            box_in(part, i).wait_recv()
        landed_rows = inboxes[part][...].reshape(8 * height, 512)
        for g in range(groups):
            rows[0, :, (first + g) * 512 : (first + g + 1) * 512] = jnp.dot(
                squeeze_map(height, groups, g), landed_rows, preferred_element_type=jnp.float32
            ).astype(jnp.bfloat16)
        for q in (2 * part, 2 * part + 1):
            for d in range(2):
                gather(d, q, 1).start()
    for copy in local:
        copy.wait()
    for copy in pair[2:]:
        copy.wait_recv()

    def swap(slot):
        return remote(half.at[slot], half_other.at[slot], half_s.at[slot], half_r.at[slot], ctx=other)

    def first_half(slot):
        half[slot] = jnp.dot(rows[slot], w_in[...], preferred_element_type=jnp.float32)
        swap(slot).start()

    def second_half(slot):
        swap(slot).wait_recv()
        both = half[slot] + half_other[slot]
        gate = both[:, :256]
        hidden = (gate / (1.0 + jnp.exp(-gate)) * both[:, 256:]).astype(jnp.bfloat16)
        total[slot] = jnp.dot(hidden, w_down[...], preferred_element_type=jnp.float32).astype(jnp.bfloat16)

    first_half(0)
    second_half(0)

    def pass_on(m, step):
        columns = pl.ds(SUBS[m][0], SUBS[m][1])
        slot = step + 1 if m < 2 else 7 - step
        return remote(
            total.at[slot, :, columns], arrived.at[m, step], rs_s.at[m, step], rs_r.at[m, step], ctx=right if m < 2 else left
        )

    def turn(r, carry):
        @pl.when(r <= 4)
        def _():
            for q in range(4):
                for d in range(2):
                    @pl.when(r <= reach(d, q))
                    def _(d=d, q=q):
                        gather(d, q, r).wait_recv()

                    @pl.when(r + 1 <= reach(d, q))
                    def _(d=d, q=q):
                        gather(d, q, r + 1).start()

            first_half(r)

            @pl.when(r < 4)
            def _():
                first_half(8 - r)

            second_half(r)

            @pl.when(r < 4)
            def _():
                second_half(8 - r)

        for m in (0, 2, 1, 3):
            slot = r if m < 2 else 8 - r
            columns = pl.ds(SUBS[m][0], SUBS[m][1])

            @pl.when(r >= 2)
            def _(m=m, slot=slot, columns=columns):
                pass_on(m, r - 2).wait_recv()
                total[slot, :, columns] = (
                    total[slot, :, columns].astype(jnp.float32) + arrived[m, r - 2].astype(jnp.float32)
                ).astype(jnp.bfloat16)

            pass_on(m, r - 1).start()
        return carry

    lax.fori_loop(1, 8, turn, 0)
    for m in (0, 2, 1, 3):
        pass_on(m, 6).wait_recv()
        columns = slice(SUBS[m][0], SUBS[m][0] + SUBS[m][1])
        summed[:, columns] = (total[0, :, columns].astype(jnp.float32) + arrived[m, 6].astype(jnp.float32)).astype(jnp.bfloat16)

    rets, backs, mixes, readies = (ret0, ret1), (back0, back1), (mix0, mix1), ready

    def give(part, i):
        return remote(
            rets[part].at[lax.rem(e + i, 8)], backs[part].at[e], back_s.at[part, i], back_r.at[part, i], exp=lax.rem(e + i, 8)
        )

    def give_in(part, i):
        source = lax.rem(e + 8 - i, 8)
        return remote(rets[part].at[source], backs[part].at[source], back_s.at[part, i], back_r.at[part, i], exp=source)

    for part, (first, groups, height) in enumerate(PARTS):
        spread = jnp.zeros((8 * height, 512), jnp.float32)
        for g in range(groups):
            spread = spread + jnp.dot(
                spread_map(height, groups, g), summed[:, (first + g) * 512 : (first + g + 1) * 512],
                preferred_element_type=jnp.float32,
            )
        rets[part][...] = spread.astype(jnp.bfloat16).reshape(8, height, 512)
        for i in range(1, 8):
            give(part, i).start()
        backs[part][pl.ds(e, 1)] = rets[part][pl.ds(e, 1)]
    for part, (first, groups, height) in enumerate(PARTS):
        for i in range(1, 8):
            give_in(part, i).wait_recv()
        span = groups * 32
        mixed = jnp.dot(mixes[part][...], backs[part][...].reshape(8 * height, 512), preferred_element_type=jnp.float32)
        combined = mixed[:span] + mixed[span:]
        layer_out = (sgs[part][...].astype(jnp.float32) + combined).astype(jnp.bfloat16)
        for g in range(groups):
            for b in range(2):
                readies[b, :, (first + g) * 512 : (first + g + 1) * 512] = layer_out[g * 32 + b * 16 : g * 32 + b * 16 + 16]

    def hand(b, core):
        return remote(ready.at[b], landed.at[core], fin_s.at[b], fin_r.at[core], pipe=over, ctx=2 * z + b)

    for b in range(2):
        hand(b, k).start()
    for b in range(2):
        hand(b, b).wait_recv()
        out_ref[:, b * HALF : (b + 1) * HALF] = landed[b]

    for b in range(2):
        hand(b, k).wait_send()
    for copy in pair:
        copy.wait_send()
    for part in range(2):
        for i in range(1, 8):
            box(part, i).wait_send()
            give(part, i).wait_send()
    for q in range(4):
        for d in range(2):
            def done(r, carry, d=d, q=q):
                gather(d, q, r).wait_send()
                return carry

            lax.fori_loop(1, reach(d, q) + 1, done, 0)

    def sent(step, carry):
        for m in range(4):
            pass_on(m, step).wait_send()
        return carry

    lax.fori_loop(0, 7, sent, 0)

    def swapped(slot, carry):
        swap(slot).wait_send()
        return carry

    lax.fori_loop(0, 8, swapped, 0)


def slot_tables(ids, weights):
    sels, mixes = [], []
    chosen = ids.reshape(2, 32)
    matches = (chosen[:, :, None] == jnp.arange(8, dtype=jnp.int32)).astype(jnp.int32)
    rank = jnp.sum((jnp.cumsum(matches, axis=1) - matches) * matches, axis=2)
    slot = (chosen * 8 + rank).reshape(32, 2)
    for first, groups, height in PARTS:
        row = np.arange(8 * height)
        inner = row % height
        row_group, row_block, row_slot = inner // 10, inner % 10 // 5, row // height * 8 + inner % 5
        row_slot = np.where(inner < groups * 10, row_slot, -1)
        col = np.arange(groups * 32)
        same = (row_group[:, None] == col[None, :] // 32) & (row_block[:, None] == col[None, :] % 32 // 16)
        tiled = jnp.tile(slot, (groups, 1))
        tiled_weights = jnp.tile(weights, (groups, 1))
        hit = (row_slot[:, None, None] == tiled[None]) & same[:, :, None]
        sels.append(jnp.any(hit, axis=2).astype(jnp.bfloat16))
        mix = jnp.sum(
            jnp.where((row_slot[None, :, None] == tiled[:, None]) & same.T[:, :, None], tiled_weights[:, None, :], 0.0), axis=2
        )
        high = mix.astype(jnp.bfloat16)
        low = (mix - high.astype(jnp.float32)).astype(jnp.bfloat16)
        mixes.append(jnp.concatenate([high, low], axis=0))
    return sels, mixes


def experts(stream, gain, ids, weights, gate_cols, up_cols, down_rows):
    packed = jnp.concatenate([ids.astype(jnp.float32), weights], axis=1)
    partner = lax.ppermute(packed, "ctx", [(i, i ^ 1) for i in range(16)])
    first = lax.rem(lax.axis_index("ctx"), 2) == 0
    low, high = jnp.where(first, packed, partner), jnp.where(first, partner, packed)
    both = jnp.concatenate([low, high], axis=0)
    (sel0, sel1), (mix0, mix1) = slot_tables(both[:, :2].astype(jnp.int32), both[:, 2:])
    bf, f32 = jnp.bfloat16, jnp.float32
    vmem, any_space = pl.BlockSpec(memory_space=pltpu.VMEM), pl.BlockSpec(memory_space=pl.ANY)
    dma = pltpu.SemaphoreType.DMA
    return pl.pallas_call(
        expert_kernel,
        out_shape=jax.ShapeDtypeStruct((16, D), bf),
        in_specs=[vmem] * 6 + [any_space] * 3,
        out_specs=vmem,
        scratch_shapes=[
            pltpu.VMEM((16, D), bf), pltpu.VMEM((16, HALF), bf), pltpu.VMEM((16, HALF), bf),
            pltpu.VMEM((128, 512), bf), pltpu.VMEM((96, 512), bf), pltpu.VMEM((128, 512), bf), pltpu.VMEM((96, 512), bf),
            pltpu.VMEM((8, 48, 512), bf), pltpu.VMEM((8, 32, 512), bf), pltpu.VMEM((8, 48, 512), bf), pltpu.VMEM((8, 32, 512), bf),
            pltpu.VMEM((HALF, 512), bf), pltpu.VMEM((256, HALF), bf),
            pltpu.VMEM((8, 80, HALF), bf), pltpu.VMEM((8, 80, 512), f32), pltpu.VMEM((8, 80, 512), f32),
            pltpu.VMEM((8, 80, HALF), bf), pltpu.VMEM((4, 7, 80, 896), bf), pltpu.VMEM((80, HALF), bf),
            pltpu.VMEM((8, 48, 512), bf), pltpu.VMEM((8, 32, 512), bf), pltpu.VMEM((8, 48, 512), bf), pltpu.VMEM((8, 32, 512), bf),
            pltpu.VMEM((2, 16, HALF), bf), pltpu.VMEM((2, 16, HALF), bf),
            dma((5,)), dma((5,)), dma((3,)), dma((2, 8)), dma((2, 8)), dma((2, 4, 5)), dma((2, 4, 5)), dma((8,)), dma((8,)),
            dma((4, 7)), dma((4, 7)), dma((2, 8)), dma((2, 8)), dma((2,)), dma((2,)),
        ],
        compiler_params=pltpu.CompilerParams(collective_id=3, has_side_effects=True, vmem_limit_bytes=56 << 20),
        cost_estimate=pl.CostEstimate(flops=3_600_000_000, bytes_accessed=6_000_000, transcendentals=164_000),
        name="experts",
    )(stream, gain, sel0, sel1, mix0, mix1, gate_cols, up_cols, down_rows)


def on_device(
    queries,
    latent_rows,
    doc_ids,
    value_up,
    out_proj,
    residual_in,
    norm_gain,
    expert_ids,
    gate_weights,
    gate_proj,
    up_proj,
    down_proj,
):
    ctx_count = lax.axis_size("ctx")
    exp_count = lax.axis_size("exp")
    ctx_rank = lax.axis_index("ctx")
    query_rows = queries[0]
    local_len = query_rows.shape[0]
    head_count = query_rows.shape[1]
    query_pos = ctx_rank * local_len + jnp.arange(local_len, dtype=jnp.int32)
    query_doc = doc_ids[0]
    score_scale = 1.0 / math.sqrt(HD + ROPE)
    start_top = jnp.full((head_count, local_len), masked_score, jnp.float32)
    start_sum = jnp.zeros((head_count, local_len), jnp.float32)
    start_acc = jnp.zeros((head_count, local_len, LAT), jnp.float32)
    key_rows = lax.all_gather(latent_rows[0], "ctx", axis=0, tiled=True)
    key_docs = lax.all_gather(doc_ids[0], "ctx", axis=0, tiled=True)
    key_span = key_rows.shape[0]

    def visit(current):
        running, totals, weighted = current
        key_pos = jnp.arange(key_span, dtype=jnp.int32)
        allowed = (key_pos[None, :] <= query_pos[:, None]) & (
            key_docs[None, :] == query_doc[:, None]
        )
        scores = (
            jnp.einsum("qhc,kc->hqk", query_rows, key_rows, preferred_element_type=jnp.float32)
            * score_scale
        )
        scores = jnp.where(allowed[None], scores, masked_score)
        highest = jnp.maximum(running, jnp.max(scores, axis=2))
        weights_now = jnp.where(allowed[None], jnp.exp(scores - highest[:, :, None]), 0.0)
        totals = jnp.sum(weights_now, axis=2)
        update = jnp.einsum(
            "hqk,kc->hqc",
            weights_now.astype(jnp.bfloat16),
            key_rows[:, :LAT],
            preferred_element_type=jnp.float32,
        )
        weighted = update
        return (highest, totals, weighted)

    running, totals, weighted = lax.cond(
        jnp.int32(0) <= query_pos[-1],
        visit,
        lambda current: current,
        (start_top, start_sum, start_acc),
    )
    latent_out = (weighted / totals[:, :, None]).astype(jnp.bfloat16)
    heads = jnp.einsum(
        "hqc,hcd->qhd", latent_out, value_up[0], preferred_element_type=jnp.float32
    ).astype(jnp.bfloat16)
    heads = heads.reshape(local_len, head_count * HD)
    everyone = lax.all_gather(heads, "ctx", axis=0, tiled=True)
    tok_count = local_len // exp_count
    grid_rows = everyone.reshape(ctx_count, exp_count, tok_count, head_count * HD)
    column_proj = out_proj[0]
    block_rows = ctx_count * tok_count
    picked = grid_rows
    picked = jnp.swapaxes(picked, 0, 1).reshape(block_rows * lax.axis_size("exp"), head_count * HD)
    attn_part = lax.psum_scatter(
        jnp.dot(picked, column_proj, preferred_element_type=jnp.float32).astype(jnp.bfloat16),
        "exp",
        scatter_dimension=0,
        tiled=True,
    )
    attention = lax.all_to_all(attn_part, "ctx", split_axis=0, concat_axis=1, tiled=True)
    stream = (residual_in[0].astype(jnp.float32) + attention.astype(jnp.float32)).astype(
        jnp.bfloat16
    )
    stream = lax.optimization_barrier(stream)
    return experts(stream, norm_gain, expert_ids[0], gate_weights[0], gate_proj[0, 0], up_proj[0, 0], down_proj[0, 0])[None]


def solution(mesh):
    return jax.shard_map(
        on_device,
        mesh=mesh,
        in_specs=(
            P("pipe", "ctx", "exp", None),
            P("pipe", "ctx", None),
            P("pipe", "ctx"),
            P("pipe", "exp", None, None),
            P("pipe", "exp", "ctx"),
            P("pipe", ("ctx", "exp"), None),
            P("pipe", None),
            P("pipe", ("ctx", "exp"), None),
            P("pipe", ("ctx", "exp"), None),
            P("pipe", "exp", None, "ctx"),
            P("pipe", "exp", None, "ctx"),
            P("pipe", "exp", "ctx", None),
        ),
        out_specs=P("pipe", ("ctx", "exp"), None),
        check_vma=False,
    )
```

```python
import math
import types

import jax
import jax.numpy as jnp
from jax import lax
from jax.experimental import pallas as pl
from jax.experimental.pallas import tpu as pltpu
from jax.sharding import PartitionSpec as P

D = 7168
HALF = D // 2
HD = 128
ROPE = 64
LAT = 512
KV = LAT + ROPE
MESH = pl.DeviceIdType.MESH

epsilon = 1e-06
masked_score = -1e30
score_scale = 1.0 / math.sqrt(HD + ROPE)


def remote(src, dst, send_sem, recv_sem, **device):
    return pltpu.make_async_remote_copy(
        src_ref=src,
        dst_ref=dst,
        send_sem=send_sem,
        recv_sem=recv_sem,
        device_id=device,
        device_id_type=MESH,
    )


def meet(peers):
    barrier = pltpu.get_barrier_semaphore()
    for device in peers:
        pl.semaphore_signal(barrier, 1, device_id=device, device_id_type=MESH)
    pl.semaphore_wait(barrier, len(peers))


def squeeze_map(rows, groups, group, dtype=jnp.bfloat16):
    row = lax.broadcasted_iota(jnp.int32, (80, 8 * rows), 0).astype(jnp.float32)
    col = lax.broadcasted_iota(jnp.int32, (80, 8 * rows), 1).astype(jnp.float32)
    source = jnp.floor((row + 0.5) * 0.1)
    want = source * rows + (row - source * 10) + group * 10
    return jnp.where(col == want, 1.0, 0.0).astype(dtype)


def spread_map(rows, groups, group, dtype=jnp.bfloat16):
    row = lax.broadcasted_iota(jnp.int32, (8 * rows, 80), 0).astype(jnp.float32)
    col = lax.broadcasted_iota(jnp.int32, (8 * rows, 80), 1).astype(jnp.float32)
    source = jnp.floor((col + 0.5) * 0.1)
    want = source * rows + (col - source * 10) + group * 10
    return jnp.where(row == want, 1.0, 0.0).astype(dtype)


PARTS = ((0, 4, 48), (4, 3, 32))
PIECES = ((0, 1024), (1024, 1024), (2048, 768), (2816, 768))
SUBS = ((0, 896), (896, 896), (1792, 896), (2688, 896))


def attend(w, q_ref, lat_ref, doc_ref, vu_ref, op_ref, residual_ref, start_rest):
    p, c, e = lax.axis_index("pipe"), lax.axis_index("ctx"), lax.axis_index("exp")
    k = lax.rem(c, 2)
    z = lax.div(c, 2)
    kk = 1 - k
    other = 2 * z + kk
    right = 2 * lax.rem(z + 1, 8) + k
    left = 2 * lax.rem(z + 7, 8) + k
    y = lax.div(e, 4)
    x = lax.rem(e, 4)
    bf, f32 = jnp.bfloat16, jnp.float32

    def chain(s, q):
        piece = pl.ds(q * 32, 32)
        return remote(w.keys.at[s - 1, k, piece], w.keys.at[s, k, piece], w.chain_s.at[s, q], w.chain_r.at[s, q], ctx=right)

    def share(s):
        return remote(w.keys.at[s, k], w.keys.at[s, k], w.share_s.at[s], w.share_r.at[s], ctx=other)

    def share_in(s):
        return remote(w.keys.at[s, kk], w.keys.at[s, kk], w.share_s.at[s], w.share_r.at[s], ctx=other)

    for q in range(4):
        chain(1, q).start()
    share(0).start()
    own_proj = pltpu.make_async_copy(op_ref, w.proj.at[k], w.load.at[8])
    own_proj.start()
    pair_proj = remote(op_ref, w.proj.at[k], w.proj_s.at[0], w.proj_r.at[0], ctx=other)
    pair_proj.start()
    up_loads = [
        pltpu.make_async_copy(vu_ref.at[h], w.value_up.at[:, pl.ds(h * 128, 128)], w.load.at[h]) for h in range(8)
    ]
    for copy in up_loads:
        copy.start()
    start_rest()

    def flatten(j, carry):
        block = q_ref[pl.ds(j * 16, 16)].astype(f32).reshape(128, KV)
        w.queries[pl.ds(pl.multiple_of(j * 128, 128), 128), :] = block.astype(bf)
        return carry

    lax.fori_loop(0, 8, flatten, 0)
    expand = lax.shift_right_logical(lax.broadcasted_iota(jnp.int32, (1024, 128), 0), 3) == lax.broadcasted_iota(
        jnp.int32, (1024, 128), 1
    )
    own_tail = w.keys[0, pl.ds(k, 1), :, 512:640].reshape(128, 128)
    own_docs = jnp.dot(jnp.where(expand, 1.0, 0.0).astype(bf), own_tail, preferred_element_type=f32)
    w.query_doc[...] = jnp.broadcast_to(own_docs[:, 64:65], (1024, 128))
    w.top[...] = jnp.full((1024, 128), masked_score, f32)
    w.sums[...] = jnp.zeros((1024, 128), f32)
    w.mixed[...] = jnp.zeros((1024, LAT), f32)
    picker = jnp.where(lax.broadcasted_iota(jnp.int32, (8, 128), 1) == 64, 1.0, 0.0).astype(bf)
    contract_last = (((1,), (1,)), ((), ()))

    def visit(s, carry):
        @pl.when(s >= 1)
        def _():
            for q in range(4):
                chain(s, q).wait_recv()

                @pl.when(s < 4)
                def _(q=q):
                    chain(s + 1, q).start()

            share(s).start()

        share_in(s).wait_recv()
        block = w.keys[s].reshape(256, 640)
        key_doc = lax.dot_general(picker, block[:, 512:640], contract_last, preferred_element_type=f32)[0:1]
        key_pos = lax.rem(z + 8 - s, 8) * 256 + lax.broadcasted_iota(jnp.int32, (256, 256), 1)

        def some(j, carry):
            at = pl.ds(pl.multiple_of(j * 256, 256), 256)
            scores = lax.dot_general(w.queries[at], block[:, :KV], contract_last, preferred_element_type=f32) * score_scale
            query_pos = c * 128 + j * 32 + lax.shift_right_logical(lax.broadcasted_iota(jnp.int32, (256, 256), 0), 3)
            query_doc = w.query_doc[at]
            allowed = (key_pos <= query_pos) & (jnp.concatenate([query_doc, query_doc], axis=1) == key_doc)
            scores = jnp.where(allowed, scores, masked_score)
            before = w.top[at]
            highest = jnp.maximum(before, jnp.max(scores, axis=1, keepdims=True))
            shrink = jnp.exp(before - highest)
            weights = jnp.where(allowed, jnp.exp(scores - jnp.concatenate([highest, highest], axis=1)), 0.0)
            w.top[at] = highest
            w.sums[at] = w.sums[at] * shrink + jnp.sum(weights, axis=1, keepdims=True)
            update = jnp.dot(weights.astype(bf), block[:, :LAT], preferred_element_type=f32)
            w.mixed[at] = w.mixed[at] * jnp.concatenate([shrink] * 4, axis=1) + update
            return carry

        lax.fori_loop(0, 4, some, 0)
        return carry

    lax.fori_loop(0, 5, visit, 0)

    for copy in up_loads:
        copy.wait()

    def gather(d, q, r):
        piece = pl.ds(q * 64, 64)
        if d == 0:
            return remote(w.heads.at[r - 1, piece], w.heads.at[r, piece], w.head_s.at[d, q, r], w.head_r.at[d, q, r], ctx=right)
        return remote(
            w.heads.at[lax.rem(9 - r, 8), piece], w.heads.at[8 - r, piece], w.head_s.at[d, q, r], w.head_r.at[d, q, r], ctx=left
        )

    def reach(d, q):
        return 4 if q == d else 3

    own_head = lax.shift_right_logical(lax.broadcasted_iota(jnp.int32, (256, 1024), 1), 7) == (
        lax.broadcasted_iota(jnp.int32, (256, 1024), 0) & 7
    )
    for q in range(2):
        def finish(j, carry):
            at = pl.ds(pl.multiple_of(j * 256, 256), 256)
            latent_out = (w.mixed[at] / jnp.concatenate([w.sums[at]] * 4, axis=1)).astype(bf)
            every = jnp.dot(latent_out, w.value_up[...], preferred_element_type=f32)
            chosen = jnp.sum(jnp.where(own_head, every, 0.0).reshape(32, 8, 1024), axis=1)
            w.heads[0, pl.ds(pl.multiple_of(j * 32, 32), 32), :] = chosen.astype(bf)
            return carry

        lax.fori_loop(2 * q, 2 * q + 2, finish, 0)
        for d in range(2):
            gather(d, q, 1).start()

    own_proj.wait()
    pair_proj.wait_recv()
    w.proj_all[:, 0:448] = w.proj[0]
    w.proj_all[:, 448:896] = w.proj[1]

    y_mine = pl.multiple_of(y * 64, 64)
    y_theirs = pl.multiple_of((1 - y) * 64, 64)
    x_mine = pl.multiple_of(x * 16, 16)

    def fold(slot):
        return remote(w.fold_out.at[slot], w.fold_in.at[slot], w.fold_s.at[slot], w.fold_r.at[slot], exp=lax.rem(e + 4, 8))

    def cross(slot, i):
        to = lax.rem(x + i, 4)
        return remote(
            w.cross_out.at[slot, pl.ds(pl.multiple_of(to * 16, 16), 16)], w.cross_in.at[slot, i - 1],
            w.cross_s.at[slot, i - 1], w.cross_r.at[slot, i - 1], exp=4 * y + to,
        )

    def deliver(slot):
        return remote(
            w.part_out.at[slot], w.parts.at[z], w.part_s.at[slot], w.part_r.at[slot], ctx=2 * lax.rem(z + 8 - slot, 8) + k
        )

    def deliver_in(slot):
        source = lax.rem(z + slot, 8)
        return remote(w.part_out.at[slot], w.parts.at[source], w.part_s.at[slot], w.part_r.at[slot], ctx=2 * source + k)

    def project(slot):
        w.product[slot] = jnp.dot(w.heads[slot], w.proj_all[...], preferred_element_type=f32)
        w.fold_out[slot] = w.product[slot, pl.ds(y_theirs, 64), :].astype(bf)
        fold(slot).start()

    def over_y(slot):
        fold(slot).wait_recv()
        both = w.product[slot, pl.ds(y_mine, 64), :] + w.fold_in[slot].astype(f32)
        w.product[slot, pl.ds(y_mine, 64), :] = both
        w.cross_out[slot] = both.astype(bf)
        for i in range(1, 4):
            cross(slot, i).start()

    def over_x(slot):
        whole = w.product[slot, pl.ds(pl.multiple_of(y_mine + x_mine, 16), 16), :]
        for i in range(1, 4):
            cross(slot, i).wait_recv()
            whole = whole + w.cross_in[slot, i - 1].astype(f32)
        w.part_out[slot] = whole.astype(bf)

        @pl.when(slot >= 1)
        def _():
            deliver(slot).start()

    def turn(r, carry):
        @pl.when((r >= 1) & (r <= 4))
        def _():
            for q in range(2):
                for d in range(2):
                    @pl.when(r <= reach(d, q))
                    def _(d=d, q=q):
                        gather(d, q, r).wait_recv()

                    @pl.when(r + 1 <= reach(d, q))
                    def _(d=d, q=q):
                        gather(d, q, r + 1).start()

        for stage, act in enumerate((project, over_y, over_x)):
            now = r - stage

            @pl.when((now >= 0) & (now <= 4))
            def _(act=act, now=now):
                act(now)

            @pl.when((now >= 1) & (now <= 3))
            def _(act=act, now=now):
                act(8 - now)

        return carry

    lax.fori_loop(0, 7, turn, 0)
    w.parts[pl.ds(z, 1)] = w.part_out[0:1]
    for slot in range(1, 8):
        deliver_in(slot).wait_recv()
    for other_z in range(8):
        columns = slice(other_z * 896, (other_z + 1) * 896)
        w.stream[:, columns] = (residual_ref[:, columns].astype(f32) + w.parts[other_z].astype(f32)).astype(bf)

    def settle():
        pair_proj.wait_send()

        def chained(s, carry):
            for q in range(4):
                chain(s, q).wait_send()
            return carry

        lax.fori_loop(1, 5, chained, 0)

        def shared(s, carry):
            share(s).wait_send()
            return carry

        lax.fori_loop(0, 5, shared, 0)
        for q in range(2):
            for d in range(2):
                def gathered(r, carry, d=d, q=q):
                    gather(d, q, r).wait_send()
                    return carry

                lax.fori_loop(1, reach(d, q) + 1, gathered, 0)

        def folded(slot, carry):
            fold(slot).wait_send()
            for i in range(1, 4):
                cross(slot, i).wait_send()

            @pl.when(slot >= 1)
            def _():
                deliver(slot).wait_send()
            return carry

        lax.fori_loop(0, 8, folded, 0)

    return settle


def tables(w, ids_ref, weights_ref, k):
    f32 = jnp.float32
    ids = ids_ref[...].astype(f32)
    lane = lax.broadcasted_iota(jnp.int32, (16, 128), 1)
    expert = lane.astype(f32)
    first, second = (jnp.where(ids[:, i : i + 1] == expert, 1.0, 0.0) for i in range(2))
    earlier = lax.broadcasted_iota(jnp.int32, (16, 16), 1) < lax.broadcasted_iota(jnp.int32, (16, 16), 0)
    counts = jnp.dot(jnp.where(earlier, 1.0, 0.0), first + second, preferred_element_type=f32)
    ranks = (
        jnp.sum(first * counts, axis=1, keepdims=True),
        jnp.sum(second * (counts + first), axis=1, keepdims=True),
    )
    weights = weights_ref[...]
    table = jnp.zeros((16, 128), f32)
    for i in range(2):
        table = jnp.where(lane == i, ids[:, i : i + 1] * 8.0 + ranks[i], table)
        table = jnp.where(lane == i + 2, weights[:, i : i + 1], table)
    w.table[pl.ds(k, 1)] = table[None]


def matrices(w):
    bf, f32 = jnp.bfloat16, jnp.float32
    both = w.table[...].reshape(32, 128)
    columns = jnp.concatenate([both] * 4, axis=0)
    lanes = jnp.transpose(columns)
    for part, (_, groups, height) in enumerate(PARTS):
        span, count = groups * 32, 8 * height

        def decode(shape, axis):
            row = lax.broadcasted_iota(jnp.int32, shape, axis).astype(f32)
            expert = jnp.floor((row + 0.5) * (1.0 / height))
            inner = row - expert * height
            group = jnp.floor((inner + 0.5) * 0.1)
            within = inner - group * 10.0
            block = jnp.where(within >= 5.0, 1.0, 0.0)
            slot = jnp.where(group < groups, expert * 8.0 + within - block * 5.0, -1.0)
            token = lax.broadcasted_iota(jnp.int32, shape, 1 - axis)
            owner = lax.shift_right_logical(token, 4).astype(f32)
            return slot, owner == group * 2.0 + block

        slot, same = decode((count, span), 0)
        hit = same & ((slot == lanes[0:1, :span]) | (slot == lanes[1:2, :span]))
        (w.sel0, w.sel1)[part][...] = jnp.where(hit, 1.0, 0.0).astype(bf)
        slot, same = decode((span, count), 1)
        weight = jnp.zeros((span, count), f32)
        for i in range(2):
            weight = weight + jnp.where(same & (slot == columns[:span, i : i + 1]), columns[:span, i + 2 : i + 3], 0.0)
        high = weight.astype(bf)
        mix = (w.mix0, w.mix1)[part]
        mix[0:span, :] = high
        mix[span : 2 * span, :] = (weight - high.astype(f32)).astype(bf)


def layer_kernel(
    q_ref, lat_ref, doc_ref, ids_ref, weights_ref, residual_ref, gain_ref, vu_ref, op_ref, gate_ref, up_ref, down_ref,
    out_ref, *scratch
):
    w = types.SimpleNamespace(**dict(zip(SCRATCH, scratch, strict=True)))
    p, c, e = lax.axis_index("pipe"), lax.axis_index("ctx"), lax.axis_index("exp")
    k = lax.rem(c, 2)
    z = lax.div(c, 2)
    kk = 1 - k
    other = 2 * z + kk
    right = 2 * lax.rem(z + 1, 8) + k
    left = 2 * lax.rem(z + 7, 8) + k
    over = 1 - p
    mine = pl.multiple_of(k * HALF, 128)
    theirs = pl.multiple_of(kk * HALF, 128)
    my_lane = pl.multiple_of(k * 128, 128)
    up_lane = pl.multiple_of(256 + k * 128, 128)

    bf, f32 = jnp.bfloat16, jnp.float32

    w.keys[0, pl.ds(k, 1), :, 0:KV] = lat_ref[...][None]
    diagonal = lax.broadcasted_iota(jnp.int32, (128, 128), 0) == lax.broadcasted_iota(jnp.int32, (128, 128), 1)
    doc_column = jnp.sum(jnp.where(diagonal, doc_ref[...].astype(f32), 0.0), axis=1, keepdims=True)
    w.keys[0, pl.ds(k, 1), :, KV:640] = jnp.broadcast_to(doc_column, (128, 640 - KV)).astype(bf)[None]
    tables(w, ids_ref, weights_ref, k)
    meet(
        [{"ctx": other}, {"pipe": over}, {"pipe": over, "ctx": other}]
        + [{"ctx": 2 * lax.rem(z + i, 8) + k} for i in range(1, 8)]
        + [{"exp": lax.rem(e + i, 8)} for i in range(1, 8)]
    )
    local = [
        pltpu.make_async_copy(gate_ref.at[pl.ds(mine, HALF), :], w.w_in.at[:, pl.ds(my_lane, 128)], w.loc.at[0]),
        pltpu.make_async_copy(up_ref.at[pl.ds(mine, HALF), :], w.w_in.at[:, pl.ds(up_lane, 128)], w.loc.at[1]),
        pltpu.make_async_copy(down_ref.at[:, pl.ds(mine, HALF)], w.w_down.at[pl.ds(my_lane, 128), :], w.loc.at[2]),
    ]
    pair = [
        remote(w.normed.at[:, pl.ds(theirs, HALF)], w.pn, w.pair_s.at[0], w.pair_r.at[0], ctx=other),
        remote(w.stream.at[:, pl.ds(theirs, HALF)], w.ps, w.pair_s.at[1], w.pair_r.at[1], ctx=other),
        remote(gate_ref.at[pl.ds(theirs, HALF), :], w.w_in.at[:, pl.ds(my_lane, 128)], w.pair_s.at[2], w.pair_r.at[2], ctx=other),
        remote(up_ref.at[pl.ds(theirs, HALF), :], w.w_in.at[:, pl.ds(up_lane, 128)], w.pair_s.at[3], w.pair_r.at[3], ctx=other),
        remote(down_ref.at[:, pl.ds(theirs, HALF)], w.w_down.at[pl.ds(my_lane, 128), :], w.pair_s.at[4], w.pair_r.at[4], ctx=other),
    ]
    pair.append(remote(w.table.at[k], w.table.at[k], w.pair_s.at[5], w.pair_r.at[5], ctx=other))

    def start_rest():
        pair[5].start()
        for copy in local:
            copy.start()
        for copy in pair[2:5]:
            copy.start()

    settle = attend(w, q_ref, lat_ref, doc_ref, vu_ref, op_ref, residual_ref, start_rest)
    wide = w.stream[...].astype(f32)
    mean_square = jnp.mean(wide * wide, axis=1, keepdims=True)
    w.normed[...] = (wide * lax.rsqrt(mean_square + epsilon) * gain_ref[...]).astype(bf)
    for copy in pair[:2]:
        copy.start()
    my_rows = [pl.multiple_of(g * 32 + k * 16, 16) for g in range(4)]
    their_rows = [pl.multiple_of(g * 32 + kk * 16, 16) for g in range(4)]
    xgs, sgs = (w.xg0, w.xg1), (w.sg0, w.sg1)
    for part, (first, groups, _) in enumerate(PARTS):
        for g in range(groups):
            lanes = pl.ds(pl.multiple_of(mine + (first + g) * 512, 128), 512)
            xgs[part][pl.ds(my_rows[g], 16), :] = w.normed[:, lanes]
            sgs[part][pl.ds(my_rows[g], 16), :] = w.stream[:, lanes]
    pair[5].wait_recv()
    matrices(w)
    pair[0].wait_recv()
    outboxes, inboxes, sels = (w.outbox0, w.outbox1), (w.inbox0, w.inbox1), (w.sel0, w.sel1)

    def box(part, i):
        return remote(
            outboxes[part].at[lax.rem(e + i, 8)], inboxes[part].at[e], w.box_s.at[part, i], w.box_r.at[part, i],
            exp=lax.rem(e + i, 8),
        )

    def box_in(part, i):
        source = lax.rem(e + 8 - i, 8)
        return remote(outboxes[part].at[source], inboxes[part].at[source], w.box_s.at[part, i], w.box_r.at[part, i], exp=source)

    for part, (first, groups, height) in enumerate(PARTS):
        for g in range(groups):
            lanes = slice((first + g) * 512, (first + g + 1) * 512)
            xgs[part][pl.ds(their_rows[g], 16), :] = w.pn[:, lanes]
        chosen = jnp.dot(sels[part][...], xgs[part][...], preferred_element_type=jnp.float32).astype(jnp.bfloat16)
        outboxes[part][...] = chosen.reshape(8, height, 512)
        for i in range(1, 8):
            box(part, i).start()
        inboxes[part][pl.ds(e, 1)] = outboxes[part][pl.ds(e, 1)]

    pair[1].wait_recv()
    for part, (first, groups, _) in enumerate(PARTS):
        for g in range(groups):
            lanes = slice((first + g) * 512, (first + g + 1) * 512)
            sgs[part][pl.ds(their_rows[g], 16), :] = w.ps[:, lanes]

    def gather(d, q, r):
        columns = pl.ds(PIECES[q][0], PIECES[q][1])
        if d == 0:
            return remote(w.rows.at[r - 1, :, columns], w.rows.at[r, :, columns], w.ag_s.at[d, q, r], w.ag_r.at[d, q, r], ctx=right)
        return remote(
            w.rows.at[lax.rem(9 - r, 8), :, columns], w.rows.at[8 - r, :, columns], w.ag_s.at[d, q, r], w.ag_r.at[d, q, r], ctx=left
        )

    def reach(d, q):
        return 4 if (q % 2 == 0) == (d == 0) else 3

    for part, (first, groups, height) in enumerate(PARTS):
        for i in range(1, 8):
            box_in(part, i).wait_recv()
        landed_rows = inboxes[part][...].reshape(8 * height, 512)
        for g in range(groups):
            w.rows[0, :, (first + g) * 512 : (first + g + 1) * 512] = jnp.dot(
                squeeze_map(height, groups, g), landed_rows, preferred_element_type=jnp.float32
            ).astype(jnp.bfloat16)
        for q in (2 * part, 2 * part + 1):
            for d in range(2):
                gather(d, q, 1).start()
    for copy in local:
        copy.wait()
    for copy in pair[2:5]:
        copy.wait_recv()

    def swap(slot):
        return remote(w.half.at[slot], w.half_other.at[slot], w.half_s.at[slot], w.half_r.at[slot], ctx=other)

    def first_half(slot):
        w.half[slot] = jnp.dot(w.rows[slot], w.w_in[...], preferred_element_type=jnp.float32)
        swap(slot).start()

    def second_half(slot):
        swap(slot).wait_recv()
        both = w.half[slot] + w.half_other[slot]
        gate = both[:, :256]
        hidden = (gate / (1.0 + jnp.exp(-gate)) * both[:, 256:]).astype(jnp.bfloat16)
        w.total[slot] = jnp.dot(hidden, w.w_down[...], preferred_element_type=jnp.float32).astype(jnp.bfloat16)

    first_half(0)
    second_half(0)

    def pass_on(m, step):
        columns = pl.ds(SUBS[m][0], SUBS[m][1])
        slot = step + 1 if m < 2 else 7 - step
        return remote(
            w.total.at[slot, :, columns], w.arrived.at[m, step], w.rs_s.at[m, step], w.rs_r.at[m, step], ctx=right if m < 2 else left
        )

    def turn(r, carry):
        @pl.when(r <= 4)
        def _():
            for q in range(4):
                for d in range(2):
                    @pl.when(r <= reach(d, q))
                    def _(d=d, q=q):
                        gather(d, q, r).wait_recv()

                    @pl.when(r + 1 <= reach(d, q))
                    def _(d=d, q=q):
                        gather(d, q, r + 1).start()

            first_half(r)

            @pl.when(r < 4)
            def _():
                first_half(8 - r)

            second_half(r)

            @pl.when(r < 4)
            def _():
                second_half(8 - r)

        for m in (0, 2, 1, 3):
            slot = r if m < 2 else 8 - r
            columns = pl.ds(SUBS[m][0], SUBS[m][1])

            @pl.when(r >= 2)
            def _(m=m, slot=slot, columns=columns):
                pass_on(m, r - 2).wait_recv()
                w.total[slot, :, columns] = (
                    w.total[slot, :, columns].astype(jnp.float32) + w.arrived[m, r - 2].astype(jnp.float32)
                ).astype(jnp.bfloat16)

            pass_on(m, r - 1).start()
        return carry

    lax.fori_loop(1, 8, turn, 0)
    for m in (0, 2, 1, 3):
        pass_on(m, 6).wait_recv()
        columns = slice(SUBS[m][0], SUBS[m][0] + SUBS[m][1])
        w.summed[:, columns] = (w.total[0, :, columns].astype(jnp.float32) + w.arrived[m, 6].astype(jnp.float32)).astype(jnp.bfloat16)

    rets, backs, mixes, readies = (w.ret0, w.ret1), (w.back0, w.back1), (w.mix0, w.mix1), w.ready

    def give(part, i):
        return remote(
            rets[part].at[lax.rem(e + i, 8)], backs[part].at[e], w.back_s.at[part, i], w.back_r.at[part, i], exp=lax.rem(e + i, 8)
        )

    def give_in(part, i):
        source = lax.rem(e + 8 - i, 8)
        return remote(rets[part].at[source], backs[part].at[source], w.back_s.at[part, i], w.back_r.at[part, i], exp=source)

    for part, (first, groups, height) in enumerate(PARTS):
        spread = jnp.zeros((8 * height, 512), jnp.float32)
        for g in range(groups):
            spread = spread + jnp.dot(
                spread_map(height, groups, g), w.summed[:, (first + g) * 512 : (first + g + 1) * 512],
                preferred_element_type=jnp.float32,
            )
        rets[part][...] = spread.astype(jnp.bfloat16).reshape(8, height, 512)
        for i in range(1, 8):
            give(part, i).start()
        backs[part][pl.ds(e, 1)] = rets[part][pl.ds(e, 1)]
    for part, (first, groups, height) in enumerate(PARTS):
        for i in range(1, 8):
            give_in(part, i).wait_recv()
        span = groups * 32
        mixed = jnp.dot(mixes[part][...], backs[part][...].reshape(8 * height, 512), preferred_element_type=jnp.float32)
        combined = mixed[:span] + mixed[span:]
        layer_out = (sgs[part][...].astype(jnp.float32) + combined).astype(jnp.bfloat16)
        for g in range(groups):
            for b in range(2):
                readies[b, :, (first + g) * 512 : (first + g + 1) * 512] = layer_out[g * 32 + b * 16 : g * 32 + b * 16 + 16]

    def hand(b, core):
        return remote(w.ready.at[b], w.landed.at[core], w.fin_s.at[b], w.fin_r.at[core], pipe=over, ctx=2 * z + b)

    for b in range(2):
        hand(b, k).start()
    for b in range(2):
        hand(b, b).wait_recv()
        out_ref[:, b * HALF : (b + 1) * HALF] = w.landed[b]

    for b in range(2):
        hand(b, k).wait_send()
    for copy in pair:
        copy.wait_send()
    for part in range(2):
        for i in range(1, 8):
            box(part, i).wait_send()
            give(part, i).wait_send()
    for q in range(4):
        for d in range(2):
            def done(r, carry, d=d, q=q):
                gather(d, q, r).wait_send()
                return carry

            lax.fori_loop(1, reach(d, q) + 1, done, 0)

    def sent(step, carry):
        for m in range(4):
            pass_on(m, step).wait_send()
        return carry

    lax.fori_loop(0, 7, sent, 0)

    def swapped(slot, carry):
        swap(slot).wait_send()
        return carry

    lax.fori_loop(0, 8, swapped, 0)
    settle()


BF, F32 = jnp.bfloat16, jnp.float32
SCRATCH = {
    "keys": ((5, 2, 128, 640), BF), "queries": ((1024, KV), BF), "query_doc": ((1024, 128), F32), "top": ((1024, 128), F32),
    "sums": ((1024, 128), F32), "mixed": ((1024, LAT), F32), "value_up": ((LAT, 1024), BF), "heads": ((8, 128, 1024), BF),
    "proj": ((2, 1024, 448), BF), "proj_all": ((1024, 896), BF), "product": ((8, 128, 896), F32),
    "fold_out": ((8, 64, 896), BF), "fold_in": ((8, 64, 896), BF), "cross_out": ((8, 64, 896), BF),
    "cross_in": ((8, 3, 16, 896), BF), "part_out": ((8, 16, 896), BF), "parts": ((8, 16, 896), BF), "stream": ((16, D), BF),
    "table": ((2, 16, 128), F32), "sel0": ((384, 128), BF), "sel1": ((256, 96), BF), "mix0": ((256, 384), BF), "mix1": ((192, 256), BF),
    "normed": ((16, D), BF), "pn": ((16, HALF), BF), "ps": ((16, HALF), BF),
    "xg0": ((128, 512), BF), "xg1": ((96, 512), BF), "sg0": ((128, 512), BF), "sg1": ((96, 512), BF),
    "outbox0": ((8, 48, 512), BF), "outbox1": ((8, 32, 512), BF), "inbox0": ((8, 48, 512), BF), "inbox1": ((8, 32, 512), BF),
    "w_in": ((HALF, 512), BF), "w_down": ((256, HALF), BF), "rows": ((8, 80, HALF), BF),
    "half": ((8, 80, 512), F32), "half_other": ((8, 80, 512), F32), "total": ((8, 80, HALF), BF),
    "arrived": ((4, 7, 80, 896), BF), "summed": ((80, HALF), BF),
    "ret0": ((8, 48, 512), BF), "ret1": ((8, 32, 512), BF), "back0": ((8, 48, 512), BF), "back1": ((8, 32, 512), BF),
    "ready": ((2, 16, HALF), BF), "landed": ((2, 16, HALF), BF),
    "load": ((9,), None), "chain_s": ((5, 4), None), "chain_r": ((5, 4), None), "share_s": ((5,), None), "share_r": ((5,), None),
    "proj_s": ((1,), None), "proj_r": ((1,), None), "head_s": ((2, 2, 5), None), "head_r": ((2, 2, 5), None),
    "fold_s": ((8,), None), "fold_r": ((8,), None), "cross_s": ((8, 3), None), "cross_r": ((8, 3), None),
    "part_s": ((8,), None), "part_r": ((8,), None),
    "pair_s": ((6,), None), "pair_r": ((6,), None), "loc": ((3,), None), "box_s": ((2, 8), None), "box_r": ((2, 8), None),
    "ag_s": ((2, 4, 5), None), "ag_r": ((2, 4, 5), None), "half_s": ((8,), None), "half_r": ((8,), None),
    "rs_s": ((4, 7), None), "rs_r": ((4, 7), None), "back_s": ((2, 8), None), "back_r": ((2, 8), None),
    "fin_s": ((2,), None), "fin_r": ((2,), None),
}


def on_device(
    queries, latent_rows, doc_ids, value_up, out_proj, residual_in, norm_gain, expert_ids, gate_weights, gate_proj, up_proj,
    down_proj,
):
    vmem, any_space = pl.BlockSpec(memory_space=pltpu.VMEM), pl.BlockSpec(memory_space=pl.ANY)
    return pl.pallas_call(
        layer_kernel,
        out_shape=jax.ShapeDtypeStruct((16, D), BF),
        in_specs=[vmem] * 7 + [any_space] * 5,
        out_specs=vmem,
        scratch_shapes=[
            pltpu.SemaphoreType.DMA(shape) if kind is None else pltpu.VMEM(shape, kind) for shape, kind in SCRATCH.values()
        ],
        compiler_params=pltpu.CompilerParams(collective_id=1, has_side_effects=True, vmem_limit_bytes=60 << 20),
        cost_estimate=pl.CostEstimate(flops=8_000_000_000, bytes_accessed=10_000_000, transcendentals=2_000_000),
        name="layer",
    )(
        queries[0], latent_rows[0], doc_ids, expert_ids[0], gate_weights[0], residual_in[0], norm_gain,
        value_up[0], out_proj[0], gate_proj[0, 0], up_proj[0, 0], down_proj[0, 0],
    )[None]


def solution(mesh):
    return jax.shard_map(
        on_device,
        mesh=mesh,
        in_specs=(
            P("pipe", "ctx", "exp", None),
            P("pipe", "ctx", None),
            P("pipe", "ctx"),
            P("pipe", "exp", None, None),
            P("pipe", "exp", "ctx"),
            P("pipe", ("ctx", "exp"), None),
            P("pipe", None),
            P("pipe", ("ctx", "exp"), None),
            P("pipe", ("ctx", "exp"), None),
            P("pipe", "exp", None, "ctx"),
            P("pipe", "exp", None, "ctx"),
            P("pipe", "exp", "ctx", None),
        ),
        out_specs=P("pipe", ("ctx", "exp"), None),
        check_vma=False,
    )
```

```python
import math
import types

import jax
import jax.numpy as jnp
from jax import lax
from jax.experimental import pallas as pl
from jax.experimental.pallas import tpu as pltpu
from jax.sharding import PartitionSpec as P

D = 7168
HALF = D // 2
HD = 128
ROPE = 64
LAT = 512
KV = LAT + ROPE
MESH = pl.DeviceIdType.MESH

epsilon = 1e-06
masked_score = -1e30
score_scale = 1.0 / math.sqrt(HD + ROPE)
KEY_PIECES = ((0, 144), (144, 144), (288, 144), (432, 160))


def remote(src, dst, send_sem, recv_sem, **device):
    return pltpu.make_async_remote_copy(
        src_ref=src,
        dst_ref=dst,
        send_sem=send_sem,
        recv_sem=recv_sem,
        device_id=device,
        device_id_type=MESH,
    )


def meet(peers):
    barrier = pltpu.get_barrier_semaphore()
    for device in peers:
        pl.semaphore_signal(barrier, 1, device_id=device, device_id_type=MESH)
    pl.semaphore_wait(barrier, len(peers))


def squeeze_map(rows, groups, group, dtype=jnp.bfloat16):
    row = lax.broadcasted_iota(jnp.int32, (80, 8 * rows), 0).astype(jnp.float32)
    col = lax.broadcasted_iota(jnp.int32, (80, 8 * rows), 1).astype(jnp.float32)
    source = jnp.floor((row + 0.5) * 0.1)
    want = source * rows + (row - source * 10) + group * 10
    return jnp.where(col == want, 1.0, 0.0).astype(dtype)


def spread_map(rows, groups, group, dtype=jnp.bfloat16):
    row = lax.broadcasted_iota(jnp.int32, (8 * rows, 80), 0).astype(jnp.float32)
    col = lax.broadcasted_iota(jnp.int32, (8 * rows, 80), 1).astype(jnp.float32)
    source = jnp.floor((col + 0.5) * 0.1)
    want = source * rows + (col - source * 10) + group * 10
    return jnp.where(row == want, 1.0, 0.0).astype(dtype)


PARTS = ((0, 4, 48), (4, 3, 32))
PIECES = ((0, 1024), (1024, 1024), (2048, 768), (2816, 768))
SUBS = ((0, 896), (896, 896), (1792, 896), (2688, 896))


def attend(w, q_ref, lat_ref, doc_ref, vu_ref, op_ref, residual_ref, start_rest):
    p, c, e = lax.axis_index("pipe"), lax.axis_index("ctx"), lax.axis_index("exp")
    k = lax.rem(c, 2)
    z = lax.div(c, 2)
    kk = 1 - k
    other = 2 * z + kk
    right = 2 * lax.rem(z + 1, 8) + k
    left = 2 * lax.rem(z + 7, 8) + k
    y = lax.div(e, 4)
    x = lax.rem(e, 4)
    bf, f32 = jnp.bfloat16, jnp.float32
    my_lanes = pl.ds(pl.multiple_of(k * 128, 128), 128)
    their_lanes = pl.ds(pl.multiple_of(kk * 128, 128), 128)
    my_columns = pl.ds(pl.multiple_of(k * 448, 16), 448)

    def chain(s, q):
        piece = pl.ds(*KEY_PIECES[q])
        return remote(
            w.keys.at[s - 1, piece, my_lanes], w.keys.at[s, piece, my_lanes], w.chain_s.at[s, q], w.chain_r.at[s, q], ctx=right
        )

    def share(s):
        return remote(w.keys.at[s, :, my_lanes], w.keys.at[s, :, my_lanes], w.share_s.at[s], w.share_r.at[s], ctx=other)

    def share_in(s):
        return remote(w.keys.at[s, :, their_lanes], w.keys.at[s, :, their_lanes], w.share_s.at[s], w.share_r.at[s], ctx=other)

    for q in range(4):
        chain(1, q).start()
    share(0).start()
    own_proj = pltpu.make_async_copy(op_ref, w.proj.at[my_columns], w.load.at[8])
    own_proj.start()
    pair_proj = remote(op_ref, w.proj.at[my_columns], w.proj_s.at[0], w.proj_r.at[0], ctx=other)
    pair_proj.start()
    up_loads = [
        pltpu.make_async_copy(vu_ref.at[h], w.value_up.at[h], w.load.at[h]) for h in range(8)
    ]
    for copy in up_loads:
        copy.start()
    start_rest()

    for h in range(8):
        w.queries[h * 128 : (h + 1) * 128, :] = jnp.transpose(q_ref[h])
    w.top[...] = jnp.full((1024, 128), masked_score, f32)
    w.sums[...] = jnp.zeros((1024, 128), f32)
    w.mixed[...] = jnp.zeros((1024, LAT), f32)
    contract_last = (((1,), (1,)), ((), ()))
    query_pos = c * 128 + lax.broadcasted_iota(jnp.int32, (128, 256), 0)

    def visit(s, carry):
        @pl.when(s >= 1)
        def _():
            for q in range(4):
                chain(s, q).wait_recv()

                @pl.when(s < 4)
                def _(q=q):
                    chain(s + 1, q).start()

            share(s).start()

        share_in(s).wait_recv()
        key_doc = w.keys[s, KV:, :].astype(f32)[0:1]
        key_pos = lax.rem(z + 8 - s, 8) * 256 + lax.broadcasted_iota(jnp.int32, (128, 256), 1)
        query_doc = jnp.concatenate([w.query_doc[...]] * 2, axis=1)
        hidden = jnp.where((key_pos <= query_pos) & (query_doc == key_doc), 0.0, masked_score)
        hidden = jnp.concatenate([hidden] * 4, axis=0)

        def some(j, carry):
            at = pl.ds(pl.multiple_of(j * 512, 512), 512)
            scores = jnp.dot(w.queries[at], w.keys[s, 0:KV, :], preferred_element_type=f32) * score_scale + hidden
            before = w.top[at]
            highest = jnp.maximum(before, jnp.max(scores, axis=1, keepdims=True))
            shrink = jnp.exp(before - highest)
            weights = jnp.exp(scores - jnp.concatenate([highest, highest], axis=1))
            w.top[at] = highest
            w.sums[at] = w.sums[at] * shrink + jnp.sum(weights, axis=1, keepdims=True)
            update = lax.dot_general(weights.astype(bf), w.keys[s, 0:LAT, :], contract_last, preferred_element_type=f32)
            w.mixed[at] = w.mixed[at] * jnp.concatenate([shrink] * 4, axis=1) + update
            return carry

        lax.fori_loop(0, 2, some, 0)
        return carry

    lax.fori_loop(0, 5, visit, 0)

    for copy in up_loads:
        copy.wait()

    def gather(d, q, r):
        piece = pl.ds(q * 64, 64)
        if d == 0:
            return remote(w.heads.at[r - 1, piece], w.heads.at[r, piece], w.head_s.at[d, q, r], w.head_r.at[d, q, r], ctx=right)
        return remote(
            w.heads.at[lax.rem(9 - r, 8), piece], w.heads.at[8 - r, piece], w.head_s.at[d, q, r], w.head_r.at[d, q, r], ctx=left
        )

    def reach(d, q):
        return 4 if q == d else 3

    for h in range(8):
        at = slice(h * 128, (h + 1) * 128)
        latent_out = (w.mixed[at] / jnp.concatenate([w.sums[at]] * 4, axis=1)).astype(bf)
        w.heads[0, :, at] = jnp.dot(latent_out, w.value_up[h], preferred_element_type=f32).astype(bf)
    for q in range(2):
        for d in range(2):
            gather(d, q, 1).start()

    own_proj.wait()
    pair_proj.wait_recv()
    w.proj_all[...] = jnp.transpose(w.proj[...])

    y_mine = pl.multiple_of(y * 64, 64)
    y_theirs = pl.multiple_of((1 - y) * 64, 64)
    x_mine = pl.multiple_of(x * 16, 16)

    def fold(slot):
        return remote(w.fold_out.at[slot], w.fold_in.at[slot], w.fold_s.at[slot], w.fold_r.at[slot], exp=lax.rem(e + 4, 8))

    def cross(slot, i):
        to = lax.rem(x + i, 4)
        return remote(
            w.cross_out.at[slot, pl.ds(pl.multiple_of(to * 16, 16), 16)], w.cross_in.at[slot, i - 1],
            w.cross_s.at[slot, i - 1], w.cross_r.at[slot, i - 1], exp=4 * y + to,
        )

    def deliver(slot):
        return remote(
            w.part_out.at[slot], w.parts.at[z], w.part_s.at[slot], w.part_r.at[slot], ctx=2 * lax.rem(z + 8 - slot, 8) + k
        )

    def deliver_in(slot):
        source = lax.rem(z + slot, 8)
        return remote(w.part_out.at[slot], w.parts.at[source], w.part_s.at[slot], w.part_r.at[slot], ctx=2 * source + k)

    def project(slot):
        w.product[slot] = jnp.dot(w.heads[slot], w.proj_all[...], preferred_element_type=f32)
        w.fold_out[slot] = w.product[slot, pl.ds(y_theirs, 64), :].astype(bf)
        fold(slot).start()

    def over_y(slot):
        fold(slot).wait_recv()
        both = w.product[slot, pl.ds(y_mine, 64), :] + w.fold_in[slot].astype(f32)
        w.product[slot, pl.ds(y_mine, 64), :] = both
        w.cross_out[slot] = both.astype(bf)
        for i in range(1, 4):
            cross(slot, i).start()

    def over_x(slot):
        whole = w.product[slot, pl.ds(pl.multiple_of(y_mine + x_mine, 16), 16), :]
        for i in range(1, 4):
            cross(slot, i).wait_recv()
            whole = whole + w.cross_in[slot, i - 1].astype(f32)
        w.part_out[slot] = whole.astype(bf)

        @pl.when(slot >= 1)
        def _():
            deliver(slot).start()

    def turn(r, carry):
        @pl.when((r >= 1) & (r <= 4))
        def _():
            for q in range(2):
                for d in range(2):
                    @pl.when(r <= reach(d, q))
                    def _(d=d, q=q):
                        gather(d, q, r).wait_recv()

                    @pl.when(r + 1 <= reach(d, q))
                    def _(d=d, q=q):
                        gather(d, q, r + 1).start()

        for stage, act in enumerate((project, over_y, over_x)):
            now = r - stage

            @pl.when((now >= 0) & (now <= 4))
            def _(act=act, now=now):
                act(now)

            @pl.when((now >= 1) & (now <= 3))
            def _(act=act, now=now):
                act(8 - now)

        return carry

    lax.fori_loop(0, 7, turn, 0)
    w.parts[pl.ds(z, 1)] = w.part_out[0:1]
    for slot in range(1, 8):
        deliver_in(slot).wait_recv()
    for other_z in range(8):
        columns = slice(other_z * 896, (other_z + 1) * 896)
        w.stream[:, columns] = (residual_ref[:, columns].astype(f32) + w.parts[other_z].astype(f32)).astype(bf)

    def settle():
        pair_proj.wait_send()

        def chained(s, carry):
            for q in range(4):
                chain(s, q).wait_send()
            return carry

        lax.fori_loop(1, 5, chained, 0)

        def shared(s, carry):
            share(s).wait_send()
            return carry

        lax.fori_loop(0, 5, shared, 0)
        for q in range(2):
            for d in range(2):
                def gathered(r, carry, d=d, q=q):
                    gather(d, q, r).wait_send()
                    return carry

                lax.fori_loop(1, reach(d, q) + 1, gathered, 0)

        def folded(slot, carry):
            fold(slot).wait_send()
            for i in range(1, 4):
                cross(slot, i).wait_send()

            @pl.when(slot >= 1)
            def _():
                deliver(slot).wait_send()
            return carry

        lax.fori_loop(0, 8, folded, 0)

    return settle


def column_of(rows):
    diagonal = lax.broadcasted_iota(jnp.int32, rows.shape, 0) == lax.broadcasted_iota(jnp.int32, rows.shape, 1)
    return jnp.sum(jnp.where(diagonal, rows, 0.0), axis=1, keepdims=True)


def tables(w, ids_ref, weights_ref, k):
    f32 = jnp.float32
    ids = [column_of(jnp.broadcast_to(ids_ref[i : i + 1, :].astype(f32), (16, 16))) for i in range(2)]
    weights = [column_of(jnp.broadcast_to(weights_ref[i : i + 1, :], (16, 16))) for i in range(2)]
    lane = lax.broadcasted_iota(jnp.int32, (16, 128), 1)
    expert = lane.astype(f32)
    first, second = (jnp.where(ids[i] == expert, 1.0, 0.0) for i in range(2))
    earlier = lax.broadcasted_iota(jnp.int32, (16, 16), 1) < lax.broadcasted_iota(jnp.int32, (16, 16), 0)
    counts = jnp.dot(jnp.where(earlier, 1.0, 0.0), first + second, preferred_element_type=f32)
    ranks = (
        jnp.sum(first * counts, axis=1, keepdims=True),
        jnp.sum(second * (counts + first), axis=1, keepdims=True),
    )
    table = jnp.zeros((16, 128), f32)
    for i in range(2):
        table = jnp.where(lane == i, ids[i] * 8.0 + ranks[i], table)
        table = jnp.where(lane == i + 2, weights[i], table)
    w.table[pl.ds(k, 1)] = table[None]


def matrices(w):
    bf, f32 = jnp.bfloat16, jnp.float32
    both = w.table[...].reshape(32, 128)
    columns = jnp.concatenate([both] * 4, axis=0)
    lanes = jnp.transpose(columns)
    for part, (_, groups, height) in enumerate(PARTS):
        span, count = groups * 32, 8 * height

        def decode(shape, axis):
            row = lax.broadcasted_iota(jnp.int32, shape, axis).astype(f32)
            expert = jnp.floor((row + 0.5) * (1.0 / height))
            inner = row - expert * height
            group = jnp.floor((inner + 0.5) * 0.1)
            within = inner - group * 10.0
            block = jnp.where(within >= 5.0, 1.0, 0.0)
            slot = jnp.where(group < groups, expert * 8.0 + within - block * 5.0, -1.0)
            token = lax.broadcasted_iota(jnp.int32, shape, 1 - axis)
            owner = lax.shift_right_logical(token, 4).astype(f32)
            return slot, owner == group * 2.0 + block

        slot, same = decode((count, span), 0)
        hit = same & ((slot == lanes[0:1, :span]) | (slot == lanes[1:2, :span]))
        (w.sel0, w.sel1)[part][...] = jnp.where(hit, 1.0, 0.0).astype(bf)
        slot, same = decode((span, count), 1)
        weight = jnp.zeros((span, count), f32)
        for i in range(2):
            weight = weight + jnp.where(same & (slot == columns[:span, i : i + 1]), columns[:span, i + 2 : i + 3], 0.0)
        high = weight.astype(bf)
        mix = (w.mix0, w.mix1)[part]
        mix[0:span, :] = high
        mix[span : 2 * span, :] = (weight - high.astype(f32)).astype(bf)


def layer_kernel(
    q_ref, lat_ref, doc_ref, ids_ref, weights_ref, residual_ref, gain_ref, vu_ref, op_ref, gate_ref, up_ref, down_ref,
    out_ref, *scratch
):
    w = types.SimpleNamespace(**dict(zip(SCRATCH, scratch, strict=True)))
    p, c, e = lax.axis_index("pipe"), lax.axis_index("ctx"), lax.axis_index("exp")
    k = lax.rem(c, 2)
    z = lax.div(c, 2)
    kk = 1 - k
    other = 2 * z + kk
    right = 2 * lax.rem(z + 1, 8) + k
    left = 2 * lax.rem(z + 7, 8) + k
    over = 1 - p
    mine = pl.multiple_of(k * HALF, 128)
    theirs = pl.multiple_of(kk * HALF, 128)
    my_lane = pl.multiple_of(k * 128, 128)
    up_lane = pl.multiple_of(256 + k * 128, 128)

    bf, f32 = jnp.bfloat16, jnp.float32

    w.keys[0, 0:KV, pl.ds(my_lane, 128)] = lat_ref[...]
    doc_row = jnp.broadcast_to(doc_ref[...].astype(f32), (128, 128))
    w.keys[0, KV:, pl.ds(my_lane, 128)] = doc_row[0:16].astype(bf)
    w.query_doc[...] = jnp.broadcast_to(column_of(doc_row), (128, 128))
    tables(w, ids_ref, weights_ref, k)
    meet(
        [{"ctx": other}, {"pipe": over}, {"pipe": over, "ctx": other}]
        + [{"ctx": 2 * lax.rem(z + i, 8) + k} for i in range(1, 8)]
        + [{"exp": lax.rem(e + i, 8)} for i in range(1, 8)]
    )
    local = [
        pltpu.make_async_copy(gate_ref.at[pl.ds(mine, HALF), :], w.w_in.at[:, pl.ds(my_lane, 128)], w.loc.at[0]),
        pltpu.make_async_copy(up_ref.at[pl.ds(mine, HALF), :], w.w_in.at[:, pl.ds(up_lane, 128)], w.loc.at[1]),
        pltpu.make_async_copy(down_ref.at[:, pl.ds(mine, HALF)], w.w_down.at[pl.ds(my_lane, 128), :], w.loc.at[2]),
    ]
    pair = [
        remote(w.normed.at[:, pl.ds(theirs, HALF)], w.pn, w.pair_s.at[0], w.pair_r.at[0], ctx=other),
        remote(w.stream.at[:, pl.ds(theirs, HALF)], w.ps, w.pair_s.at[1], w.pair_r.at[1], ctx=other),
        remote(gate_ref.at[pl.ds(theirs, HALF), :], w.w_in.at[:, pl.ds(my_lane, 128)], w.pair_s.at[2], w.pair_r.at[2], ctx=other),
        remote(up_ref.at[pl.ds(theirs, HALF), :], w.w_in.at[:, pl.ds(up_lane, 128)], w.pair_s.at[3], w.pair_r.at[3], ctx=other),
        remote(down_ref.at[:, pl.ds(theirs, HALF)], w.w_down.at[pl.ds(my_lane, 128), :], w.pair_s.at[4], w.pair_r.at[4], ctx=other),
    ]
    pair.append(remote(w.table.at[k], w.table.at[k], w.pair_s.at[5], w.pair_r.at[5], ctx=other))

    def start_rest():
        pair[5].start()
        for copy in local:
            copy.start()
        for copy in pair[2:5]:
            copy.start()

    settle = attend(w, q_ref, lat_ref, doc_ref, vu_ref, op_ref, residual_ref, start_rest)
    wide = w.stream[...].astype(f32)
    mean_square = jnp.mean(wide * wide, axis=1, keepdims=True)
    w.normed[...] = (wide * lax.rsqrt(mean_square + epsilon) * gain_ref[...]).astype(bf)
    for copy in pair[:2]:
        copy.start()
    my_rows = [pl.multiple_of(g * 32 + k * 16, 16) for g in range(4)]
    their_rows = [pl.multiple_of(g * 32 + kk * 16, 16) for g in range(4)]
    xgs, sgs = (w.xg0, w.xg1), (w.sg0, w.sg1)
    for part, (first, groups, _) in enumerate(PARTS):
        for g in range(groups):
            lanes = pl.ds(pl.multiple_of(mine + (first + g) * 512, 128), 512)
            xgs[part][pl.ds(my_rows[g], 16), :] = w.normed[:, lanes]
            sgs[part][pl.ds(my_rows[g], 16), :] = w.stream[:, lanes]
    pair[5].wait_recv()
    matrices(w)
    pair[0].wait_recv()
    outboxes, inboxes, sels = (w.outbox0, w.outbox1), (w.inbox0, w.inbox1), (w.sel0, w.sel1)

    def box(part, i):
        return remote(
            outboxes[part].at[lax.rem(e + i, 8)], inboxes[part].at[e], w.box_s.at[part, i], w.box_r.at[part, i],
            exp=lax.rem(e + i, 8),
        )

    def box_in(part, i):
        source = lax.rem(e + 8 - i, 8)
        return remote(outboxes[part].at[source], inboxes[part].at[source], w.box_s.at[part, i], w.box_r.at[part, i], exp=source)

    for part, (first, groups, height) in enumerate(PARTS):
        for g in range(groups):
            lanes = slice((first + g) * 512, (first + g + 1) * 512)
            xgs[part][pl.ds(their_rows[g], 16), :] = w.pn[:, lanes]
        chosen = jnp.dot(sels[part][...], xgs[part][...], preferred_element_type=jnp.float32).astype(jnp.bfloat16)
        outboxes[part][...] = chosen.reshape(8, height, 512)
        for i in range(1, 8):
            box(part, i).start()
        inboxes[part][pl.ds(e, 1)] = outboxes[part][pl.ds(e, 1)]

    pair[1].wait_recv()
    for part, (first, groups, _) in enumerate(PARTS):
        for g in range(groups):
            lanes = slice((first + g) * 512, (first + g + 1) * 512)
            sgs[part][pl.ds(their_rows[g], 16), :] = w.ps[:, lanes]

    def gather(d, q, r):
        columns = pl.ds(PIECES[q][0], PIECES[q][1])
        if d == 0:
            return remote(w.rows.at[r - 1, :, columns], w.rows.at[r, :, columns], w.ag_s.at[d, q, r], w.ag_r.at[d, q, r], ctx=right)
        return remote(
            w.rows.at[lax.rem(9 - r, 8), :, columns], w.rows.at[8 - r, :, columns], w.ag_s.at[d, q, r], w.ag_r.at[d, q, r], ctx=left
        )

    def reach(d, q):
        return 4 if (q % 2 == 0) == (d == 0) else 3

    for part, (first, groups, height) in enumerate(PARTS):
        for i in range(1, 8):
            box_in(part, i).wait_recv()
        landed_rows = inboxes[part][...].reshape(8 * height, 512)
        for g in range(groups):
            w.rows[0, :, (first + g) * 512 : (first + g + 1) * 512] = jnp.dot(
                squeeze_map(height, groups, g), landed_rows, preferred_element_type=jnp.float32
            ).astype(jnp.bfloat16)
        for q in (2 * part, 2 * part + 1):
            for d in range(2):
                gather(d, q, 1).start()
    for copy in local:
        copy.wait()
    for copy in pair[2:5]:
        copy.wait_recv()

    def swap(slot):
        return remote(w.half.at[slot], w.half_other.at[slot], w.half_s.at[slot], w.half_r.at[slot], ctx=other)

    def first_half(slot):
        w.half[slot] = jnp.dot(w.rows[slot], w.w_in[...], preferred_element_type=jnp.float32)
        swap(slot).start()

    def second_half(slot):
        swap(slot).wait_recv()
        both = w.half[slot] + w.half_other[slot]
        gate = both[:, :256]
        hidden = (gate / (1.0 + jnp.exp(-gate)) * both[:, 256:]).astype(jnp.bfloat16)
        w.total[slot] = jnp.dot(hidden, w.w_down[...], preferred_element_type=jnp.float32).astype(jnp.bfloat16)

    first_half(0)
    second_half(0)

    def pass_on(m, step):
        columns = pl.ds(SUBS[m][0], SUBS[m][1])
        slot = step + 1 if m < 2 else 7 - step
        return remote(
            w.total.at[slot, :, columns], w.arrived.at[m, step], w.rs_s.at[m, step], w.rs_r.at[m, step], ctx=right if m < 2 else left
        )

    def turn(r, carry):
        @pl.when(r <= 4)
        def _():
            for q in range(4):
                for d in range(2):
                    @pl.when(r <= reach(d, q))
                    def _(d=d, q=q):
                        gather(d, q, r).wait_recv()

                    @pl.when(r + 1 <= reach(d, q))
                    def _(d=d, q=q):
                        gather(d, q, r + 1).start()

            first_half(r)

            @pl.when(r < 4)
            def _():
                first_half(8 - r)

            second_half(r)

            @pl.when(r < 4)
            def _():
                second_half(8 - r)

        for m in (0, 2, 1, 3):
            slot = r if m < 2 else 8 - r
            columns = pl.ds(SUBS[m][0], SUBS[m][1])

            @pl.when(r >= 2)
            def _(m=m, slot=slot, columns=columns):
                pass_on(m, r - 2).wait_recv()
                w.total[slot, :, columns] = (
                    w.total[slot, :, columns].astype(jnp.float32) + w.arrived[m, r - 2].astype(jnp.float32)
                ).astype(jnp.bfloat16)

            pass_on(m, r - 1).start()
        return carry

    lax.fori_loop(1, 8, turn, 0)
    for m in (0, 2, 1, 3):
        pass_on(m, 6).wait_recv()
        columns = slice(SUBS[m][0], SUBS[m][0] + SUBS[m][1])
        w.summed[:, columns] = (w.total[0, :, columns].astype(jnp.float32) + w.arrived[m, 6].astype(jnp.float32)).astype(jnp.bfloat16)

    rets, backs, mixes, readies = (w.ret0, w.ret1), (w.back0, w.back1), (w.mix0, w.mix1), w.ready

    def give(part, i):
        return remote(
            rets[part].at[lax.rem(e + i, 8)], backs[part].at[e], w.back_s.at[part, i], w.back_r.at[part, i], exp=lax.rem(e + i, 8)
        )

    def give_in(part, i):
        source = lax.rem(e + 8 - i, 8)
        return remote(rets[part].at[source], backs[part].at[source], w.back_s.at[part, i], w.back_r.at[part, i], exp=source)

    for part, (first, groups, height) in enumerate(PARTS):
        spread = jnp.zeros((8 * height, 512), jnp.float32)
        for g in range(groups):
            spread = spread + jnp.dot(
                spread_map(height, groups, g), w.summed[:, (first + g) * 512 : (first + g + 1) * 512],
                preferred_element_type=jnp.float32,
            )
        rets[part][...] = spread.astype(jnp.bfloat16).reshape(8, height, 512)
        for i in range(1, 8):
            give(part, i).start()
        backs[part][pl.ds(e, 1)] = rets[part][pl.ds(e, 1)]
    for part, (first, groups, height) in enumerate(PARTS):
        for i in range(1, 8):
            give_in(part, i).wait_recv()
        span = groups * 32
        mixed = jnp.dot(mixes[part][...], backs[part][...].reshape(8 * height, 512), preferred_element_type=jnp.float32)
        combined = mixed[:span] + mixed[span:]
        layer_out = (sgs[part][...].astype(jnp.float32) + combined).astype(jnp.bfloat16)
        for g in range(groups):
            for b in range(2):
                readies[b, :, (first + g) * 512 : (first + g + 1) * 512] = layer_out[g * 32 + b * 16 : g * 32 + b * 16 + 16]

    def hand(b, core):
        return remote(w.ready.at[b], w.landed.at[core], w.fin_s.at[b], w.fin_r.at[core], pipe=over, ctx=2 * z + b)

    for b in range(2):
        hand(b, k).start()
    for b in range(2):
        hand(b, b).wait_recv()
        out_ref[:, b * HALF : (b + 1) * HALF] = w.landed[b]

    for b in range(2):
        hand(b, k).wait_send()
    for copy in pair:
        copy.wait_send()
    for part in range(2):
        for i in range(1, 8):
            box(part, i).wait_send()
            give(part, i).wait_send()
    for q in range(4):
        for d in range(2):
            def done(r, carry, d=d, q=q):
                gather(d, q, r).wait_send()
                return carry

            lax.fori_loop(1, reach(d, q) + 1, done, 0)

    def sent(step, carry):
        for m in range(4):
            pass_on(m, step).wait_send()
        return carry

    lax.fori_loop(0, 7, sent, 0)

    def swapped(slot, carry):
        swap(slot).wait_send()
        return carry

    lax.fori_loop(0, 8, swapped, 0)
    settle()


BF, F32 = jnp.bfloat16, jnp.float32
SCRATCH = {
    "keys": ((5, KV + 16, 256), BF), "queries": ((1024, KV), BF), "query_doc": ((128, 128), F32), "top": ((1024, 128), F32),
    "sums": ((1024, 128), F32), "mixed": ((1024, LAT), F32), "value_up": ((8, LAT, 128), BF), "heads": ((8, 128, 1024), BF),
    "proj": ((896, 1024), BF), "proj_all": ((1024, 896), BF), "product": ((8, 128, 896), F32),
    "fold_out": ((8, 64, 896), BF), "fold_in": ((8, 64, 896), BF), "cross_out": ((8, 64, 896), BF),
    "cross_in": ((8, 3, 16, 896), BF), "part_out": ((8, 16, 896), BF), "parts": ((8, 16, 896), BF), "stream": ((16, D), BF),
    "table": ((2, 16, 128), F32), "sel0": ((384, 128), BF), "sel1": ((256, 96), BF), "mix0": ((256, 384), BF), "mix1": ((192, 256), BF),
    "normed": ((16, D), BF), "pn": ((16, HALF), BF), "ps": ((16, HALF), BF),
    "xg0": ((128, 512), BF), "xg1": ((96, 512), BF), "sg0": ((128, 512), BF), "sg1": ((96, 512), BF),
    "outbox0": ((8, 48, 512), BF), "outbox1": ((8, 32, 512), BF), "inbox0": ((8, 48, 512), BF), "inbox1": ((8, 32, 512), BF),
    "w_in": ((HALF, 512), BF), "w_down": ((256, HALF), BF), "rows": ((8, 80, HALF), BF),
    "half": ((8, 80, 512), F32), "half_other": ((8, 80, 512), F32), "total": ((8, 80, HALF), BF),
    "arrived": ((4, 7, 80, 896), BF), "summed": ((80, HALF), BF),
    "ret0": ((8, 48, 512), BF), "ret1": ((8, 32, 512), BF), "back0": ((8, 48, 512), BF), "back1": ((8, 32, 512), BF),
    "ready": ((2, 16, HALF), BF), "landed": ((2, 16, HALF), BF),
    "load": ((9,), None), "chain_s": ((5, 4), None), "chain_r": ((5, 4), None), "share_s": ((5,), None), "share_r": ((5,), None),
    "proj_s": ((1,), None), "proj_r": ((1,), None), "head_s": ((2, 2, 5), None), "head_r": ((2, 2, 5), None),
    "fold_s": ((8,), None), "fold_r": ((8,), None), "cross_s": ((8, 3), None), "cross_r": ((8, 3), None),
    "part_s": ((8,), None), "part_r": ((8,), None),
    "pair_s": ((6,), None), "pair_r": ((6,), None), "loc": ((3,), None), "box_s": ((2, 8), None), "box_r": ((2, 8), None),
    "ag_s": ((2, 4, 5), None), "ag_r": ((2, 4, 5), None), "half_s": ((8,), None), "half_r": ((8,), None),
    "rs_s": ((4, 7), None), "rs_r": ((4, 7), None), "back_s": ((2, 8), None), "back_r": ((2, 8), None),
    "fin_s": ((2,), None), "fin_r": ((2,), None),
}


def on_device(
    queries, latent_rows, doc_ids, value_up, out_proj, residual_in, norm_gain, expert_ids, gate_weights, gate_proj, up_proj,
    down_proj,
):
    vmem, any_space = pl.BlockSpec(memory_space=pltpu.VMEM), pl.BlockSpec(memory_space=pl.ANY)
    return pl.pallas_call(
        layer_kernel,
        out_shape=jax.ShapeDtypeStruct((16, D), BF),
        in_specs=[vmem] * 7 + [any_space] * 5,
        out_specs=vmem,
        scratch_shapes=[
            pltpu.SemaphoreType.DMA(shape) if kind is None else pltpu.VMEM(shape, kind) for shape, kind in SCRATCH.values()
        ],
        compiler_params=pltpu.CompilerParams(collective_id=1, has_side_effects=True, vmem_limit_bytes=60 << 20),
        cost_estimate=pl.CostEstimate(flops=8_000_000_000, bytes_accessed=10_000_000, transcendentals=2_000_000),
        name="layer",
    )(
        queries[0].transpose(1, 2, 0), latent_rows[0].T, doc_ids, expert_ids[0].T, gate_weights[0].T, residual_in[0], norm_gain,
        value_up[0], out_proj[0].T, gate_proj[0, 0], up_proj[0, 0], down_proj[0, 0],
    )[None]


def solution(mesh):
    return jax.shard_map(
        on_device,
        mesh=mesh,
        in_specs=(
            P("pipe", "ctx", "exp", None),
            P("pipe", "ctx", None),
            P("pipe", "ctx"),
            P("pipe", "exp", None, None),
            P("pipe", "exp", "ctx"),
            P("pipe", ("ctx", "exp"), None),
            P("pipe", None),
            P("pipe", ("ctx", "exp"), None),
            P("pipe", ("ctx", "exp"), None),
            P("pipe", "exp", None, "ctx"),
            P("pipe", "exp", None, "ctx"),
            P("pipe", "exp", "ctx", None),
        ),
        out_specs=P("pipe", ("ctx", "exp"), None),
        check_vma=False,
    )
```

```python
import math
import types

import jax
import jax.numpy as jnp
from jax import lax
from jax.experimental import pallas as pl
from jax.experimental.pallas import tpu as pltpu
from jax.sharding import PartitionSpec as P

D = 7168
HALF = D // 2
HD = 128
ROPE = 64
LAT = 512
KV = LAT + ROPE
MESH = pl.DeviceIdType.MESH

epsilon = 1e-06
masked_score = -1e30
score_scale = 1.0 / math.sqrt(HD + ROPE)
KEY_PIECES = ((0, 144), (144, 144), (288, 144), (432, 160))


def remote(src, dst, send_sem, recv_sem, **device):
    return pltpu.make_async_remote_copy(
        src_ref=src,
        dst_ref=dst,
        send_sem=send_sem,
        recv_sem=recv_sem,
        device_id=device,
        device_id_type=MESH,
    )


def meet(peers):
    barrier = pltpu.get_barrier_semaphore()
    for device in peers:
        pl.semaphore_signal(barrier, 1, device_id=device, device_id_type=MESH)
    pl.semaphore_wait(barrier, len(peers))


def squeeze_map(rows, groups, group, dtype=jnp.bfloat16):
    row = lax.broadcasted_iota(jnp.int32, (80, 8 * rows), 0).astype(jnp.float32)
    col = lax.broadcasted_iota(jnp.int32, (80, 8 * rows), 1).astype(jnp.float32)
    source = jnp.floor((row + 0.5) * 0.1)
    want = source * rows + (row - source * 10) + group * 10
    return jnp.where(col == want, 1.0, 0.0).astype(dtype)


def spread_map(rows, groups, group, dtype=jnp.bfloat16):
    row = lax.broadcasted_iota(jnp.int32, (8 * rows, 80), 0).astype(jnp.float32)
    col = lax.broadcasted_iota(jnp.int32, (8 * rows, 80), 1).astype(jnp.float32)
    source = jnp.floor((col + 0.5) * 0.1)
    want = source * rows + (col - source * 10) + group * 10
    return jnp.where(row == want, 1.0, 0.0).astype(dtype)


RING = 2560
GROUP = 640
PLANE = HALF - RING


def reach(d, q):
    return 4 if q % 2 == d else 3


def attend(w, q_ref, lat_ref, doc_ref, vu_ref, op_ref, residual_ref, start_rest, share_tables, make_tables):
    p, c, e = lax.axis_index("pipe"), lax.axis_index("ctx"), lax.axis_index("exp")
    k = lax.rem(c, 2)
    z = lax.div(c, 2)
    kk = 1 - k
    other = 2 * z + kk
    right = 2 * lax.rem(z + 1, 8) + k
    left = 2 * lax.rem(z + 7, 8) + k
    y = lax.div(e, 4)
    x = lax.rem(e, 4)
    bf, f32 = jnp.bfloat16, jnp.float32
    my_lanes = pl.ds(pl.multiple_of(k * 128, 128), 128)
    their_lanes = pl.ds(pl.multiple_of(kk * 128, 128), 128)
    my_columns = pl.ds(pl.multiple_of(k * 448, 16), 448)

    def chain(s, q):
        piece = pl.ds(*KEY_PIECES[q])
        return remote(
            w.keys.at[s - 1, piece, my_lanes], w.keys.at[s, piece, my_lanes], w.chain_s.at[s, q], w.chain_r.at[s, q], ctx=right
        )

    def share(s):
        return remote(w.keys.at[s, :, my_lanes], w.keys.at[s, :, my_lanes], w.share_s.at[s], w.share_r.at[s], ctx=other)

    def share_in(s):
        return remote(w.keys.at[s, :, their_lanes], w.keys.at[s, :, their_lanes], w.share_s.at[s], w.share_r.at[s], ctx=other)

    for q in range(4):
        chain(1, q).start()
    share(0).start()
    own_proj = pltpu.make_async_copy(op_ref, w.proj.at[my_columns], w.load.at[8])
    own_proj.start()
    pair_proj = remote(op_ref, w.proj.at[my_columns], w.proj_s.at[0], w.proj_r.at[0], ctx=other)
    pair_proj.start()
    up_loads = [
        pltpu.make_async_copy(vu_ref.at[h], w.value_up.at[h], w.load.at[h]) for h in range(8)
    ]
    for copy in up_loads:
        copy.start()
    start_rest()

    for h in range(8):
        w.queries[h * 128 : (h + 1) * 128, :] = jnp.transpose(q_ref[h])
    w.top[...] = jnp.full((1024, 128), masked_score, f32)
    w.sums[...] = jnp.zeros((1024, 128), f32)
    w.mixed[...] = jnp.zeros((1024, LAT), f32)
    contract_last = (((1,), (1,)), ((), ()))
    query_pos = c * 128 + lax.broadcasted_iota(jnp.int32, (128, 256), 0)

    def visit(s, carry):
        @pl.when(s >= 1)
        def _():
            for q in range(4):
                chain(s, q).wait_recv()

                @pl.when(s < 4)
                def _(q=q):
                    chain(s + 1, q).start()

            share(s).start()

        share_in(s).wait_recv()
        key_doc = w.keys[s, KV:, :].astype(f32)[0:1]
        key_pos = lax.rem(z + 8 - s, 8) * 256 + lax.broadcasted_iota(jnp.int32, (128, 256), 1)
        query_doc = jnp.concatenate([w.query_doc[...]] * 2, axis=1)
        hidden = jnp.where((key_pos <= query_pos) & (query_doc == key_doc), 0.0, masked_score)
        hidden = jnp.concatenate([hidden] * 4, axis=0)

        def some(j, carry):
            at = pl.ds(pl.multiple_of(j * 512, 512), 512)
            scores = jnp.dot(w.queries[at], w.keys[s, 0:KV, :], preferred_element_type=f32) * score_scale + hidden
            before = w.top[at]
            highest = jnp.maximum(before, jnp.max(scores, axis=1, keepdims=True))
            shrink = jnp.exp(before - highest)
            weights = jnp.exp(scores - jnp.concatenate([highest, highest], axis=1))
            w.top[at] = highest
            w.sums[at] = w.sums[at] * shrink + jnp.sum(weights, axis=1, keepdims=True)
            update = lax.dot_general(weights.astype(bf), w.keys[s, 0:LAT, :], contract_last, preferred_element_type=f32)
            w.mixed[at] = w.mixed[at] * jnp.concatenate([shrink] * 4, axis=1) + update
            return carry

        lax.fori_loop(0, 2, some, 0)
        return carry

    lax.fori_loop(0, 5, visit, 0)
    share_tables()

    for copy in up_loads:
        copy.wait()

    def gather(d, q, r):
        piece = pl.ds(q * 64, 64)
        if d == 0:
            return remote(w.heads.at[r - 1, piece], w.heads.at[r, piece], w.head_s.at[d, q, r], w.head_r.at[d, q, r], ctx=right)
        return remote(
            w.heads.at[lax.rem(9 - r, 8), piece], w.heads.at[8 - r, piece], w.head_s.at[d, q, r], w.head_r.at[d, q, r], ctx=left
        )

    for h in range(8):
        at = slice(h * 128, (h + 1) * 128)
        latent_out = (w.mixed[at] / jnp.concatenate([w.sums[at]] * 4, axis=1)).astype(bf)
        w.heads[0, :, at] = jnp.dot(latent_out, w.value_up[h], preferred_element_type=f32).astype(bf)
    for q in range(2):
        for d in range(2):
            gather(d, q, 1).start()

    own_proj.wait()
    pair_proj.wait_recv()
    w.proj_all[...] = jnp.transpose(w.proj[...])
    make_tables()

    y_mine = pl.multiple_of(y * 64, 64)
    y_theirs = pl.multiple_of((1 - y) * 64, 64)
    x_mine = pl.multiple_of(x * 16, 16)

    def fold(slot):
        return remote(w.fold_out.at[slot], w.fold_in.at[slot], w.fold_s.at[slot], w.fold_r.at[slot], exp=lax.rem(e + 4, 8))

    def cross(slot, i):
        to = lax.rem(x + i, 4)
        return remote(
            w.cross_out.at[slot, pl.ds(pl.multiple_of(to * 16, 16), 16)], w.cross_in.at[slot, i - 1],
            w.cross_s.at[slot, i - 1], w.cross_r.at[slot, i - 1], exp=4 * y + to,
        )

    def deliver(slot):
        return remote(
            w.part_out.at[slot], w.parts.at[z], w.part_s.at[slot], w.part_r.at[slot], ctx=2 * lax.rem(z + 8 - slot, 8) + k
        )

    def deliver_in(slot):
        source = lax.rem(z + slot, 8)
        return remote(w.part_out.at[slot], w.parts.at[source], w.part_s.at[slot], w.part_r.at[slot], ctx=2 * source + k)

    def project(slot):
        w.product[slot] = jnp.dot(w.heads[slot], w.proj_all[...], preferred_element_type=f32)
        w.fold_out[slot] = w.product[slot, pl.ds(y_theirs, 64), :].astype(bf)
        fold(slot).start()

    def over_y(slot):
        fold(slot).wait_recv()
        both = w.product[slot, pl.ds(y_mine, 64), :] + w.fold_in[slot].astype(f32)
        w.product[slot, pl.ds(y_mine, 64), :] = both
        w.cross_out[slot] = both.astype(bf)
        for i in range(1, 4):
            cross(slot, i).start()

    def over_x(slot):
        whole = w.product[slot, pl.ds(pl.multiple_of(y_mine + x_mine, 16), 16), :]
        for i in range(1, 4):
            cross(slot, i).wait_recv()
            whole = whole + w.cross_in[slot, i - 1].astype(f32)
        w.part_out[slot] = whole.astype(bf)

        @pl.when(slot >= 1)
        def _():
            deliver(slot).start()

    def turn(r, carry):
        @pl.when((r >= 1) & (r <= 4))
        def _():
            for q in range(2):
                for d in range(2):
                    @pl.when(r <= reach(d, q))
                    def _(d=d, q=q):
                        gather(d, q, r).wait_recv()

                    @pl.when(r + 1 <= reach(d, q))
                    def _(d=d, q=q):
                        gather(d, q, r + 1).start()

        for stage, act in enumerate((project, over_y, over_x)):
            now = r - stage

            @pl.when((now >= 0) & (now <= 4))
            def _(act=act, now=now):
                act(now)

            @pl.when((now >= 1) & (now <= 3))
            def _(act=act, now=now):
                act(8 - now)

        return carry

    lax.fori_loop(0, 7, turn, 0)
    w.parts[pl.ds(z, 1)] = w.part_out[0:1]
    for slot in range(1, 8):
        deliver_in(slot).wait_recv()
    for other_z in range(8):
        columns = slice(other_z * 896, (other_z + 1) * 896)
        w.stream[:, columns] = (residual_ref[:, columns].astype(f32) + w.parts[other_z].astype(f32)).astype(bf)

    def settle():
        pair_proj.wait_send()

        def chained(s, carry):
            for q in range(4):
                chain(s, q).wait_send()
            return carry

        lax.fori_loop(1, 5, chained, 0)

        def shared(s, carry):
            share(s).wait_send()
            return carry

        lax.fori_loop(0, 5, shared, 0)
        for q in range(2):
            for d in range(2):
                def gathered(r, carry, d=d, q=q):
                    gather(d, q, r).wait_send()
                    return carry

                lax.fori_loop(1, reach(d, q) + 1, gathered, 0)

        def folded(slot, carry):
            fold(slot).wait_send()
            for i in range(1, 4):
                cross(slot, i).wait_send()

            @pl.when(slot >= 1)
            def _():
                deliver(slot).wait_send()
            return carry

        lax.fori_loop(0, 8, folded, 0)

    return settle


def column_of(rows):
    diagonal = lax.broadcasted_iota(jnp.int32, rows.shape, 0) == lax.broadcasted_iota(jnp.int32, rows.shape, 1)
    return jnp.sum(jnp.where(diagonal, rows, 0.0), axis=1, keepdims=True)


def tables(w, ids_ref, weights_ref, k):
    f32 = jnp.float32
    ids = [column_of(jnp.broadcast_to(ids_ref[i : i + 1, :].astype(f32), (16, 16))) for i in range(2)]
    weights = [column_of(jnp.broadcast_to(weights_ref[i : i + 1, :], (16, 16))) for i in range(2)]
    lane = lax.broadcasted_iota(jnp.int32, (16, 128), 1)
    expert = lane.astype(f32)
    first, second = (jnp.where(ids[i] == expert, 1.0, 0.0) for i in range(2))
    earlier = lax.broadcasted_iota(jnp.int32, (16, 16), 1) < lax.broadcasted_iota(jnp.int32, (16, 16), 0)
    counts = jnp.dot(jnp.where(earlier, 1.0, 0.0), first + second, preferred_element_type=f32)
    ranks = (
        jnp.sum(first * counts, axis=1, keepdims=True),
        jnp.sum(second * (counts + first), axis=1, keepdims=True),
    )
    table = jnp.zeros((16, 128), f32)
    for i in range(2):
        table = jnp.where(lane == i, ids[i] * 8.0 + ranks[i], table)
        table = jnp.where(lane == i + 2, weights[i], table)
    w.table[0, pl.ds(k, 1)] = table[None]


def matrices(w):
    bf, f32 = jnp.bfloat16, jnp.float32
    chip = jnp.concatenate([w.table[0].reshape(32, 128)] * 4, axis=0)
    column = w.table[...].reshape(256, 128)
    for columns, sel, mix, groups, height in ((chip, w.sel, w.mix, 4, 48), (column, w.plane_sel, w.plane_mix, 8, 80)):
        span, count = groups * 32, 8 * height
        lanes = jnp.transpose(columns)

        def decode(shape, axis):
            row = lax.broadcasted_iota(jnp.int32, shape, axis).astype(f32)
            expert = jnp.floor((row + 0.5) * (1.0 / height))
            inner = row - expert * height
            group = jnp.floor((inner + 0.5) * 0.1)
            within = inner - group * 10.0
            block = jnp.where(within >= 5.0, 1.0, 0.0)
            slot = jnp.where(group < groups, expert * 8.0 + within - block * 5.0, -1.0)
            owner = group * 2.0 + block
            return slot, owner

        slot, owner = decode((count, 1), 0)
        token = lax.shift_right_logical(lax.broadcasted_iota(jnp.int32, (count, span), 1), 4).astype(f32)
        hit = (owner == token) & ((slot == lanes[0:1, :]) | (slot == lanes[1:2, :]))
        sel[...] = jnp.where(hit, 1.0, 0.0).astype(bf)
        slot, owner = decode((1, count), 1)
        token = lax.shift_right_logical(lax.broadcasted_iota(jnp.int32, (span, count), 0), 4).astype(f32)
        slot = jnp.where(owner == token, slot, -1.0)
        weight = jnp.zeros((span, count), f32)
        for i in range(2):
            weight = weight + jnp.where(slot == columns[:, i : i + 1], columns[:, i + 2 : i + 3], 0.0)
        high = weight.astype(bf)
        mix[0:span, :] = high
        mix[span : 2 * span, :] = (weight - high.astype(f32)).astype(bf)


def layer_kernel(
    q_ref, lat_ref, doc_ref, ids_ref, weights_ref, residual_ref, gain_ref, vu_ref, op_ref, gate_ref, up_ref, down_ref,
    out_ref, *scratch
):
    w = types.SimpleNamespace(**dict(zip(SCRATCH, scratch, strict=True)))
    p, c, e = lax.axis_index("pipe"), lax.axis_index("ctx"), lax.axis_index("exp")
    k = lax.rem(c, 2)
    z = lax.div(c, 2)
    kk = 1 - k
    other = 2 * z + kk
    right = 2 * lax.rem(z + 1, 8) + k
    left = 2 * lax.rem(z + 7, 8) + k
    over = 1 - p
    mine = pl.multiple_of(k * HALF, 128)
    theirs = pl.multiple_of(kk * HALF, 128)
    my_lane = pl.multiple_of(k * 128, 128)
    up_lane = pl.multiple_of(256 + k * 128, 128)

    bf, f32 = jnp.bfloat16, jnp.float32

    w.keys[0, 0:KV, pl.ds(my_lane, 128)] = lat_ref[...]
    doc_row = jnp.broadcast_to(doc_ref[...].astype(f32), (128, 128))
    w.keys[0, KV:, pl.ds(my_lane, 128)] = doc_row[0:16].astype(bf)
    w.query_doc[...] = jnp.broadcast_to(column_of(doc_row), (128, 128))
    tables(w, ids_ref, weights_ref, k)
    meet(
        [{"ctx": other}, {"pipe": over}, {"pipe": over, "ctx": other}]
        + [{"ctx": 2 * lax.rem(z + i, 8) + k} for i in range(1, 8)]
        + [{"exp": lax.rem(e + i, 8)} for i in range(1, 8)]
    )
    local = [
        pltpu.make_async_copy(gate_ref.at[pl.ds(mine, HALF), :], w.w_in.at[:, pl.ds(my_lane, 128)], w.loc.at[0]),
        pltpu.make_async_copy(up_ref.at[pl.ds(mine, HALF), :], w.w_in.at[:, pl.ds(up_lane, 128)], w.loc.at[1]),
        pltpu.make_async_copy(down_ref.at[:, pl.ds(mine, HALF)], w.w_down.at[pl.ds(my_lane, 128), :], w.loc.at[2]),
    ]
    pair = [
        remote(w.normed.at[:, pl.ds(theirs, HALF)], w.pn, w.pair_s.at[0], w.pair_r.at[0], ctx=other),
        remote(w.stream.at[:, pl.ds(theirs, HALF)], w.ps, w.pair_s.at[1], w.pair_r.at[1], ctx=other),
        remote(gate_ref.at[pl.ds(theirs, HALF), :], w.w_in.at[:, pl.ds(my_lane, 128)], w.pair_s.at[2], w.pair_r.at[2], ctx=other),
        remote(up_ref.at[pl.ds(theirs, HALF), :], w.w_in.at[:, pl.ds(up_lane, 128)], w.pair_s.at[3], w.pair_r.at[3], ctx=other),
        remote(down_ref.at[:, pl.ds(theirs, HALF)], w.w_down.at[pl.ds(my_lane, 128), :], w.pair_s.at[4], w.pair_r.at[4], ctx=other),
    ]
    pair.append(remote(w.table.at[0, k], w.table.at[0, k], w.pair_s.at[5], w.pair_r.at[5], ctx=other))

    def start_rest():
        pair[5].start()
        for copy in local:
            copy.start()
        for copy in pair[2:5]:
            copy.start()

    def spread_table(i):
        return remote(w.table.at[0], w.table.at[i], w.table_s.at[i], w.table_r.at[i], ctx=2 * lax.rem(z + i, 8) + k)

    def share_tables():
        pair[5].wait_recv()
        for i in range(1, 8):
            spread_table(i).start()

    def make_tables():
        for i in range(1, 8):
            spread_table(i).wait_recv()
        matrices(w)

    settle = attend(w, q_ref, lat_ref, doc_ref, vu_ref, op_ref, residual_ref, start_rest, share_tables, make_tables)
    wide = w.stream[...].astype(f32)
    mean_square = jnp.mean(wide * wide, axis=1, keepdims=True)
    w.normed[...] = (wide * lax.rsqrt(mean_square + epsilon) * gain_ref[...]).astype(bf)
    for copy in pair[:2]:
        copy.start()

    def place(target, plane_target, source, start, core):
        for g in range(4):
            lanes = pl.ds(start + g * GROUP if isinstance(start, int) else pl.multiple_of(start + g * GROUP, 128), GROUP)
            target[pl.ds(pl.multiple_of(g * 32 + core * 16, 16), 16), :] = source[:, lanes]
        lanes = pl.ds(start + RING if isinstance(start, int) else pl.multiple_of(start + RING, 128), PLANE)
        plane_target[pl.ds(pl.multiple_of(core * 16, 16), 16), :] = source[:, lanes]

    place(w.xg, w.tokens.at[0], w.normed, mine, k)
    place(w.sg, w.plane_stream, w.stream, mine, k)
    pair[0].wait_recv()
    place(w.xg, w.tokens.at[0], w.pn, 0, kk)

    def relay(d, q, r):
        columns = pl.ds(q * 512, 512)
        src, dst, to = (r - 1, r, right) if d == 0 else (lax.rem(9 - r, 8), 8 - r, left)
        return remote(w.tokens.at[src, :, columns], w.tokens.at[dst, :, columns], w.relay_s.at[d, q, r], w.relay_r.at[d, q, r], ctx=to)

    def relay_round(r):
        for q in range(2):
            for d in range(2):
                if r <= reach(d, q):
                    relay(d, q, r).wait_recv()
                if r + 1 <= reach(d, q):
                    relay(d, q, r + 1).start()

    for q in range(2):
        for d in range(2):
            relay(d, q, 1).start()

    def box(i):
        to = lax.rem(e + i, 8)
        return remote(w.outbox.at[to], w.inbox.at[e], w.box_s.at[i], w.box_r.at[i], exp=to)

    def box_in(i):
        source = lax.rem(e + 8 - i, 8)
        return remote(w.outbox.at[source], w.inbox.at[source], w.box_s.at[i], w.box_r.at[i], exp=source)

    chosen = jnp.dot(w.sel[...], w.xg[...], preferred_element_type=f32).astype(bf)
    w.outbox[...] = chosen.reshape(8, 48, GROUP)
    for i in range(1, 8):
        box(i).start()
    w.inbox[pl.ds(e, 1)] = w.outbox[pl.ds(e, 1)]
    relay_round(1)
    relay_round(2)
    pair[1].wait_recv()
    place(w.sg, w.plane_stream, w.ps, 0, kk)

    def gather(d, q, r):
        columns = pl.ds(q * GROUP, GROUP)
        src, dst, to = (r - 1, r, right) if d == 0 else (lax.rem(9 - r, 8), 8 - r, left)
        return remote(w.rows.at[src, :, columns], w.rows.at[dst, :, columns], w.ag_s.at[d, q, r], w.ag_r.at[d, q, r], ctx=to)

    for i in range(1, 8):
        box_in(i).wait_recv()
    landed_rows = w.inbox[...].reshape(384, GROUP)
    for q in range(4):
        w.rows[0, :, q * GROUP : (q + 1) * GROUP] = jnp.dot(
            squeeze_map(48, 4, q), landed_rows, preferred_element_type=f32
        ).astype(bf)
        for d in range(2):
            gather(d, q, 1).start()
    relay_round(3)
    relay_round(4)

    def plane_box(h, i):
        to = lax.rem(e + i, 8)
        return remote(w.plane_out.at[h, to], w.plane_in.at[h, e], w.plane_s.at[h, i], w.plane_r.at[h, i], exp=to)

    def plane_box_in(h, i):
        source = lax.rem(e + 8 - i, 8)
        return remote(w.plane_out.at[h, source], w.plane_in.at[h, source], w.plane_s.at[h, i], w.plane_r.at[h, i], exp=source)

    for h in range(2):
        tokens = w.tokens[:, :, h * 512 : (h + 1) * 512].reshape(256, 512)
        chosen = jnp.dot(w.plane_sel[...], tokens, preferred_element_type=f32).astype(bf)
        w.plane_out[h] = chosen.reshape(8, 80, 512)
        for i in range(1, 8):
            plane_box(h, i).start()
        w.plane_in[h, pl.ds(e, 1)] = w.plane_out[h, pl.ds(e, 1)]
    for copy in local:
        copy.wait()
    for copy in pair[2:5]:
        copy.wait_recv()

    def swap(slot):
        return remote(w.half.at[slot], w.half_other.at[slot], w.half_s.at[slot], w.half_r.at[slot], ctx=other)

    def ring_half(slot):
        w.half[slot] = jnp.dot(w.rows[slot], w.w_in[0:RING, :], preferred_element_type=f32)

    ring_half(0)

    def collect(r, carry):
        for q in range(4):
            for d in range(2):
                @pl.when(r <= reach(d, q))
                def _(d=d, q=q):
                    gather(d, q, r).wait_recv()

                @pl.when(r + 1 <= reach(d, q))
                def _(d=d, q=q):
                    gather(d, q, r + 1).start()

        ring_half(r)

        @pl.when(r < 4)
        def _():
            ring_half(8 - r)

        return carry

    lax.fori_loop(1, 5, collect, 0)
    for h in range(2):
        for i in range(1, 8):
            plane_box_in(h, i).wait_recv()

    def plane_half(slot):
        pick = squeeze_map(80, 8, slot)
        total = w.half[slot]
        for h in range(2):
            mine_now = jnp.dot(pick, w.plane_in[h].reshape(640, 512), preferred_element_type=f32).astype(bf)
            total = total + jnp.dot(mine_now, w.w_in[RING + h * 512 : RING + (h + 1) * 512, :], preferred_element_type=f32)
        w.half[slot] = total
        swap(slot).start()

    w.hidden[...] = jnp.zeros((640, 256), f32)

    def second_half(slot):
        swap(slot).wait_recv()
        both = w.half[slot] + w.half_other[slot]
        gate = both[:, :256]
        hidden = (gate / (1.0 + jnp.exp(-gate)) * both[:, 256:]).astype(bf)
        w.total[slot] = jnp.dot(hidden, w.w_down[:, 0:RING], preferred_element_type=f32).astype(bf)
        w.hidden[...] = w.hidden[...] + jnp.dot(spread_map(80, 8, slot), hidden, preferred_element_type=f32)

    def scatter(d, q, j):
        far = reach(d, q) + 1 - j
        slot, to = (far, left) if d == 0 else (8 - far, right)
        columns = pl.ds(q * GROUP, GROUP)
        return remote(w.total.at[slot, :, columns], w.arrived.at[d, q, j - 1], w.rs_s.at[d, q, j - 1], w.rs_r.at[d, q, j - 1], ctx=to)

    def scatter_on(j):
        for q in range(4):
            for d in range(2):
                if j + 1 <= reach(d, q):
                    far = reach(d, q) - j
                    slot = far if d == 0 else 8 - far
                    columns = slice(q * GROUP, (q + 1) * GROUP)
                    scatter(d, q, j).wait_recv()
                    w.total[slot, :, columns] = (
                        w.total[slot, :, columns].astype(f32) + w.arrived[d, q, j - 1].astype(f32)
                    ).astype(bf)
                    scatter(d, q, j + 1).start()

    def place_of(i):
        step = lax.div(i + 1, 2)
        return jnp.where(lax.rem(i, 2) == 0, 4 + step, 4 - step)

    def work(i, carry):
        @pl.when(i < 8)
        def _():
            plane_half(place_of(i))

        @pl.when(i >= 1)
        def _():
            second_half(place_of(i - 1))

        @pl.when(i == 3)
        def _():
            for q in range(4):
                for d in range(2):
                    scatter(d, q, 1).start()

        return carry

    lax.fori_loop(0, 9, work, 0)

    def plane_give(h, i):
        to = lax.rem(e + i, 8)
        return remote(w.plane_ret.at[h, to], w.plane_back.at[h, e], w.give_s.at[h, i], w.give_r.at[h, i], exp=to)

    def plane_give_in(h, i):
        source = lax.rem(e + 8 - i, 8)
        return remote(w.plane_ret.at[h, source], w.plane_back.at[h, source], w.give_s.at[h, i], w.give_r.at[h, i], exp=source)

    hidden = w.hidden[...].astype(bf)
    for h in range(2):
        out = jnp.dot(hidden, w.w_down[:, RING + h * 512 : RING + (h + 1) * 512], preferred_element_type=f32).astype(bf)
        w.plane_ret[h] = out.reshape(8, 80, 512)
        for i in range(1, 8):
            plane_give(h, i).start()
        w.plane_back[h, pl.ds(e, 1)] = w.plane_ret[h, pl.ds(e, 1)]

    def reduce(h, d, q, j):
        far = reach(d, q) + 1 - j
        slot, to = (far, left) if d == 0 else (8 - far, right)
        columns = pl.ds(h * 512 + q * 256, 256)
        return remote(
            w.partial.at[slot, :, columns], w.plane_arrived.at[h, d, q, j - 1], w.red_s.at[h, d, q, j - 1],
            w.red_r.at[h, d, q, j - 1], ctx=to,
        )

    def reduce_start(h):
        for i in range(1, 8):
            plane_give_in(h, i).wait_recv()
        mixed = jnp.dot(w.plane_mix[...], w.plane_back[h].reshape(640, 512), preferred_element_type=f32)
        mixed = mixed[:256] + mixed[256:]
        w.plane_own[:, h * 512 : (h + 1) * 512] = mixed[:32]
        w.partial[:, :, h * 512 : (h + 1) * 512] = mixed.astype(bf).reshape(8, 32, 512)
        for q in range(2):
            for d in range(2):
                reduce(h, d, q, 1).start()

    def reduce_on(h, j):
        for q in range(2):
            for d in range(2):
                if j + 1 <= reach(d, q):
                    far = reach(d, q) - j
                    slot = far if d == 0 else 8 - far
                    columns = slice(h * 512 + q * 256, h * 512 + (q + 1) * 256)
                    reduce(h, d, q, j).wait_recv()
                    w.partial[slot, :, columns] = (
                        w.partial[slot, :, columns].astype(f32) + w.plane_arrived[h, d, q, j - 1].astype(f32)
                    ).astype(bf)
                    reduce(h, d, q, j + 1).start()

    def reduce_end(h):
        for q in range(2):
            columns = slice(h * 512 + q * 256, h * 512 + (q + 1) * 256)
            whole = w.plane_own[:, columns] + w.plane_stream[:, columns].astype(f32)
            for d in range(2):
                reduce(h, d, q, reach(d, q)).wait_recv()
                whole = whole + w.plane_arrived[h, d, q, reach(d, q) - 1].astype(f32)
            whole = whole.astype(bf)
            for b in range(2):
                w.ready[b, :, RING + h * 512 + q * 256 : RING + h * 512 + (q + 1) * 256] = whole[b * 16 : (b + 1) * 16]

    def give(i):
        to = lax.rem(e + i, 8)
        return remote(w.ret.at[to], w.back.at[e], w.back_s.at[i], w.back_r.at[i], exp=to)

    def give_in(i):
        source = lax.rem(e + 8 - i, 8)
        return remote(w.ret.at[source], w.back.at[source], w.back_s.at[i], w.back_r.at[i], exp=source)

    scatter_on(1)
    scatter_on(2)
    reduce_start(0)
    scatter_on(3)
    reduce_on(0, 1)
    reduce_start(1)
    reduce_on(0, 2)
    spread = jnp.zeros((384, GROUP), f32)
    for q in range(4):
        columns = slice(q * GROUP, (q + 1) * GROUP)
        whole = w.total[0, :, columns].astype(f32)
        for d in range(2):
            scatter(d, q, reach(d, q)).wait_recv()
            whole = whole + w.arrived[d, q, reach(d, q) - 1].astype(f32)
        spread = spread + jnp.dot(spread_map(48, 4, q), whole.astype(bf), preferred_element_type=f32)
    w.ret[...] = spread.astype(bf).reshape(8, 48, GROUP)
    for i in range(1, 8):
        give(i).start()
    w.back[pl.ds(e, 1)] = w.ret[pl.ds(e, 1)]
    reduce_on(0, 3)
    reduce_on(1, 1)
    reduce_on(1, 2)
    reduce_end(0)
    reduce_on(1, 3)
    for i in range(1, 8):
        give_in(i).wait_recv()
    mixed = jnp.dot(w.mix[...], w.back[...].reshape(384, GROUP), preferred_element_type=f32)
    layer_out = (w.sg[...].astype(f32) + (mixed[:128] + mixed[128:])).astype(bf)
    for g in range(4):
        for b in range(2):
            w.ready[b, :, g * GROUP : (g + 1) * GROUP] = layer_out[g * 32 + b * 16 : g * 32 + b * 16 + 16]

    def hand(part, b, core):
        columns = pl.ds(0, RING) if part == 0 else pl.ds(RING, PLANE)
        return remote(
            w.ready.at[b, :, columns], w.landed.at[core, :, columns], w.fin_s.at[part, b], w.fin_r.at[part, core],
            pipe=over, ctx=2 * z + b,
        )

    for b in range(2):
        hand(0, b, k).start()
    reduce_end(1)
    for b in range(2):
        hand(1, b, k).start()
    for part in range(2):
        for b in range(2):
            hand(part, b, b).wait_recv()
    for b in range(2):
        out_ref[:, b * HALF : (b + 1) * HALF] = w.landed[b]

    for part in range(2):
        for b in range(2):
            hand(part, b, k).wait_send()
    for copy in pair:
        copy.wait_send()

    def sent(i, carry):
        box(i).wait_send()
        give(i).wait_send()
        spread_table(i).wait_send()
        for h in range(2):
            plane_box(h, i).wait_send()
            plane_give(h, i).wait_send()
        return carry

    lax.fori_loop(1, 8, sent, 0)

    def gone(r, carry):
        for q in range(4):
            for d in range(2):
                @pl.when(r <= reach(d, q))
                def _(d=d, q=q):
                    gather(d, q, r).wait_send()
                    scatter(d, q, r).wait_send()
                    if q < 2:
                        relay(d, q, r).wait_send()
                        for h in range(2):
                            reduce(h, d, q, r).wait_send()
        return carry

    lax.fori_loop(1, 5, gone, 0)

    def swapped(slot, carry):
        swap(slot).wait_send()
        return carry

    lax.fori_loop(0, 8, swapped, 0)
    settle()


BF, F32 = jnp.bfloat16, jnp.float32
SCRATCH = {
    "keys": ((5, KV + 16, 256), BF), "queries": ((1024, KV), BF), "query_doc": ((128, 128), F32), "top": ((1024, 128), F32),
    "sums": ((1024, 128), F32), "mixed": ((1024, LAT), F32), "value_up": ((8, LAT, 128), BF), "heads": ((8, 128, 1024), BF),
    "proj": ((896, 1024), BF), "proj_all": ((1024, 896), BF), "product": ((8, 128, 896), F32),
    "fold_out": ((8, 64, 896), BF), "fold_in": ((8, 64, 896), BF), "cross_out": ((8, 64, 896), BF),
    "cross_in": ((8, 3, 16, 896), BF), "part_out": ((8, 16, 896), BF), "parts": ((8, 16, 896), BF), "stream": ((16, D), BF),
    "table": ((8, 2, 16, 128), F32), "sel": ((384, 128), BF), "mix": ((256, 384), BF),
    "plane_sel": ((640, 256), BF), "plane_mix": ((512, 640), BF),
    "normed": ((16, D), BF), "pn": ((16, HALF), BF), "ps": ((16, HALF), BF), "tokens": ((8, 32, PLANE), BF),
    "xg": ((128, GROUP), BF), "sg": ((128, GROUP), BF), "plane_stream": ((32, PLANE), BF),
    "outbox": ((8, 48, GROUP), BF), "inbox": ((8, 48, GROUP), BF), "ret": ((8, 48, GROUP), BF), "back": ((8, 48, GROUP), BF),
    "plane_out": ((2, 8, 80, 512), BF), "plane_in": ((2, 8, 80, 512), BF),
    "plane_ret": ((2, 8, 80, 512), BF), "plane_back": ((2, 8, 80, 512), BF),
    "w_in": ((HALF, 512), BF), "w_down": ((256, HALF), BF), "rows": ((8, 80, RING), BF),
    "half": ((8, 80, 512), F32), "half_other": ((8, 80, 512), F32), "hidden": ((640, 256), F32), "total": ((8, 80, RING), BF),
    "arrived": ((2, 4, 4, 80, GROUP), BF), "partial": ((8, 32, PLANE), BF), "plane_own": ((32, PLANE), F32),
    "plane_arrived": ((2, 2, 2, 4, 32, 256), BF), "ready": ((2, 16, HALF), BF), "landed": ((2, 16, HALF), BF),
    "load": ((9,), None), "chain_s": ((5, 4), None), "chain_r": ((5, 4), None), "share_s": ((5,), None), "share_r": ((5,), None),
    "proj_s": ((1,), None), "proj_r": ((1,), None), "head_s": ((2, 2, 5), None), "head_r": ((2, 2, 5), None),
    "fold_s": ((8,), None), "fold_r": ((8,), None), "cross_s": ((8, 3), None), "cross_r": ((8, 3), None),
    "part_s": ((8,), None), "part_r": ((8,), None),
    "pair_s": ((6,), None), "pair_r": ((6,), None), "loc": ((3,), None), "table_s": ((8,), None), "table_r": ((8,), None),
    "box_s": ((8,), None), "box_r": ((8,), None), "relay_s": ((2, 2, 5), None), "relay_r": ((2, 2, 5), None),
    "plane_s": ((2, 8), None), "plane_r": ((2, 8), None), "give_s": ((2, 8), None), "give_r": ((2, 8), None),
    "ag_s": ((2, 4, 5), None), "ag_r": ((2, 4, 5), None), "half_s": ((8,), None), "half_r": ((8,), None),
    "rs_s": ((2, 4, 4), None), "rs_r": ((2, 4, 4), None), "red_s": ((2, 2, 2, 4), None), "red_r": ((2, 2, 2, 4), None),
    "back_s": ((8,), None), "back_r": ((8,), None), "fin_s": ((2, 2), None), "fin_r": ((2, 2), None),
}


def on_device(
    queries, latent_rows, doc_ids, value_up, out_proj, residual_in, norm_gain, expert_ids, gate_weights, gate_proj, up_proj,
    down_proj,
):
    vmem, any_space = pl.BlockSpec(memory_space=pltpu.VMEM), pl.BlockSpec(memory_space=pl.ANY)
    return pl.pallas_call(
        layer_kernel,
        out_shape=jax.ShapeDtypeStruct((16, D), BF),
        in_specs=[vmem] * 7 + [any_space] * 5,
        out_specs=vmem,
        scratch_shapes=[
            pltpu.SemaphoreType.DMA(shape) if kind is None else pltpu.VMEM(shape, kind) for shape, kind in SCRATCH.values()
        ],
        compiler_params=pltpu.CompilerParams(collective_id=1, has_side_effects=True, vmem_limit_bytes=60 << 20),
        cost_estimate=pl.CostEstimate(flops=8_000_000_000, bytes_accessed=10_000_000, transcendentals=2_000_000),
        name="layer",
    )(
        queries[0].transpose(1, 2, 0), latent_rows[0].T, doc_ids, expert_ids[0].T, gate_weights[0].T, residual_in[0], norm_gain,
        value_up[0], out_proj[0].T, gate_proj[0, 0], up_proj[0, 0], down_proj[0, 0],
    )[None]


def solution(mesh):
    return jax.shard_map(
        on_device,
        mesh=mesh,
        in_specs=(
            P("pipe", "ctx", "exp", None),
            P("pipe", "ctx", None),
            P("pipe", "ctx"),
            P("pipe", "exp", None, None),
            P("pipe", "exp", "ctx"),
            P("pipe", ("ctx", "exp"), None),
            P("pipe", None),
            P("pipe", ("ctx", "exp"), None),
            P("pipe", ("ctx", "exp"), None),
            P("pipe", "exp", None, "ctx"),
            P("pipe", "exp", None, "ctx"),
            P("pipe", "exp", "ctx", None),
        ),
        out_specs=P("pipe", ("ctx", "exp"), None),
        check_vma=False,
    )
```

```python
import math
import types

import jax
import jax.numpy as jnp
from jax import lax
from jax.experimental import pallas as pl
from jax.experimental.pallas import tpu as pltpu
from jax.sharding import PartitionSpec as P

D = 7168
HALF = D // 2
HD = 128
ROPE = 64
LAT = 512
KV = LAT + ROPE
MESH = pl.DeviceIdType.MESH

epsilon = 1e-06
masked_score = -1e30
score_scale = 1.0 / math.sqrt(HD + ROPE)
KEY_PIECES = ((0, 144), (144, 144), (288, 144), (432, 160))


def remote(src, dst, send_sem, recv_sem, **device):
    return pltpu.make_async_remote_copy(
        src_ref=src,
        dst_ref=dst,
        send_sem=send_sem,
        recv_sem=recv_sem,
        device_id=device,
        device_id_type=MESH,
    )


def meet(peers):
    barrier = pltpu.get_barrier_semaphore()
    for device in peers:
        pl.semaphore_signal(barrier, 1, device_id=device, device_id_type=MESH)
    pl.semaphore_wait(barrier, len(peers))


def squeeze_map(rows, groups, group, dtype=jnp.bfloat16):
    row = lax.broadcasted_iota(jnp.int32, (80, 8 * rows), 0).astype(jnp.float32)
    col = lax.broadcasted_iota(jnp.int32, (80, 8 * rows), 1).astype(jnp.float32)
    source = jnp.floor((row + 0.5) * 0.1)
    want = source * rows + (row - source * 10) + group * 10
    return jnp.where(col == want, 1.0, 0.0).astype(dtype)


def spread_map(rows, groups, group, dtype=jnp.bfloat16):
    row = lax.broadcasted_iota(jnp.int32, (8 * rows, 80), 0).astype(jnp.float32)
    col = lax.broadcasted_iota(jnp.int32, (8 * rows, 80), 1).astype(jnp.float32)
    source = jnp.floor((col + 0.5) * 0.1)
    want = source * rows + (col - source * 10) + group * 10
    return jnp.where(row == want, 1.0, 0.0).astype(dtype)


RING = 2304
GROUP = 384
PIECES = RING // GROUP
PLANE = HALF - RING
WIDE = PLANE // 2
SUMS = (((0, 384), (384, 256)), ((640, 256), (896, 384)))


def reach(d, q):
    return 4 if q % 2 == d else 3


def attend(w, q_ref, lat_ref, doc_ref, vu_ref, op_ref, residual_ref, start_rest, share_tables, make_tables):
    p, c, e = lax.axis_index("pipe"), lax.axis_index("ctx"), lax.axis_index("exp")
    k = lax.rem(c, 2)
    z = lax.div(c, 2)
    kk = 1 - k
    other = 2 * z + kk
    right = 2 * lax.rem(z + 1, 8) + k
    left = 2 * lax.rem(z + 7, 8) + k
    y = lax.div(e, 4)
    x = lax.rem(e, 4)
    bf, f32 = jnp.bfloat16, jnp.float32
    my_lanes = pl.ds(pl.multiple_of(k * 128, 128), 128)
    their_lanes = pl.ds(pl.multiple_of(kk * 128, 128), 128)
    my_columns = pl.ds(pl.multiple_of(k * 448, 16), 448)

    def chain(s, q):
        piece = pl.ds(*KEY_PIECES[q])
        return remote(
            w.keys.at[s - 1, piece, my_lanes], w.keys.at[s, piece, my_lanes], w.chain_s.at[s, q], w.chain_r.at[s, q], ctx=right
        )

    def share(s):
        return remote(w.keys.at[s, :, my_lanes], w.keys.at[s, :, my_lanes], w.share_s.at[s], w.share_r.at[s], ctx=other)

    def share_in(s):
        return remote(w.keys.at[s, :, their_lanes], w.keys.at[s, :, their_lanes], w.share_s.at[s], w.share_r.at[s], ctx=other)

    for q in range(4):
        chain(1, q).start()
    share(0).start()
    own_proj = pltpu.make_async_copy(op_ref, w.proj.at[my_columns], w.load.at[8])
    own_proj.start()
    pair_proj = remote(op_ref, w.proj.at[my_columns], w.proj_s.at[0], w.proj_r.at[0], ctx=other)
    pair_proj.start()
    up_loads = [
        pltpu.make_async_copy(vu_ref.at[h], w.value_up.at[h], w.load.at[h]) for h in range(8)
    ]
    for copy in up_loads:
        copy.start()
    start_rest()

    for h in range(8):
        w.queries[h * 128 : (h + 1) * 128, :] = jnp.transpose(q_ref[h])
    w.top[...] = jnp.full((1024, 128), masked_score, f32)
    w.sums[...] = jnp.zeros((1024, 128), f32)
    w.mixed[...] = jnp.zeros((1024, LAT), f32)
    contract_last = (((1,), (1,)), ((), ()))
    query_pos = c * 128 + lax.broadcasted_iota(jnp.int32, (128, 256), 0)

    def visit(s, carry):
        @pl.when(s >= 1)
        def _():
            for q in range(4):
                chain(s, q).wait_recv()

                @pl.when(s < 4)
                def _(q=q):
                    chain(s + 1, q).start()

            share(s).start()

        share_in(s).wait_recv()
        key_doc = w.keys[s, KV:, :].astype(f32)[0:1]
        key_pos = lax.rem(z + 8 - s, 8) * 256 + lax.broadcasted_iota(jnp.int32, (128, 256), 1)
        query_doc = jnp.concatenate([w.query_doc[...]] * 2, axis=1)
        hidden = jnp.where((key_pos <= query_pos) & (query_doc == key_doc), 0.0, masked_score)
        hidden = jnp.concatenate([hidden] * 4, axis=0)

        def some(j, carry):
            at = pl.ds(pl.multiple_of(j * 512, 512), 512)
            scores = jnp.dot(w.queries[at], w.keys[s, 0:KV, :], preferred_element_type=f32) * score_scale + hidden
            before = w.top[at]
            highest = jnp.maximum(before, jnp.max(scores, axis=1, keepdims=True))
            shrink = jnp.exp(before - highest)
            weights = jnp.exp(scores - jnp.concatenate([highest, highest], axis=1))
            w.top[at] = highest
            w.sums[at] = w.sums[at] * shrink + jnp.sum(weights, axis=1, keepdims=True)
            update = lax.dot_general(weights.astype(bf), w.keys[s, 0:LAT, :], contract_last, preferred_element_type=f32)
            w.mixed[at] = w.mixed[at] * jnp.concatenate([shrink] * 4, axis=1) + update
            return carry

        lax.fori_loop(0, 2, some, 0)
        return carry

    lax.fori_loop(0, 5, visit, 0)
    share_tables()

    for copy in up_loads:
        copy.wait()

    def gather(d, q, r):
        piece = pl.ds(q * 64, 64)
        if d == 0:
            return remote(w.heads.at[r - 1, piece], w.heads.at[r, piece], w.head_s.at[d, q, r], w.head_r.at[d, q, r], ctx=right)
        return remote(
            w.heads.at[lax.rem(9 - r, 8), piece], w.heads.at[8 - r, piece], w.head_s.at[d, q, r], w.head_r.at[d, q, r], ctx=left
        )

    for h in range(8):
        at = slice(h * 128, (h + 1) * 128)
        latent_out = (w.mixed[at] / jnp.concatenate([w.sums[at]] * 4, axis=1)).astype(bf)
        w.heads[0, :, at] = jnp.dot(latent_out, w.value_up[h], preferred_element_type=f32).astype(bf)
    for q in range(2):
        for d in range(2):
            gather(d, q, 1).start()

    own_proj.wait()
    pair_proj.wait_recv()
    w.proj_all[...] = jnp.transpose(w.proj[...])

    y_mine = pl.multiple_of(y * 64, 64)
    y_theirs = pl.multiple_of((1 - y) * 64, 64)
    x_mine = pl.multiple_of(x * 16, 16)

    def fold(slot):
        return remote(w.fold_out.at[slot], w.fold_in.at[slot], w.fold_s.at[slot], w.fold_r.at[slot], exp=lax.rem(e + 4, 8))

    def cross(slot, i):
        to = lax.rem(x + i, 4)
        return remote(
            w.cross_out.at[slot, pl.ds(pl.multiple_of(to * 16, 16), 16)], w.cross_in.at[slot, i - 1],
            w.cross_s.at[slot, i - 1], w.cross_r.at[slot, i - 1], exp=4 * y + to,
        )

    def deliver(slot):
        return remote(
            w.part_out.at[slot], w.parts.at[z], w.part_s.at[slot], w.part_r.at[slot], ctx=2 * lax.rem(z + 8 - slot, 8) + k
        )

    def deliver_in(slot):
        source = lax.rem(z + slot, 8)
        return remote(w.part_out.at[slot], w.parts.at[source], w.part_s.at[slot], w.part_r.at[slot], ctx=2 * source + k)

    def project(slot):
        w.product[slot] = jnp.dot(w.heads[slot], w.proj_all[...], preferred_element_type=f32)
        w.fold_out[slot] = w.product[slot, pl.ds(y_theirs, 64), :].astype(bf)
        fold(slot).start()

    def over_y(slot):
        fold(slot).wait_recv()
        both = w.product[slot, pl.ds(y_mine, 64), :] + w.fold_in[slot].astype(f32)
        w.product[slot, pl.ds(y_mine, 64), :] = both
        w.cross_out[slot] = both.astype(bf)
        for i in range(1, 4):
            cross(slot, i).start()

    def over_x(slot):
        whole = w.product[slot, pl.ds(pl.multiple_of(y_mine + x_mine, 16), 16), :]
        for i in range(1, 4):
            cross(slot, i).wait_recv()
            whole = whole + w.cross_in[slot, i - 1].astype(f32)
        w.part_out[slot] = whole.astype(bf)

        @pl.when(slot >= 1)
        def _():
            deliver(slot).start()

    def turn(r, carry):
        @pl.when((r >= 1) & (r <= 4))
        def _():
            for q in range(2):
                for d in range(2):
                    @pl.when(r <= reach(d, q))
                    def _(d=d, q=q):
                        gather(d, q, r).wait_recv()

                    @pl.when(r + 1 <= reach(d, q))
                    def _(d=d, q=q):
                        gather(d, q, r + 1).start()

        for stage, act in enumerate((project, over_y, over_x)):
            now = r - stage

            @pl.when((now >= 0) & (now <= 4))
            def _(act=act, now=now):
                act(now)

            @pl.when((now >= 1) & (now <= 3))
            def _(act=act, now=now):
                act(8 - now)

        make_tables(r)
        return carry

    lax.fori_loop(0, 7, turn, 0)
    w.parts[pl.ds(z, 1)] = w.part_out[0:1]
    for slot in range(1, 8):
        deliver_in(slot).wait_recv()
    for other_z in range(8):
        columns = slice(other_z * 896, (other_z + 1) * 896)
        w.stream[:, columns] = (residual_ref[:, columns].astype(f32) + w.parts[other_z].astype(f32)).astype(bf)

    def settle():
        pair_proj.wait_send()

        def chained(s, carry):
            for q in range(4):
                chain(s, q).wait_send()
            return carry

        lax.fori_loop(1, 5, chained, 0)

        def shared(s, carry):
            share(s).wait_send()
            return carry

        lax.fori_loop(0, 5, shared, 0)
        for q in range(2):
            for d in range(2):
                def gathered(r, carry, d=d, q=q):
                    gather(d, q, r).wait_send()
                    return carry

                lax.fori_loop(1, reach(d, q) + 1, gathered, 0)

        def folded(slot, carry):
            fold(slot).wait_send()
            for i in range(1, 4):
                cross(slot, i).wait_send()

            @pl.when(slot >= 1)
            def _():
                deliver(slot).wait_send()
            return carry

        lax.fori_loop(0, 8, folded, 0)

    return settle


def column_of(rows):
    diagonal = lax.broadcasted_iota(jnp.int32, rows.shape, 0) == lax.broadcasted_iota(jnp.int32, rows.shape, 1)
    return jnp.sum(jnp.where(diagonal, rows, 0.0), axis=1, keepdims=True)


def tables(w, ids_ref, weights_ref, k):
    f32 = jnp.float32
    ids = [column_of(jnp.broadcast_to(ids_ref[i : i + 1, :].astype(f32), (16, 16))) for i in range(2)]
    weights = [column_of(jnp.broadcast_to(weights_ref[i : i + 1, :], (16, 16))) for i in range(2)]
    lane = lax.broadcasted_iota(jnp.int32, (16, 128), 1)
    expert = lane.astype(f32)
    first, second = (jnp.where(ids[i] == expert, 1.0, 0.0) for i in range(2))
    earlier = lax.broadcasted_iota(jnp.int32, (16, 16), 1) < lax.broadcasted_iota(jnp.int32, (16, 16), 0)
    counts = jnp.dot(jnp.where(earlier, 1.0, 0.0), first + second, preferred_element_type=f32)
    ranks = (
        jnp.sum(first * counts, axis=1, keepdims=True),
        jnp.sum(second * (counts + first), axis=1, keepdims=True),
    )
    table = jnp.zeros((16, 128), f32)
    for i in range(2):
        table = jnp.where(lane == i, ids[i] * 8.0 + ranks[i], table)
        table = jnp.where(lane == i + 2, weights[i], table)
    w.table[0, pl.ds(k, 1)] = table[None]


def decode(shape, axis, groups, height):
    row = lax.broadcasted_iota(jnp.int32, shape, axis).astype(jnp.float32)
    expert = jnp.floor((row + 0.5) * (1.0 / height))
    inner = row - expert * height
    group = jnp.floor((inner + 0.5) * 0.1)
    within = inner - group * 10.0
    block = jnp.where(within >= 5.0, 1.0, 0.0)
    slot = jnp.where(group < groups, expert * 8.0 + within - block * 5.0, -1.0)
    return slot, group * 2.0 + block


def choose_matrix(columns, sel, groups, height):
    span, count = groups * 32, 8 * height
    lanes = jnp.transpose(columns)
    slot, owner = decode((count, 1), 0, groups, height)
    token = lax.shift_right_logical(lax.broadcasted_iota(jnp.int32, (count, span), 1), 4).astype(jnp.float32)
    hit = (owner == token) & ((slot == lanes[0:1, :span]) | (slot == lanes[1:2, :span]))
    sel[...] = jnp.where(hit, 1.0, 0.0).astype(jnp.bfloat16)


def weigh_matrix(columns, mix, groups, height):
    span, count = groups * 32, 8 * height
    slot, owner = decode((1, count), 1, groups, height)
    token = lax.shift_right_logical(lax.broadcasted_iota(jnp.int32, (span, count), 0), 4).astype(jnp.float32)
    slot = jnp.where(owner == token, slot, -1.0)
    weight = jnp.zeros((span, count), jnp.float32)
    for i in range(2):
        weight = weight + jnp.where(slot == columns[:span, i : i + 1], columns[:span, i + 2 : i + 3], 0.0)
    high = weight.astype(jnp.bfloat16)
    mix[0:span, :] = high
    mix[span : 2 * span, :] = (weight - high.astype(jnp.float32)).astype(jnp.bfloat16)


def layer_kernel(
    q_ref, lat_ref, doc_ref, ids_ref, weights_ref, residual_ref, gain_ref, vu_ref, op_ref, gate_ref, up_ref, down_ref,
    out_ref, *scratch
):
    w = types.SimpleNamespace(**dict(zip(SCRATCH, scratch, strict=True)))
    p, c, e = lax.axis_index("pipe"), lax.axis_index("ctx"), lax.axis_index("exp")
    k = lax.rem(c, 2)
    z = lax.div(c, 2)
    kk = 1 - k
    other = 2 * z + kk
    right = 2 * lax.rem(z + 1, 8) + k
    left = 2 * lax.rem(z + 7, 8) + k
    over = 1 - p
    mine = pl.multiple_of(k * HALF, 128)
    theirs = pl.multiple_of(kk * HALF, 128)
    my_lane = pl.multiple_of(k * 128, 128)
    up_lane = pl.multiple_of(256 + k * 128, 128)

    bf, f32 = jnp.bfloat16, jnp.float32

    w.keys[0, 0:KV, pl.ds(my_lane, 128)] = lat_ref[...]
    doc_row = jnp.broadcast_to(doc_ref[...].astype(f32), (128, 128))
    w.keys[0, KV:, pl.ds(my_lane, 128)] = doc_row[0:16].astype(bf)
    w.query_doc[...] = jnp.broadcast_to(column_of(doc_row), (128, 128))
    tables(w, ids_ref, weights_ref, k)
    meet(
        [{"ctx": other}, {"pipe": over}, {"pipe": over, "ctx": other}]
        + [{"ctx": 2 * lax.rem(z + i, 8) + k} for i in range(1, 8)]
        + [{"exp": lax.rem(e + i, 8)} for i in range(1, 8)]
    )
    local = [
        pltpu.make_async_copy(gate_ref.at[pl.ds(mine, HALF), :], w.w_in.at[:, pl.ds(my_lane, 128)], w.loc.at[0]),
        pltpu.make_async_copy(up_ref.at[pl.ds(mine, HALF), :], w.w_in.at[:, pl.ds(up_lane, 128)], w.loc.at[1]),
        pltpu.make_async_copy(down_ref.at[:, pl.ds(mine, HALF)], w.w_down.at[pl.ds(my_lane, 128), :], w.loc.at[2]),
    ]
    pair = [
        remote(w.normed.at[:, pl.ds(theirs, HALF)], w.pn, w.pair_s.at[0], w.pair_r.at[0], ctx=other),
        remote(w.stream.at[:, pl.ds(theirs, HALF)], w.ps, w.pair_s.at[1], w.pair_r.at[1], ctx=other),
        remote(gate_ref.at[pl.ds(theirs, HALF), :], w.w_in.at[:, pl.ds(my_lane, 128)], w.pair_s.at[2], w.pair_r.at[2], ctx=other),
        remote(up_ref.at[pl.ds(theirs, HALF), :], w.w_in.at[:, pl.ds(up_lane, 128)], w.pair_s.at[3], w.pair_r.at[3], ctx=other),
        remote(down_ref.at[:, pl.ds(theirs, HALF)], w.w_down.at[pl.ds(my_lane, 128), :], w.pair_s.at[4], w.pair_r.at[4], ctx=other),
    ]
    pair.append(remote(w.table.at[0, k], w.table.at[0, k], w.pair_s.at[5], w.pair_r.at[5], ctx=other))

    def start_rest():
        pair[5].start()
        for copy in local:
            copy.start()
        for copy in pair[2:5]:
            copy.start()

    def spread_table(i):
        return remote(w.table.at[0], w.table.at[i], w.table_s.at[i], w.table_r.at[i], ctx=2 * lax.rem(z + i, 8) + k)

    def share_tables():
        pair[5].wait_recv()
        for i in range(1, 8):
            spread_table(i).start()

    def chip_table():
        return jnp.concatenate([w.table[0].reshape(32, 128)] * 4, axis=0)

    def column_table():
        return w.table[...].reshape(256, 128)

    def make_tables(r):
        @pl.when(r == 1)
        def _():
            choose_matrix(chip_table(), w.sel, 3, 32)

        @pl.when(r == 2)
        def _():
            for i in range(1, 8):
                spread_table(i).wait_recv()
            choose_matrix(column_table(), w.plane_sel, 8, 80)

    settle = attend(w, q_ref, lat_ref, doc_ref, vu_ref, op_ref, residual_ref, start_rest, share_tables, make_tables)
    wide = w.stream[...].astype(f32)
    mean_square = jnp.mean(wide * wide, axis=1, keepdims=True)
    w.normed[...] = (wide * lax.rsqrt(mean_square + epsilon) * gain_ref[...]).astype(bf)
    for copy in pair[:2]:
        copy.start()

    def place(target, plane_target, source, start, core):
        for g in range(PIECES):
            lanes = pl.ds(start + g * GROUP if isinstance(start, int) else pl.multiple_of(start + g * GROUP, 128), GROUP)
            target[g // 3, pl.ds(pl.multiple_of(g % 3 * 32 + core * 16, 16), 16), :] = source[:, lanes]
        lanes = pl.ds(start + RING if isinstance(start, int) else pl.multiple_of(start + RING, 128), PLANE)
        plane_target[pl.ds(pl.multiple_of(core * 16, 16), 16), :] = source[:, lanes]

    place(w.xg, w.tokens.at[0], w.normed, mine, k)
    place(w.sg, w.plane_stream, w.stream, mine, k)
    pair[0].wait_recv()
    place(w.xg, w.tokens.at[0], w.pn, 0, kk)

    def relay(d, q, r):
        columns = pl.ds(q * WIDE, WIDE)
        src, dst, to = (r - 1, r, right) if d == 0 else (lax.rem(9 - r, 8), 8 - r, left)
        return remote(w.tokens.at[src, :, columns], w.tokens.at[dst, :, columns], w.relay_s.at[d, q, r], w.relay_r.at[d, q, r], ctx=to)

    def relay_round(r):
        for q in range(2):
            for d in range(2):
                if r <= reach(d, q):
                    relay(d, q, r).wait_recv()
                if r + 1 <= reach(d, q):
                    relay(d, q, r + 1).start()

    for q in range(2):
        for d in range(2):
            relay(d, q, 1).start()

    def box(part, i):
        to = lax.rem(e + i, 8)
        return remote(w.outbox.at[part, to], w.inbox.at[part, e], w.box_s.at[part, i], w.box_r.at[part, i], exp=to)

    def box_in(part, i):
        source = lax.rem(e + 8 - i, 8)
        return remote(
            w.outbox.at[part, source], w.inbox.at[part, source], w.box_s.at[part, i], w.box_r.at[part, i], exp=source
        )

    for part in range(2):
        chosen = jnp.dot(w.sel[...], w.xg[part], preferred_element_type=f32).astype(bf)
        w.outbox[part] = chosen.reshape(8, 32, GROUP)
        for i in range(1, 8):
            box(part, i).start()
        w.inbox[part, pl.ds(e, 1)] = w.outbox[part, pl.ds(e, 1)]
    relay_round(1)

    def gather(d, q, r):
        columns = pl.ds(q * GROUP, GROUP)
        src, dst, to = (r - 1, r, right) if d == 0 else (lax.rem(9 - r, 8), 8 - r, left)
        return remote(w.rows.at[src, :, columns], w.rows.at[dst, :, columns], w.ag_s.at[d, q, r], w.ag_r.at[d, q, r], ctx=to)

    for part in range(2):
        for i in range(1, 8):
            box_in(part, i).wait_recv()
        landed_rows = w.inbox[part].reshape(256, GROUP)
        for g in range(3):
            q = part * 3 + g
            w.rows[0, :, q * GROUP : (q + 1) * GROUP] = jnp.dot(
                squeeze_map(32, 3, g), landed_rows, preferred_element_type=f32
            ).astype(bf)
            for d in range(2):
                gather(d, q, 1).start()
        relay_round(2 + part)
    relay_round(4)

    def plane_box(h, i):
        to = lax.rem(e + i, 8)
        return remote(w.plane_out.at[h, to], w.plane_in.at[h, e], w.plane_s.at[h, i], w.plane_r.at[h, i], exp=to)

    def plane_box_in(h, i):
        source = lax.rem(e + 8 - i, 8)
        return remote(w.plane_out.at[h, source], w.plane_in.at[h, source], w.plane_s.at[h, i], w.plane_r.at[h, i], exp=source)

    for h in range(2):
        tokens = w.tokens[:, :, h * WIDE : (h + 1) * WIDE].reshape(256, WIDE)
        chosen = jnp.dot(w.plane_sel[...], tokens, preferred_element_type=f32).astype(bf)
        w.plane_out[h] = chosen.reshape(8, 80, WIDE)
        for i in range(1, 8):
            plane_box(h, i).start()
        w.plane_in[h, pl.ds(e, 1)] = w.plane_out[h, pl.ds(e, 1)]
    pair[1].wait_recv()
    place(w.sg, w.plane_stream, w.ps, 0, kk)
    for copy in local:
        copy.wait()
    for copy in pair[2:5]:
        copy.wait_recv()

    BATCHES = ((0, 4), (5, 3), (4, 1))

    def swap(n):
        slots = pl.ds(*BATCHES[n])
        return remote(w.half.at[slots], w.half_other.at[slots], w.half_s.at[n], w.half_r.at[n], ctx=other)

    def ring_half(slot):
        w.half[slot] = w.half[slot] + jnp.dot(w.rows[slot], w.w_in[0:RING, :], preferred_element_type=f32)

    def second_half(n):
        first, count = BATCHES[n]
        swap(n).wait_recv()
        slots = slice(first, first + count)
        both = (w.half[slots] + w.half_other[slots]).reshape(count * 80, 512)
        gate = both[:, :256]
        hidden = (gate / (1.0 + jnp.exp(-gate)) * both[:, 256:]).astype(bf)
        w.hidden[first * 80 : (first + count) * 80, :] = hidden
        for part in range(2):
            columns = slice(part * 3 * GROUP, (part + 1) * 3 * GROUP)
            out = jnp.dot(hidden, w.w_down[:, columns], preferred_element_type=f32).astype(bf)
            w.total[slots, :, columns] = out.reshape(count, 80, 3 * GROUP)

    w.half[...] = jnp.zeros((8, 80, 512), f32)
    ring_half(0)
    for r in range(1, 5):
        for q in range(PIECES):
            for d in range(2):
                if r <= reach(d, q):
                    gather(d, q, r).wait_recv()
                if r + 1 <= reach(d, q):
                    gather(d, q, r + 1).start()
        ring_half(r)
        if r < 4:
            ring_half(8 - r)
        if r == 1:
            weigh_matrix(chip_table(), w.mix, 3, 32)
            for slot in range(8):
                w.turn[slot * 80 : (slot + 1) * 80, :] = squeeze_map(80, 8, slot)
        if r == 2:
            weigh_matrix(column_table(), w.plane_mix, 8, 80)
        if r == 3:
            for h in range(2):
                for i in range(1, 8):
                    plane_box_in(h, i).wait_recv()
                turned = jnp.dot(w.turn[...], w.plane_in[h].reshape(640, WIDE), preferred_element_type=f32).astype(bf)
                lanes = slice(RING + h * WIDE, RING + (h + 1) * WIDE)
                more = jnp.dot(turned, w.w_in[lanes, :], preferred_element_type=f32)
                w.half[...] = w.half[...] + more.reshape(8, 80, 512)
            swap(0).start()
            swap(1).start()
            second_half(0)
            second_half(1)
    swap(2).start()
    second_half(2)

    def scatter(d, q, j):
        far = reach(d, q) + 1 - j
        slot, to = (far, left) if d == 0 else (8 - far, right)
        columns = pl.ds(q * GROUP, GROUP)
        return remote(w.total.at[slot, :, columns], w.arrived.at[d, q, j - 1], w.rs_s.at[d, q, j - 1], w.rs_r.at[d, q, j - 1], ctx=to)

    def scatter_on(j):
        for q in range(PIECES):
            for d in range(2):
                if j + 1 <= reach(d, q):
                    far = reach(d, q) - j
                    slot = far if d == 0 else 8 - far
                    columns = slice(q * GROUP, (q + 1) * GROUP)
                    scatter(d, q, j).wait_recv()
                    w.total[slot, :, columns] = (
                        w.total[slot, :, columns].astype(f32) + w.arrived[d, q, j - 1].astype(f32)
                    ).astype(bf)
                    scatter(d, q, j + 1).start()

    for q in range(PIECES):
        for d in range(2):
            scatter(d, q, 1).start()

    def plane_give(h, i):
        to = lax.rem(e + i, 8)
        return remote(w.plane_ret.at[h, to], w.plane_back.at[h, e], w.give_s.at[h, i], w.give_r.at[h, i], exp=to)

    def plane_give_in(h, i):
        source = lax.rem(e + 8 - i, 8)
        return remote(w.plane_ret.at[h, source], w.plane_back.at[h, source], w.give_s.at[h, i], w.give_r.at[h, i], exp=source)

    hidden = jnp.dot(w.turn[...], w.hidden[...], preferred_element_type=f32).astype(bf)
    for h in range(2):
        out = jnp.dot(hidden, w.w_down[:, RING + h * WIDE : RING + (h + 1) * WIDE], preferred_element_type=f32).astype(bf)
        w.plane_ret[h] = out.reshape(8, 80, WIDE)
        for i in range(1, 8):
            plane_give(h, i).start()
        w.plane_back[h, pl.ds(e, 1)] = w.plane_ret[h, pl.ds(e, 1)]

    def reduce(h, d, q, j):
        far = reach(d, q) + 1 - j
        slot, to = (far, left) if d == 0 else (8 - far, right)
        columns = pl.ds(*SUMS[h][q])
        return remote(
            w.partial.at[slot, :, columns], w.plane_arrived.at[h, d, q, j - 1, :, pl.ds(0, SUMS[h][q][1])], w.red_s.at[h, d, q, j - 1],
            w.red_r.at[h, d, q, j - 1], ctx=to,
        )

    def reduce_start(h):
        for i in range(1, 8):
            plane_give_in(h, i).wait_recv()
        mixed = jnp.dot(w.plane_mix[...], w.plane_back[h].reshape(640, WIDE), preferred_element_type=f32)
        mixed = mixed[:256] + mixed[256:]
        w.plane_own[:, h * WIDE : (h + 1) * WIDE] = mixed[:32]
        w.partial[:, :, h * WIDE : (h + 1) * WIDE] = mixed.astype(bf).reshape(8, 32, WIDE)
        for q in range(2):
            for d in range(2):
                reduce(h, d, q, 1).start()

    def reduce_on(h, j):
        for q in range(2):
            for d in range(2):
                if j + 1 <= reach(d, q):
                    far = reach(d, q) - j
                    slot = far if d == 0 else 8 - far
                    start, width = SUMS[h][q]
                    columns = slice(start, start + width)
                    reduce(h, d, q, j).wait_recv()
                    w.partial[slot, :, columns] = (
                        w.partial[slot, :, columns].astype(f32) + w.plane_arrived[h, d, q, j - 1, :, 0:width].astype(f32)
                    ).astype(bf)
                    reduce(h, d, q, j + 1).start()

    def reduce_end(h):
        for q in range(2):
            start, width = SUMS[h][q]
            columns = slice(start, start + width)
            whole = w.plane_own[:, columns] + w.plane_stream[:, columns].astype(f32)
            for d in range(2):
                reduce(h, d, q, reach(d, q)).wait_recv()
                whole = whole + w.plane_arrived[h, d, q, reach(d, q) - 1, :, 0:width].astype(f32)
            whole = whole.astype(bf)
            for b in range(2):
                w.ready[b, :, RING + start : RING + start + width] = whole[b * 16 : (b + 1) * 16]

    def give(part, i):
        to = lax.rem(e + i, 8)
        return remote(w.ret.at[part, to], w.back.at[part, e], w.back_s.at[part, i], w.back_r.at[part, i], exp=to)

    def give_in(part, i):
        source = lax.rem(e + 8 - i, 8)
        return remote(w.ret.at[part, source], w.back.at[part, source], w.back_s.at[part, i], w.back_r.at[part, i], exp=source)

    def send_back(part):
        spread = jnp.zeros((256, GROUP), f32)
        for g in range(3):
            q = part * 3 + g
            columns = slice(q * GROUP, (q + 1) * GROUP)
            whole = w.total[0, :, columns].astype(f32)
            for d in range(2):
                scatter(d, q, reach(d, q)).wait_recv()
                whole = whole + w.arrived[d, q, reach(d, q) - 1].astype(f32)
            spread = spread + jnp.dot(spread_map(32, 3, g), whole.astype(bf), preferred_element_type=f32)
        w.ret[part] = spread.astype(bf).reshape(8, 32, GROUP)
        for i in range(1, 8):
            give(part, i).start()
        w.back[part, pl.ds(e, 1)] = w.ret[part, pl.ds(e, 1)]

    def hand(part, b, core):
        columns = pl.ds(part * 3 * GROUP, 3 * GROUP) if part < 2 else pl.ds(RING, PLANE)
        return remote(
            w.ready.at[b, :, columns], w.landed.at[core, :, columns], w.fin_s.at[part, b], w.fin_r.at[part, core],
            pipe=over, ctx=2 * z + b,
        )

    def finish_ring(part):
        for i in range(1, 8):
            give_in(part, i).wait_recv()
        mixed = jnp.dot(w.mix[...], w.back[part].reshape(256, GROUP), preferred_element_type=f32)
        layer_out = (w.sg[part].astype(f32) + (mixed[:96] + mixed[96:])).astype(bf)
        for g in range(3):
            start = (part * 3 + g) * GROUP
            for b in range(2):
                w.ready[b, :, start : start + GROUP] = layer_out[g * 32 + b * 16 : g * 32 + b * 16 + 16]
        for b in range(2):
            hand(part, b, k).start()

    scatter_on(1)
    scatter_on(2)
    reduce_start(0)
    scatter_on(3)
    reduce_on(0, 1)
    reduce_start(1)
    reduce_on(0, 2)
    reduce_on(0, 3)
    reduce_on(1, 1)
    send_back(0)
    send_back(1)
    reduce_on(1, 2)
    reduce_end(0)
    reduce_on(1, 3)
    finish_ring(0)
    reduce_end(1)
    for b in range(2):
        hand(2, b, k).start()
    finish_ring(1)
    for part in range(3):
        for b in range(2):
            hand(part, b, b).wait_recv()
    for b in range(2):
        out_ref[:, b * HALF : (b + 1) * HALF] = w.landed[b]

    for part in range(3):
        for b in range(2):
            hand(part, b, k).wait_send()
    for copy in pair:
        copy.wait_send()

    def sent(i, carry):
        spread_table(i).wait_send()
        for h in range(2):
            plane_box(h, i).wait_send()
            plane_give(h, i).wait_send()
            box(h, i).wait_send()
            give(h, i).wait_send()
        return carry

    lax.fori_loop(1, 8, sent, 0)

    def gone(r, carry):
        for q in range(PIECES):
            for d in range(2):
                @pl.when(r <= reach(d, q))
                def _(d=d, q=q):
                    gather(d, q, r).wait_send()
                    scatter(d, q, r).wait_send()
                    if q < 2:
                        relay(d, q, r).wait_send()
                        for h in range(2):
                            reduce(h, d, q, r).wait_send()
        return carry

    lax.fori_loop(1, 5, gone, 0)

    for n in range(3):
        swap(n).wait_send()
    settle()


BF, F32 = jnp.bfloat16, jnp.float32
SCRATCH = {
    "keys": ((5, KV + 16, 256), BF), "queries": ((1024, KV), BF), "query_doc": ((128, 128), F32), "top": ((1024, 128), F32),
    "sums": ((1024, 128), F32), "mixed": ((1024, LAT), F32), "value_up": ((8, LAT, 128), BF), "heads": ((8, 128, 1024), BF),
    "proj": ((896, 1024), BF), "proj_all": ((1024, 896), BF), "product": ((8, 128, 896), F32),
    "fold_out": ((8, 64, 896), BF), "fold_in": ((8, 64, 896), BF), "cross_out": ((8, 64, 896), BF),
    "cross_in": ((8, 3, 16, 896), BF), "part_out": ((8, 16, 896), BF), "parts": ((8, 16, 896), BF), "stream": ((16, D), BF),
    "table": ((8, 2, 16, 128), F32), "sel": ((256, 96), BF), "mix": ((192, 256), BF), "turn": ((640, 640), BF),
    "plane_sel": ((640, 256), BF), "plane_mix": ((512, 640), BF),
    "normed": ((16, D), BF), "pn": ((16, HALF), BF), "ps": ((16, HALF), BF), "tokens": ((8, 32, PLANE), BF),
    "xg": ((2, 96, GROUP), BF), "sg": ((2, 96, GROUP), BF), "plane_stream": ((32, PLANE), BF),
    "outbox": ((2, 8, 32, GROUP), BF), "inbox": ((2, 8, 32, GROUP), BF), "ret": ((2, 8, 32, GROUP), BF),
    "back": ((2, 8, 32, GROUP), BF), "plane_out": ((2, 8, 80, WIDE), BF), "plane_in": ((2, 8, 80, WIDE), BF),
    "plane_ret": ((2, 8, 80, WIDE), BF), "plane_back": ((2, 8, 80, WIDE), BF),
    "w_in": ((HALF, 512), BF), "w_down": ((256, HALF), BF), "rows": ((8, 80, RING), BF),
    "half": ((8, 80, 512), F32), "half_other": ((8, 80, 512), F32), "hidden": ((640, 256), BF), "total": ((8, 80, RING), BF),
    "arrived": ((2, PIECES, 4, 80, GROUP), BF), "partial": ((8, 32, PLANE), BF), "plane_own": ((32, PLANE), F32),
    "plane_arrived": ((2, 2, 2, 4, 32, 384), BF), "ready": ((2, 16, HALF), BF), "landed": ((2, 16, HALF), BF),
    "load": ((9,), None), "chain_s": ((5, 4), None), "chain_r": ((5, 4), None), "share_s": ((5,), None), "share_r": ((5,), None),
    "proj_s": ((1,), None), "proj_r": ((1,), None), "head_s": ((2, 2, 5), None), "head_r": ((2, 2, 5), None),
    "fold_s": ((8,), None), "fold_r": ((8,), None), "cross_s": ((8, 3), None), "cross_r": ((8, 3), None),
    "part_s": ((8,), None), "part_r": ((8,), None),
    "pair_s": ((6,), None), "pair_r": ((6,), None), "loc": ((3,), None), "table_s": ((8,), None), "table_r": ((8,), None),
    "box_s": ((2, 8), None), "box_r": ((2, 8), None), "relay_s": ((2, 2, 5), None), "relay_r": ((2, 2, 5), None),
    "plane_s": ((2, 8), None), "plane_r": ((2, 8), None), "give_s": ((2, 8), None), "give_r": ((2, 8), None),
    "ag_s": ((2, PIECES, 5), None), "ag_r": ((2, PIECES, 5), None), "half_s": ((3,), None), "half_r": ((3,), None),
    "rs_s": ((2, PIECES, 4), None), "rs_r": ((2, PIECES, 4), None), "red_s": ((2, 2, 2, 4), None), "red_r": ((2, 2, 2, 4), None),
    "back_s": ((2, 8), None), "back_r": ((2, 8), None), "fin_s": ((3, 2), None), "fin_r": ((3, 2), None),
}


def on_device(
    queries, latent_rows, doc_ids, value_up, out_proj, residual_in, norm_gain, expert_ids, gate_weights, gate_proj, up_proj,
    down_proj,
):
    vmem, any_space = pl.BlockSpec(memory_space=pltpu.VMEM), pl.BlockSpec(memory_space=pl.ANY)
    return pl.pallas_call(
        layer_kernel,
        out_shape=jax.ShapeDtypeStruct((16, D), BF),
        in_specs=[vmem] * 7 + [any_space] * 5,
        out_specs=vmem,
        scratch_shapes=[
            pltpu.SemaphoreType.DMA(shape) if kind is None else pltpu.VMEM(shape, kind) for shape, kind in SCRATCH.values()
        ],
        compiler_params=pltpu.CompilerParams(collective_id=1, has_side_effects=True, vmem_limit_bytes=60 << 20),
        cost_estimate=pl.CostEstimate(flops=8_000_000_000, bytes_accessed=10_000_000, transcendentals=2_000_000),
        name="layer",
    )(
        queries[0].transpose(1, 2, 0), latent_rows[0].T, doc_ids, expert_ids[0].T, gate_weights[0].T, residual_in[0], norm_gain,
        value_up[0], out_proj[0].T, gate_proj[0, 0], up_proj[0, 0], down_proj[0, 0],
    )[None]


def solution(mesh):
    return jax.shard_map(
        on_device,
        mesh=mesh,
        in_specs=(
            P("pipe", "ctx", "exp", None),
            P("pipe", "ctx", None),
            P("pipe", "ctx"),
            P("pipe", "exp", None, None),
            P("pipe", "exp", "ctx"),
            P("pipe", ("ctx", "exp"), None),
            P("pipe", None),
            P("pipe", ("ctx", "exp"), None),
            P("pipe", ("ctx", "exp"), None),
            P("pipe", "exp", None, "ctx"),
            P("pipe", "exp", None, "ctx"),
            P("pipe", "exp", "ctx", None),
        ),
        out_specs=P("pipe", ("ctx", "exp"), None),
        check_vma=False,
    )
```

```python
import math
import types

import jax
import jax.numpy as jnp
from jax import lax
from jax.experimental import pallas as pl
from jax.experimental.pallas import tpu as pltpu
from jax.sharding import PartitionSpec as P

D = 7168
HALF = D // 2
HD = 128
ROPE = 64
LAT = 512
KV = LAT + ROPE
MESH = pl.DeviceIdType.MESH

epsilon = 1e-06
masked_score = -1e30
score_scale = 1.0 / math.sqrt(HD + ROPE)
KEY_PIECES = ((0, 144), (144, 144), (288, 144), (432, 160))


def remote(src, dst, send_sem, recv_sem, **device):
    return pltpu.make_async_remote_copy(
        src_ref=src,
        dst_ref=dst,
        send_sem=send_sem,
        recv_sem=recv_sem,
        device_id=device,
        device_id_type=MESH,
    )


def meet(peers):
    barrier = pltpu.get_barrier_semaphore()
    for device in peers:
        pl.semaphore_signal(barrier, 1, device_id=device, device_id_type=MESH)
    pl.semaphore_wait(barrier, len(peers))


def squeeze_map(rows, groups, group, dtype=jnp.bfloat16):
    row = lax.broadcasted_iota(jnp.int32, (80, 8 * rows), 0).astype(jnp.float32)
    col = lax.broadcasted_iota(jnp.int32, (80, 8 * rows), 1).astype(jnp.float32)
    source = jnp.floor((row + 0.5) * 0.1)
    want = source * rows + (row - source * 10) + group * 10
    return jnp.where(col == want, 1.0, 0.0).astype(dtype)


def spread_map(rows, groups, group, dtype=jnp.bfloat16):
    row = lax.broadcasted_iota(jnp.int32, (8 * rows, 80), 0).astype(jnp.float32)
    col = lax.broadcasted_iota(jnp.int32, (8 * rows, 80), 1).astype(jnp.float32)
    source = jnp.floor((col + 0.5) * 0.1)
    want = source * rows + (col - source * 10) + group * 10
    return jnp.where(row == want, 1.0, 0.0).astype(dtype)


RING = 2304
GROUP = 384
PIECES = RING // GROUP
PLANE = HALF - RING
SHARES = ((0, 896), (896, 384))
HANDS = ((0, 3 * GROUP), (3 * GROUP, 3 * GROUP), (RING, 896), (RING + 896, 384))
SUMS = ((0, 512), (512, 384))


def reach(d, q):
    return 4 if q % 2 == d else 3


def attend(w, q_ref, lat_ref, doc_ref, vu_ref, op_ref, residual_ref, start_rest, make_tables):
    p, c, e = lax.axis_index("pipe"), lax.axis_index("ctx"), lax.axis_index("exp")
    k = lax.rem(c, 2)
    z = lax.div(c, 2)
    kk = 1 - k
    other = 2 * z + kk
    right = 2 * lax.rem(z + 1, 8) + k
    left = 2 * lax.rem(z + 7, 8) + k
    y = lax.div(e, 4)
    x = lax.rem(e, 4)
    bf, f32 = jnp.bfloat16, jnp.float32
    my_lanes = pl.ds(pl.multiple_of(k * 128, 128), 128)
    their_lanes = pl.ds(pl.multiple_of(kk * 128, 128), 128)
    my_columns = pl.ds(pl.multiple_of(k * 448, 16), 448)

    def chain(s, q):
        piece = pl.ds(*KEY_PIECES[q])
        return remote(
            w.keys.at[s - 1, piece, my_lanes], w.keys.at[s, piece, my_lanes], w.chain_s.at[s, q], w.chain_r.at[s, q], ctx=right
        )

    def share(s):
        return remote(w.keys.at[s, :, my_lanes], w.keys.at[s, :, my_lanes], w.share_s.at[s], w.share_r.at[s], ctx=other)

    def share_in(s):
        return remote(w.keys.at[s, :, their_lanes], w.keys.at[s, :, their_lanes], w.share_s.at[s], w.share_r.at[s], ctx=other)

    for q in range(4):
        chain(1, q).start()
    share(0).start()
    own_proj = pltpu.make_async_copy(op_ref, w.proj.at[my_columns], w.load.at[8])
    own_proj.start()
    pair_proj = remote(op_ref, w.proj.at[my_columns], w.proj_s.at[0], w.proj_r.at[0], ctx=other)
    pair_proj.start()
    up_loads = [
        pltpu.make_async_copy(vu_ref.at[h], w.value_up.at[h], w.load.at[h]) for h in range(8)
    ]
    for copy in up_loads:
        copy.start()
    start_rest()

    for h in range(8):
        w.queries[h * 128 : (h + 1) * 128, :] = jnp.transpose(q_ref[h])
    w.top[...] = jnp.full((1024, 128), masked_score, f32)
    w.sums[...] = jnp.zeros((1024, 128), f32)
    w.mixed[...] = jnp.zeros((1024, LAT), f32)
    contract_last = (((1,), (1,)), ((), ()))
    query_pos = c * 128 + lax.broadcasted_iota(jnp.int32, (128, 256), 0)

    def visit(s, carry):
        @pl.when(s >= 1)
        def _():
            for q in range(4):
                chain(s, q).wait_recv()

                @pl.when(s < 4)
                def _(q=q):
                    chain(s + 1, q).start()

            share(s).start()

        share_in(s).wait_recv()
        key_doc = w.keys[s, KV:, :].astype(f32)[0:1]
        key_pos = lax.rem(z + 8 - s, 8) * 256 + lax.broadcasted_iota(jnp.int32, (128, 256), 1)
        query_doc = jnp.concatenate([w.query_doc[...]] * 2, axis=1)
        hidden = jnp.where((key_pos <= query_pos) & (query_doc == key_doc), 0.0, masked_score)
        hidden = jnp.concatenate([hidden] * 4, axis=0)

        def some(j, carry):
            at = pl.ds(pl.multiple_of(j * 512, 512), 512)
            scores = jnp.dot(w.queries[at], w.keys[s, 0:KV, :], preferred_element_type=f32) * score_scale + hidden
            before = w.top[at]
            highest = jnp.maximum(before, jnp.max(scores, axis=1, keepdims=True))
            shrink = jnp.exp(before - highest)
            weights = jnp.exp(scores - jnp.concatenate([highest, highest], axis=1))
            w.top[at] = highest
            w.sums[at] = w.sums[at] * shrink + jnp.sum(weights, axis=1, keepdims=True)
            update = lax.dot_general(weights.astype(bf), w.keys[s, 0:LAT, :], contract_last, preferred_element_type=f32)
            w.mixed[at] = w.mixed[at] * jnp.concatenate([shrink] * 4, axis=1) + update
            return carry

        lax.fori_loop(0, 2, some, 0)
        return carry

    lax.fori_loop(0, 5, visit, 0)

    for copy in up_loads:
        copy.wait()

    def gather(d, q, r):
        piece = pl.ds(q * 64, 64)
        if d == 0:
            return remote(w.heads.at[r - 1, piece], w.heads.at[r, piece], w.head_s.at[d, q, r], w.head_r.at[d, q, r], ctx=right)
        return remote(
            w.heads.at[lax.rem(9 - r, 8), piece], w.heads.at[8 - r, piece], w.head_s.at[d, q, r], w.head_r.at[d, q, r], ctx=left
        )

    for h in range(8):
        at = slice(h * 128, (h + 1) * 128)
        latent_out = (w.mixed[at] / jnp.concatenate([w.sums[at]] * 4, axis=1)).astype(bf)
        w.heads[0, :, at] = jnp.dot(latent_out, w.value_up[h], preferred_element_type=f32).astype(bf)
    for q in range(2):
        for d in range(2):
            gather(d, q, 1).start()

    own_proj.wait()
    pair_proj.wait_recv()
    w.proj_all[...] = jnp.transpose(w.proj[...])

    y_mine = pl.multiple_of(y * 64, 64)
    y_theirs = pl.multiple_of((1 - y) * 64, 64)
    x_mine = pl.multiple_of(x * 16, 16)

    def fold(slot):
        return remote(w.fold_out.at[slot], w.fold_in.at[slot], w.fold_s.at[slot], w.fold_r.at[slot], exp=lax.rem(e + 4, 8))

    def cross(slot, i):
        to = lax.rem(x + i, 4)
        return remote(
            w.cross_out.at[slot, pl.ds(pl.multiple_of(to * 16, 16), 16)], w.cross_in.at[slot, i - 1],
            w.cross_s.at[slot, i - 1], w.cross_r.at[slot, i - 1], exp=4 * y + to,
        )

    def deliver(slot):
        return remote(
            w.part_out.at[slot], w.parts.at[z], w.part_s.at[slot], w.part_r.at[slot], ctx=2 * lax.rem(z + 8 - slot, 8) + k
        )

    def deliver_in(slot):
        source = lax.rem(z + slot, 8)
        return remote(w.part_out.at[slot], w.parts.at[source], w.part_s.at[slot], w.part_r.at[slot], ctx=2 * source + k)

    def project(slot):
        w.product[slot] = jnp.dot(w.heads[slot], w.proj_all[...], preferred_element_type=f32)
        w.fold_out[slot] = w.product[slot, pl.ds(y_theirs, 64), :].astype(bf)
        fold(slot).start()

    def direct(i):
        to = lax.rem(e + i, 8)
        return remote(
            w.direct_out.at[pl.ds(pl.multiple_of(to * 16, 16), 16)], w.direct_in.at[i - 1], w.direct_s.at[i], w.direct_r.at[i], exp=to
        )

    def project_last():
        w.product[4] = jnp.dot(w.heads[4], w.proj_all[...], preferred_element_type=f32)
        w.direct_out[...] = w.product[4].astype(bf)
        for i in range(1, 8):
            direct(i).start()

    def sum_last():
        whole = w.product[4, pl.ds(pl.multiple_of(e * 16, 16), 16), :]
        for i in range(1, 8):
            direct(i).wait_recv()
            whole = whole + w.direct_in[i - 1].astype(f32)
        w.part_out[4] = whole.astype(bf)
        deliver(4).start()

    def over_y(slot):
        fold(slot).wait_recv()
        both = w.product[slot, pl.ds(y_mine, 64), :] + w.fold_in[slot].astype(f32)
        w.product[slot, pl.ds(y_mine, 64), :] = both
        w.cross_out[slot] = both.astype(bf)
        for i in range(1, 4):
            cross(slot, i).start()

    def over_x(slot):
        whole = w.product[slot, pl.ds(pl.multiple_of(y_mine + x_mine, 16), 16), :]
        for i in range(1, 4):
            cross(slot, i).wait_recv()
            whole = whole + w.cross_in[slot, i - 1].astype(f32)
        w.part_out[slot] = whole.astype(bf)

        @pl.when(slot >= 1)
        def _():
            deliver(slot).start()

    def turn(r, carry):
        @pl.when((r >= 1) & (r <= 4))
        def _():
            for q in range(2):
                for d in range(2):
                    @pl.when(r <= reach(d, q))
                    def _(d=d, q=q):
                        gather(d, q, r).wait_recv()

                    @pl.when(r + 1 <= reach(d, q))
                    def _(d=d, q=q):
                        gather(d, q, r + 1).start()

        @pl.when(r == 4)
        def _():
            project_last()

        for stage, act in enumerate((project, over_y, over_x)):
            now = r - stage

            @pl.when((now >= 0) & (now <= 3))
            def _(act=act, now=now):
                act(now)

            @pl.when((now >= 1) & (now <= 3))
            def _(act=act, now=now):
                act(8 - now)

        @pl.when(r == 5)
        def _():
            sum_last()

        make_tables(r)
        return carry

    lax.fori_loop(0, 7, turn, 0)
    w.parts[pl.ds(z, 1)] = w.part_out[0:1]
    for slot in range(1, 8):
        deliver_in(slot).wait_recv()
    for other_z in range(8):
        columns = slice(other_z * 896, (other_z + 1) * 896)
        w.stream[:, columns] = (residual_ref[:, columns].astype(f32) + w.parts[other_z].astype(f32)).astype(bf)

    def settle():
        pair_proj.wait_send()

        def chained(s, carry):
            for q in range(4):
                chain(s, q).wait_send()
            return carry

        lax.fori_loop(1, 5, chained, 0)

        def shared(s, carry):
            share(s).wait_send()
            return carry

        lax.fori_loop(0, 5, shared, 0)
        for q in range(2):
            for d in range(2):
                def gathered(r, carry, d=d, q=q):
                    gather(d, q, r).wait_send()
                    return carry

                lax.fori_loop(1, reach(d, q) + 1, gathered, 0)

        for i in range(1, 8):
            direct(i).wait_send()

        def folded(slot, carry):
            @pl.when(slot != 4)
            def _():
                fold(slot).wait_send()
                for i in range(1, 4):
                    cross(slot, i).wait_send()

            @pl.when(slot >= 1)
            def _():
                deliver(slot).wait_send()
            return carry

        lax.fori_loop(0, 8, folded, 0)

    return settle


def column_of(rows):
    diagonal = lax.broadcasted_iota(jnp.int32, rows.shape, 0) == lax.broadcasted_iota(jnp.int32, rows.shape, 1)
    return jnp.sum(jnp.where(diagonal, rows, 0.0), axis=1, keepdims=True)


def tables(w, ids_ref, weights_ref, k):
    f32 = jnp.float32
    ids = [column_of(jnp.broadcast_to(ids_ref[i : i + 1, :].astype(f32), (16, 16))) for i in range(2)]
    weights = [column_of(jnp.broadcast_to(weights_ref[i : i + 1, :], (16, 16))) for i in range(2)]
    lane = lax.broadcasted_iota(jnp.int32, (16, 128), 1)
    expert = lane.astype(f32)
    first, second = (jnp.where(ids[i] == expert, 1.0, 0.0) for i in range(2))
    earlier = lax.broadcasted_iota(jnp.int32, (16, 16), 1) < lax.broadcasted_iota(jnp.int32, (16, 16), 0)
    counts = jnp.dot(jnp.where(earlier, 1.0, 0.0), first + second, preferred_element_type=f32)
    ranks = (
        jnp.sum(first * counts, axis=1, keepdims=True),
        jnp.sum(second * (counts + first), axis=1, keepdims=True),
    )
    table = jnp.zeros((16, 128), f32)
    for i in range(2):
        table = jnp.where(lane == i, ids[i] * 8.0 + ranks[i], table)
        table = jnp.where(lane == i + 2, weights[i], table)
    w.table[pl.ds(k, 1)] = table[None]


def decode(shape, axis, groups, height):
    row = lax.broadcasted_iota(jnp.int32, shape, axis).astype(jnp.float32)
    expert = jnp.floor((row + 0.5) * (1.0 / height))
    inner = row - expert * height
    group = jnp.floor((inner + 0.5) * 0.1)
    within = inner - group * 10.0
    block = jnp.where(within >= 5.0, 1.0, 0.0)
    slot = jnp.where(group < groups, expert * 8.0 + within - block * 5.0, -1.0)
    return slot, group * 2.0 + block


def choose_matrix(columns, sel, groups, height):
    span, count = groups * 32, 8 * height
    lanes = jnp.transpose(columns)
    slot, owner = decode((count, 1), 0, groups, height)
    token = lax.shift_right_logical(lax.broadcasted_iota(jnp.int32, (count, span), 1), 4).astype(jnp.float32)
    hit = (owner == token) & ((slot == lanes[0:1, :span]) | (slot == lanes[1:2, :span]))
    sel[...] = jnp.where(hit, 1.0, 0.0).astype(jnp.bfloat16)


def weigh_matrix(columns, mix, groups, height):
    span, count = groups * 32, 8 * height
    slot, owner = decode((1, count), 1, groups, height)
    token = lax.shift_right_logical(lax.broadcasted_iota(jnp.int32, (span, count), 0), 4).astype(jnp.float32)
    slot = jnp.where(owner == token, slot, -1.0)
    weight = jnp.zeros((span, count), jnp.float32)
    for i in range(2):
        weight = weight + jnp.where(slot == columns[:span, i : i + 1], columns[:span, i + 2 : i + 3], 0.0)
    high = weight.astype(jnp.bfloat16)
    mix[0:span, :] = high
    mix[span : 2 * span, :] = (weight - high.astype(jnp.float32)).astype(jnp.bfloat16)


def layer_kernel(
    q_ref, lat_ref, doc_ref, ids_ref, weights_ref, residual_ref, gain_ref, vu_ref, op_ref, gate_ref, up_ref, down_ref,
    out_ref, *scratch
):
    w = types.SimpleNamespace(**dict(zip(SCRATCH, scratch, strict=True)))
    p, c, e = lax.axis_index("pipe"), lax.axis_index("ctx"), lax.axis_index("exp")
    k = lax.rem(c, 2)
    z = lax.div(c, 2)
    kk = 1 - k
    other = 2 * z + kk
    right = 2 * lax.rem(z + 1, 8) + k
    left = 2 * lax.rem(z + 7, 8) + k
    over = 1 - p
    mine = pl.multiple_of(k * HALF, 128)
    theirs = pl.multiple_of(kk * HALF, 128)
    my_lane = pl.multiple_of(k * 128, 128)
    up_lane = pl.multiple_of(256 + k * 128, 128)

    bf, f32 = jnp.bfloat16, jnp.float32

    w.keys[0, 0:KV, pl.ds(my_lane, 128)] = lat_ref[...]
    doc_row = jnp.broadcast_to(doc_ref[...].astype(f32), (128, 128))
    w.keys[0, KV:, pl.ds(my_lane, 128)] = doc_row[0:16].astype(bf)
    w.query_doc[...] = jnp.broadcast_to(column_of(doc_row), (128, 128))
    meet(
        [{"ctx": other}, {"pipe": over}, {"pipe": over, "ctx": other}]
        + [{"ctx": 2 * lax.rem(z + i, 8) + k} for i in range(1, 8)]
        + [{"exp": lax.rem(e + i, 8)} for i in range(1, 8)]
    )
    local = [
        pltpu.make_async_copy(gate_ref.at[pl.ds(mine, HALF), :], w.w_in.at[:, pl.ds(my_lane, 128)], w.loc.at[0]),
        pltpu.make_async_copy(up_ref.at[pl.ds(mine, HALF), :], w.w_in.at[:, pl.ds(up_lane, 128)], w.loc.at[1]),
        pltpu.make_async_copy(down_ref.at[:, pl.ds(mine, HALF)], w.w_down.at[pl.ds(my_lane, 128), :], w.loc.at[2]),
    ]
    pair = [
        remote(w.normed.at[:, pl.ds(theirs, HALF)], w.pn, w.pair_s.at[0], w.pair_r.at[0], ctx=other),
        remote(w.stream.at[:, pl.ds(theirs, HALF)], w.ps, w.pair_s.at[1], w.pair_r.at[1], ctx=other),
        remote(gate_ref.at[pl.ds(theirs, HALF), :], w.w_in.at[:, pl.ds(my_lane, 128)], w.pair_s.at[2], w.pair_r.at[2], ctx=other),
        remote(up_ref.at[pl.ds(theirs, HALF), :], w.w_in.at[:, pl.ds(up_lane, 128)], w.pair_s.at[3], w.pair_r.at[3], ctx=other),
        remote(down_ref.at[:, pl.ds(theirs, HALF)], w.w_down.at[pl.ds(my_lane, 128), :], w.pair_s.at[4], w.pair_r.at[4], ctx=other),
    ]
    pair.append(remote(w.table.at[k], w.table.at[k], w.pair_s.at[5], w.pair_r.at[5], ctx=other))

    def start_rest():
        tables(w, ids_ref, weights_ref, k)
        pair[5].start()
        for copy in local:
            copy.start()
        for copy in pair[2:5]:
            copy.start()

    def spread_table(i):
        return remote(w.brief.at[0], w.brief.at[i], w.table_s.at[i], w.table_r.at[i], ctx=2 * lax.rem(z + i, 8) + k)

    def chip_table():
        return jnp.concatenate([w.table[...].reshape(32, 128)] * 4, axis=0)

    def make_tables(r):
        @pl.when(r == 3)
        def _():
            pair[5].wait_recv()
            w.brief[0] = jnp.transpose(chip_table())[0:8]
            for i in range(1, 8):
                spread_table(i).start()

        @pl.when(r == 4)
        def _():
            choose_matrix(chip_table(), w.sel, 3, 32)

        @pl.when(r == 6)
        def _():
            for i in range(1, 8):
                spread_table(i).wait_recv()
            for i in range(8):
                w.column[i * 32 : (i + 1) * 32, :] = jnp.transpose(jnp.concatenate([w.brief[i]] * 16, axis=0))[0:32]
            choose_matrix(w.column[...], w.plane_sel, 8, 80)

    settle = attend(w, q_ref, lat_ref, doc_ref, vu_ref, op_ref, residual_ref, start_rest, make_tables)
    wide = w.stream[...].astype(f32)
    mean_square = jnp.mean(wide * wide, axis=1, keepdims=True)
    w.normed[...] = (wide * lax.rsqrt(mean_square + epsilon) * gain_ref[...]).astype(bf)
    for copy in pair[:2]:
        copy.start()

    def place(target, plane_target, source, start, core):
        for g in range(PIECES):
            lanes = pl.ds(start + g * GROUP if isinstance(start, int) else pl.multiple_of(start + g * GROUP, 128), GROUP)
            target[g // 3, pl.ds(pl.multiple_of(g % 3 * 32 + core * 16, 16), 16), :] = source[:, lanes]
        lanes = pl.ds(start + RING if isinstance(start, int) else pl.multiple_of(start + RING, 128), PLANE)
        plane_target[pl.ds(pl.multiple_of(core * 16, 16), 16), :] = source[:, lanes]

    place(w.xg, w.tokens.at[0], w.normed, mine, k)
    place(w.sg, w.plane_stream, w.stream, mine, k)
    pair[0].wait_recv()
    place(w.xg, w.tokens.at[0], w.pn, 0, kk)

    def relay(d, q, r):
        columns = pl.ds(q * (PLANE // 2), PLANE // 2)
        src, dst, to = (r - 1, r, right) if d == 0 else (lax.rem(9 - r, 8), 8 - r, left)
        return remote(w.tokens.at[src, :, columns], w.tokens.at[dst, :, columns], w.relay_s.at[d, q, r], w.relay_r.at[d, q, r], ctx=to)

    def relay_round(r):
        for q in range(2):
            for d in range(2):
                if r <= reach(d, q):
                    relay(d, q, r).wait_recv()
                if r + 1 <= reach(d, q):
                    relay(d, q, r + 1).start()

    for q in range(2):
        for d in range(2):
            relay(d, q, 1).start()

    def box(part, i):
        to = lax.rem(e + i, 8)
        return remote(w.outbox.at[part, to], w.inbox.at[part, e], w.box_s.at[part, i], w.box_r.at[part, i], exp=to)

    def box_in(part, i):
        source = lax.rem(e + 8 - i, 8)
        return remote(
            w.outbox.at[part, source], w.inbox.at[part, source], w.box_s.at[part, i], w.box_r.at[part, i], exp=source
        )

    for part in range(2):
        chosen = jnp.dot(w.sel[...], w.xg[part], preferred_element_type=f32).astype(bf)
        w.outbox[part] = chosen.reshape(8, 32, GROUP)
        for i in range(1, 8):
            box(part, i).start()
        w.inbox[part, pl.ds(e, 1)] = w.outbox[part, pl.ds(e, 1)]
    relay_round(1)

    def gather(d, q, r):
        columns = pl.ds(q * GROUP, GROUP)
        src, dst, to = (r - 1, r, right) if d == 0 else (lax.rem(9 - r, 8), 8 - r, left)
        return remote(w.rows.at[src, :, columns], w.rows.at[dst, :, columns], w.ag_s.at[d, q, r], w.ag_r.at[d, q, r], ctx=to)

    for part in range(2):
        for i in range(1, 8):
            box_in(part, i).wait_recv()
        landed_rows = w.inbox[part].reshape(256, GROUP)
        for g in range(3):
            q = part * 3 + g
            w.rows[0, :, q * GROUP : (q + 1) * GROUP] = jnp.dot(
                squeeze_map(32, 3, g), landed_rows, preferred_element_type=f32
            ).astype(bf)
            for d in range(2):
                gather(d, q, 1).start()
        relay_round(2 + part)
    relay_round(4)

    plane_out, plane_in = (w.plane_out0, w.plane_out1), (w.plane_in0, w.plane_in1)
    plane_ret, plane_back = (w.plane_ret0, w.plane_ret1), (w.plane_back0, w.plane_back1)

    def plane_box(h, i):
        to = lax.rem(e + i, 8)
        return remote(plane_out[h].at[to], plane_in[h].at[e], w.plane_s.at[h, i], w.plane_r.at[h, i], exp=to)

    def plane_box_in(h, i):
        source = lax.rem(e + 8 - i, 8)
        return remote(plane_out[h].at[source], plane_in[h].at[source], w.plane_s.at[h, i], w.plane_r.at[h, i], exp=source)

    for h, (start, width) in enumerate(SHARES):
        tokens = w.tokens[:, :, start : start + width].reshape(256, width)
        chosen = jnp.dot(w.plane_sel[...], tokens, preferred_element_type=f32).astype(bf)
        plane_out[h][...] = chosen.reshape(8, 80, width)
        for i in range(1, 8):
            plane_box(h, i).start()
        plane_in[h][pl.ds(e, 1)] = plane_out[h][pl.ds(e, 1)]
    pair[1].wait_recv()
    place(w.sg, w.plane_stream, w.ps, 0, kk)
    for copy in local:
        copy.wait()
    for copy in pair[2:5]:
        copy.wait_recv()

    BATCHES = ((0, 4), (5, 3), (4, 1))

    def swap(n):
        slots = pl.ds(*BATCHES[n])
        return remote(w.half.at[slots], w.half_other.at[slots], w.half_s.at[n], w.half_r.at[n], ctx=other)

    def ring_half(slot):
        w.half[slot] = w.half[slot] + jnp.dot(w.rows[slot], w.w_in[0:RING, :], preferred_element_type=f32)

    def second_half(n):
        first, count = BATCHES[n]
        swap(n).wait_recv()
        slots = slice(first, first + count)
        both = (w.half[slots] + w.half_other[slots]).reshape(count * 80, 512)
        gate = both[:, :256]
        hidden = (gate / (1.0 + jnp.exp(-gate)) * both[:, 256:]).astype(bf)
        w.hidden[first * 80 : (first + count) * 80, :] = hidden
        for part in range(2):
            columns = slice(part * 3 * GROUP, (part + 1) * 3 * GROUP)
            out = jnp.dot(hidden, w.w_down[:, columns], preferred_element_type=f32).astype(bf)
            w.total[slots, :, columns] = out.reshape(count, 80, 3 * GROUP)

    w.half[...] = jnp.zeros((8, 80, 512), f32)
    ring_half(0)
    for r in range(1, 5):
        for q in range(PIECES):
            for d in range(2):
                if r <= reach(d, q):
                    gather(d, q, r).wait_recv()
                if r + 1 <= reach(d, q):
                    gather(d, q, r + 1).start()
        ring_half(r)
        if r < 4:
            ring_half(8 - r)
        if r == 1:
            weigh_matrix(chip_table(), w.mix, 3, 32)
            for slot in range(8):
                w.turn[slot * 80 : (slot + 1) * 80, :] = squeeze_map(80, 8, slot)
        if r == 2:
            weigh_matrix(w.column[...], w.plane_mix, 8, 80)
        if r == 3:
            for h, (start, width) in enumerate(SHARES):
                for i in range(1, 8):
                    plane_box_in(h, i).wait_recv()
                turned = jnp.dot(w.turn[...], plane_in[h][...].reshape(640, width), preferred_element_type=f32).astype(bf)
                lanes = slice(RING + start, RING + start + width)
                more = jnp.dot(turned, w.w_in[lanes, :], preferred_element_type=f32)
                w.half[...] = w.half[...] + more.reshape(8, 80, 512)
            swap(0).start()
            swap(1).start()
            second_half(0)
            second_half(1)
    swap(2).start()
    second_half(2)

    def scatter(d, q, j):
        far = reach(d, q) + 1 - j
        slot, to = (far, left) if d == 0 else (8 - far, right)
        columns = pl.ds(q * GROUP, GROUP)
        return remote(w.total.at[slot, :, columns], w.arrived.at[d, q, j - 1], w.rs_s.at[d, q, j - 1], w.rs_r.at[d, q, j - 1], ctx=to)

    def scatter_on(j):
        for q in range(PIECES):
            for d in range(2):
                if j + 1 <= reach(d, q):
                    far = reach(d, q) - j
                    slot = far if d == 0 else 8 - far
                    columns = slice(q * GROUP, (q + 1) * GROUP)
                    scatter(d, q, j).wait_recv()
                    w.total[slot, :, columns] = (
                        w.total[slot, :, columns].astype(f32) + w.arrived[d, q, j - 1].astype(f32)
                    ).astype(bf)
                    scatter(d, q, j + 1).start()

    for q in range(PIECES):
        for d in range(2):
            scatter(d, q, 1).start()

    def plane_give(h, i):
        to = lax.rem(e + i, 8)
        return remote(plane_ret[h].at[to], plane_back[h].at[e], w.give_s.at[h, i], w.give_r.at[h, i], exp=to)

    def plane_give_in(h, i):
        source = lax.rem(e + 8 - i, 8)
        return remote(plane_ret[h].at[source], plane_back[h].at[source], w.give_s.at[h, i], w.give_r.at[h, i], exp=source)

    hidden = jnp.dot(w.turn[...], w.hidden[...], preferred_element_type=f32).astype(bf)
    for h, (start, width) in enumerate(SHARES):
        out = jnp.dot(hidden, w.w_down[:, RING + start : RING + start + width], preferred_element_type=f32).astype(bf)
        plane_ret[h][...] = out.reshape(8, 80, width)
        for i in range(1, 8):
            plane_give(h, i).start()
        plane_back[h][pl.ds(e, 1)] = plane_ret[h][pl.ds(e, 1)]

    def reduce(d, q, j):
        far = reach(d, q) + 1 - j
        slot, to = (far, left) if d == 0 else (8 - far, right)
        start, width = SUMS[q]
        return remote(
            w.partial.at[slot, :, pl.ds(start, width)], w.plane_arrived.at[d, q, j - 1, :, pl.ds(0, width)],
            w.red_s.at[d, q, j - 1], w.red_r.at[d, q, j - 1], ctx=to,
        )

    def straight(slot):
        start, width = SHARES[1]
        return remote(
            w.partial.at[slot, :, pl.ds(start, width)], w.straight_in.at[slot], w.straight_s.at[slot], w.straight_r.at[slot],
            ctx=2 * lax.rem(z + 8 - slot, 8) + k,
        )

    def reduce_start(h):
        start, width = SHARES[h]
        for i in range(1, 8):
            plane_give_in(h, i).wait_recv()
        mixed = jnp.dot(w.plane_mix[...], plane_back[h][...].reshape(640, width), preferred_element_type=f32)
        mixed = mixed[:256] + mixed[256:]
        w.plane_own[:, start : start + width] = mixed[:32]
        w.partial[:, :, start : start + width] = mixed.astype(bf).reshape(8, 32, width)
        if h == 0:
            for q in range(2):
                for d in range(2):
                    reduce(d, q, 1).start()
        else:
            for slot in (4, 3, 5, 2, 6, 1, 7):
                straight(slot).start()

    def reduce_on(j):
        for q, (start, width) in enumerate(SUMS):
            for d in range(2):
                if j + 1 <= reach(d, q):
                    far = reach(d, q) - j
                    slot = far if d == 0 else 8 - far
                    columns = slice(start, start + width)
                    reduce(d, q, j).wait_recv()
                    w.partial[slot, :, columns] = (
                        w.partial[slot, :, columns].astype(f32) + w.plane_arrived[d, q, j - 1, :, 0:width].astype(f32)
                    ).astype(bf)
                    reduce(d, q, j + 1).start()

    def keep(whole, start, width):
        whole = whole.astype(bf)
        for b in range(2):
            w.ready[b, :, RING + start : RING + start + width] = whole[b * 16 : (b + 1) * 16]

    def reduce_end():
        for q, (start, width) in enumerate(SUMS):
            columns = slice(start, start + width)
            whole = w.plane_own[:, columns] + w.plane_stream[:, columns].astype(f32)
            for d in range(2):
                reduce(d, q, reach(d, q)).wait_recv()
                whole = whole + w.plane_arrived[d, q, reach(d, q) - 1, :, 0:width].astype(f32)
            keep(whole, start, width)
        for b in range(2):
            hand(2, b, k).start()

    def straight_end():
        start, width = SHARES[1]
        columns = slice(start, start + width)
        whole = w.plane_own[:, columns] + w.plane_stream[:, columns].astype(f32)
        for slot in range(1, 8):
            straight(slot).wait_recv()
            whole = whole + w.straight_in[slot].astype(f32)
        keep(whole, start, width)
        for b in range(2):
            hand(3, b, k).start()

    def give(part, i):
        to = lax.rem(e + i, 8)
        return remote(w.ret.at[part, to], w.back.at[part, e], w.back_s.at[part, i], w.back_r.at[part, i], exp=to)

    def give_in(part, i):
        source = lax.rem(e + 8 - i, 8)
        return remote(w.ret.at[part, source], w.back.at[part, source], w.back_s.at[part, i], w.back_r.at[part, i], exp=source)

    def send_back(part):
        spread = jnp.zeros((256, GROUP), f32)
        for g in range(3):
            q = part * 3 + g
            columns = slice(q * GROUP, (q + 1) * GROUP)
            whole = w.total[0, :, columns].astype(f32)
            for d in range(2):
                scatter(d, q, reach(d, q)).wait_recv()
                whole = whole + w.arrived[d, q, reach(d, q) - 1].astype(f32)
            spread = spread + jnp.dot(spread_map(32, 3, g), whole.astype(bf), preferred_element_type=f32)
        w.ret[part] = spread.astype(bf).reshape(8, 32, GROUP)
        for i in range(1, 8):
            give(part, i).start()
        w.back[part, pl.ds(e, 1)] = w.ret[part, pl.ds(e, 1)]

    def hand(part, b, core):
        start, width = HANDS[part]
        columns = pl.ds(start, width)
        return remote(
            w.ready.at[b, :, columns], w.landed.at[core, :, columns], w.fin_s.at[part, b], w.fin_r.at[part, core],
            pipe=over, ctx=2 * z + b,
        )

    def finish_ring(part):
        for i in range(1, 8):
            give_in(part, i).wait_recv()
        mixed = jnp.dot(w.mix[...], w.back[part].reshape(256, GROUP), preferred_element_type=f32)
        layer_out = (w.sg[part].astype(f32) + (mixed[:96] + mixed[96:])).astype(bf)
        for g in range(3):
            start = (part * 3 + g) * GROUP
            for b in range(2):
                w.ready[b, :, start : start + GROUP] = layer_out[g * 32 + b * 16 : g * 32 + b * 16 + 16]
        for b in range(2):
            hand(part, b, k).start()

    scatter_on(1)
    scatter_on(2)
    reduce_start(0)
    scatter_on(3)
    reduce_on(1)
    send_back(0)
    send_back(1)
    reduce_on(2)
    reduce_start(1)
    reduce_on(3)
    finish_ring(0)
    reduce_end()
    finish_ring(1)
    straight_end()
    for part in range(4):
        for b in range(2):
            hand(part, b, b).wait_recv()
    for b in range(2):
        out_ref[:, b * HALF : (b + 1) * HALF] = w.landed[b]

    for part in range(4):
        for b in range(2):
            hand(part, b, k).wait_send()
    for copy in pair:
        copy.wait_send()

    def sent(i, carry):
        spread_table(i).wait_send()
        straight(i).wait_send()
        for h in range(2):
            plane_box(h, i).wait_send()
            plane_give(h, i).wait_send()
            box(h, i).wait_send()
            give(h, i).wait_send()
        return carry

    lax.fori_loop(1, 8, sent, 0)

    def gone(r, carry):
        for q in range(PIECES):
            for d in range(2):
                @pl.when(r <= reach(d, q))
                def _(d=d, q=q):
                    gather(d, q, r).wait_send()
                    scatter(d, q, r).wait_send()
                    if q < 2:
                        relay(d, q, r).wait_send()
                        reduce(d, q, r).wait_send()
        return carry

    lax.fori_loop(1, 5, gone, 0)

    for n in range(3):
        swap(n).wait_send()
    settle()


BF, F32 = jnp.bfloat16, jnp.float32
SCRATCH = {
    "keys": ((5, KV + 16, 256), BF), "queries": ((1024, KV), BF), "query_doc": ((128, 128), F32), "top": ((1024, 128), F32),
    "sums": ((1024, 128), F32), "mixed": ((1024, LAT), F32), "value_up": ((8, LAT, 128), BF), "heads": ((8, 128, 1024), BF),
    "proj": ((896, 1024), BF), "proj_all": ((1024, 896), BF), "product": ((8, 128, 896), F32),
    "fold_out": ((8, 64, 896), BF), "fold_in": ((8, 64, 896), BF), "cross_out": ((8, 64, 896), BF),
    "cross_in": ((8, 3, 16, 896), BF), "direct_out": ((128, 896), BF), "direct_in": ((7, 16, 896), BF), "part_out": ((8, 16, 896), BF), "parts": ((8, 16, 896), BF), "stream": ((16, D), BF),
    "table": ((2, 16, 128), F32), "brief": ((8, 8, 128), F32), "column": ((256, 128), F32), "sel": ((256, 96), BF), "mix": ((192, 256), BF), "turn": ((640, 640), BF),
    "plane_sel": ((640, 256), BF), "plane_mix": ((512, 640), BF),
    "normed": ((16, D), BF), "pn": ((16, HALF), BF), "ps": ((16, HALF), BF), "tokens": ((8, 32, PLANE), BF),
    "xg": ((2, 96, GROUP), BF), "sg": ((2, 96, GROUP), BF), "plane_stream": ((32, PLANE), BF),
    "outbox": ((2, 8, 32, GROUP), BF), "inbox": ((2, 8, 32, GROUP), BF), "ret": ((2, 8, 32, GROUP), BF),
    "back": ((2, 8, 32, GROUP), BF), "plane_out0": ((8, 80, 896), BF), "plane_in0": ((8, 80, 896), BF),
    "plane_ret0": ((8, 80, 896), BF), "plane_back0": ((8, 80, 896), BF), "plane_out1": ((8, 80, 384), BF),
    "plane_in1": ((8, 80, 384), BF), "plane_ret1": ((8, 80, 384), BF), "plane_back1": ((8, 80, 384), BF),
    "straight_in": ((8, 32, 384), BF),
    "w_in": ((HALF, 512), BF), "w_down": ((256, HALF), BF), "rows": ((8, 80, RING), BF),
    "half": ((8, 80, 512), F32), "half_other": ((8, 80, 512), F32), "hidden": ((640, 256), BF), "total": ((8, 80, RING), BF),
    "arrived": ((2, PIECES, 4, 80, GROUP), BF), "partial": ((8, 32, PLANE), BF), "plane_own": ((32, PLANE), F32),
    "plane_arrived": ((2, 2, 4, 32, 512), BF), "ready": ((2, 16, HALF), BF), "landed": ((2, 16, HALF), BF),
    "load": ((9,), None), "chain_s": ((5, 4), None), "chain_r": ((5, 4), None), "share_s": ((5,), None), "share_r": ((5,), None),
    "proj_s": ((1,), None), "proj_r": ((1,), None), "head_s": ((2, 2, 5), None), "head_r": ((2, 2, 5), None),
    "fold_s": ((8,), None), "fold_r": ((8,), None), "cross_s": ((8, 3), None), "cross_r": ((8, 3), None),
    "part_s": ((8,), None), "part_r": ((8,), None), "direct_s": ((8,), None), "direct_r": ((8,), None),
    "pair_s": ((6,), None), "pair_r": ((6,), None), "loc": ((3,), None), "table_s": ((8,), None), "table_r": ((8,), None),
    "box_s": ((2, 8), None), "box_r": ((2, 8), None), "relay_s": ((2, 2, 5), None), "relay_r": ((2, 2, 5), None),
    "plane_s": ((2, 8), None), "plane_r": ((2, 8), None), "give_s": ((2, 8), None), "give_r": ((2, 8), None),
    "ag_s": ((2, PIECES, 5), None), "ag_r": ((2, PIECES, 5), None), "half_s": ((3,), None), "half_r": ((3,), None),
    "rs_s": ((2, PIECES, 4), None), "rs_r": ((2, PIECES, 4), None), "red_s": ((2, 2, 4), None), "red_r": ((2, 2, 4), None), "straight_s": ((8,), None), "straight_r": ((8,), None),
    "back_s": ((2, 8), None), "back_r": ((2, 8), None), "fin_s": ((4, 2), None), "fin_r": ((4, 2), None),
}


def on_device(
    queries, latent_rows, doc_ids, value_up, out_proj, residual_in, norm_gain, expert_ids, gate_weights, gate_proj, up_proj,
    down_proj,
):
    vmem, any_space = pl.BlockSpec(memory_space=pltpu.VMEM), pl.BlockSpec(memory_space=pl.ANY)
    return pl.pallas_call(
        layer_kernel,
        out_shape=jax.ShapeDtypeStruct((16, D), BF),
        in_specs=[vmem] * 7 + [any_space] * 5,
        out_specs=vmem,
        scratch_shapes=[
            pltpu.SemaphoreType.DMA(shape) if kind is None else pltpu.VMEM(shape, kind) for shape, kind in SCRATCH.values()
        ],
        compiler_params=pltpu.CompilerParams(collective_id=1, has_side_effects=True, vmem_limit_bytes=60 << 20),
        cost_estimate=pl.CostEstimate(flops=8_000_000_000, bytes_accessed=10_000_000, transcendentals=2_000_000),
        name="layer",
    )(
        queries[0].transpose(1, 2, 0), latent_rows[0].T, doc_ids, expert_ids[0].T, gate_weights[0].T, residual_in[0], norm_gain,
        value_up[0], out_proj[0].T, gate_proj[0, 0], up_proj[0, 0], down_proj[0, 0],
    )[None]


def solution(mesh):
    return jax.shard_map(
        on_device,
        mesh=mesh,
        in_specs=(
            P("pipe", "ctx", "exp", None),
            P("pipe", "ctx", None),
            P("pipe", "ctx"),
            P("pipe", "exp", None, None),
            P("pipe", "exp", "ctx"),
            P("pipe", ("ctx", "exp"), None),
            P("pipe", None),
            P("pipe", ("ctx", "exp"), None),
            P("pipe", ("ctx", "exp"), None),
            P("pipe", "exp", None, "ctx"),
            P("pipe", "exp", None, "ctx"),
            P("pipe", "exp", "ctx", None),
        ),
        out_specs=P("pipe", ("ctx", "exp"), None),
        check_vma=False,
    )
```

```python
import math
import types

import jax
import jax.numpy as jnp
from jax import lax
from jax.experimental import pallas as pl
from jax.experimental.pallas import tpu as pltpu
from jax.sharding import PartitionSpec as P

D = 7168
HALF = D // 2
HD = 128
ROPE = 64
LAT = 512
KV = LAT + ROPE
MESH = pl.DeviceIdType.MESH

epsilon = 1e-06
masked_score = -1e30
score_scale = 1.0 / math.sqrt(HD + ROPE)
KEY_PIECES = ((0, 144), (144, 144), (288, 144), (432, 160))


def remote(src, dst, send_sem, recv_sem, **device):
    return pltpu.make_async_remote_copy(
        src_ref=src,
        dst_ref=dst,
        send_sem=send_sem,
        recv_sem=recv_sem,
        device_id=device,
        device_id_type=MESH,
    )


def take(ref, sem):
    pltpu.make_async_copy(ref, ref, sem).wait()


def meet(peers):
    barrier = pltpu.get_barrier_semaphore()
    for device in peers:
        pl.semaphore_signal(barrier, 1, device_id=device, device_id_type=MESH)
    pl.semaphore_wait(barrier, len(peers))


def squeeze_map(rows, groups, group, dtype=jnp.bfloat16):
    row = lax.broadcasted_iota(jnp.int32, (80, 8 * rows), 0).astype(jnp.float32)
    col = lax.broadcasted_iota(jnp.int32, (80, 8 * rows), 1).astype(jnp.float32)
    source = jnp.floor((row + 0.5) * 0.1)
    want = source * rows + (row - source * 10) + group * 10
    return jnp.where(col == want, 1.0, 0.0).astype(dtype)


def spread_map(rows, groups, group, dtype=jnp.bfloat16):
    row = lax.broadcasted_iota(jnp.int32, (8 * rows, 80), 0).astype(jnp.float32)
    col = lax.broadcasted_iota(jnp.int32, (8 * rows, 80), 1).astype(jnp.float32)
    source = jnp.floor((col + 0.5) * 0.1)
    want = source * rows + (col - source * 10) + group * 10
    return jnp.where(row == want, 1.0, 0.0).astype(dtype)


RING = 2304
GROUP = 384
PIECES = RING // GROUP
PLANE = HALF - RING
SHARES = ((0, 896), (896, 384))
HANDS = ((0, 3 * GROUP), (3 * GROUP, 3 * GROUP), (RING, 896), (RING + 896, 384))
SUMS = ((0, 512), (512, 384))


def reach(d, q):
    return 4 if q % 2 == d else 3


def attend(w, q_ref, lat_ref, doc_ref, vu_ref, op_ref, residual_ref, start_rest, make_tables):
    p, c, e = lax.axis_index("pipe"), lax.axis_index("ctx"), lax.axis_index("exp")
    k = lax.rem(c, 2)
    z = lax.div(c, 2)
    kk = 1 - k
    other = 2 * z + kk
    right = 2 * lax.rem(z + 1, 8) + k
    left = 2 * lax.rem(z + 7, 8) + k
    y = lax.div(e, 4)
    x = lax.rem(e, 4)
    bf, f32 = jnp.bfloat16, jnp.float32
    my_lanes = pl.ds(pl.multiple_of(k * 128, 128), 128)
    their_lanes = pl.ds(pl.multiple_of(kk * 128, 128), 128)
    my_columns = pl.ds(pl.multiple_of(k * 448, 16), 448)

    def chain(s, q):
        piece = pl.ds(*KEY_PIECES[q])
        return remote(
            w.keys.at[s - 1, piece, my_lanes], w.keys.at[s, piece, my_lanes], w.chain_s.at[0], w.chain_r.at[s - 1, q], ctx=right
        )

    def share(s):
        return remote(w.keys.at[s, :, my_lanes], w.keys.at[s, :, my_lanes], w.share_s.at[0], w.share_r.at[s], ctx=other)

    def share_in(s):
        return remote(w.keys.at[s, :, their_lanes], w.keys.at[s, :, their_lanes], w.share_s.at[0], w.share_r.at[s], ctx=other)

    for q in range(4):
        chain(1, q).start()
    share(0).start()
    own_proj = pltpu.make_async_copy(op_ref, w.proj.at[my_columns], w.load.at[1])
    own_proj.start()
    pair_proj = remote(op_ref, w.proj.at[my_columns], w.proj_s.at[0], w.proj_r.at[0], ctx=other)
    pair_proj.start()
    up_loads = [
        pltpu.make_async_copy(vu_ref.at[h], w.value_up.at[h], w.load.at[0]) for h in range(8)
    ]
    for copy in up_loads:
        copy.start()
    start_rest()

    for h in range(8):
        w.queries[h * 128 : (h + 1) * 128, :] = jnp.transpose(q_ref[h])
    w.top[...] = jnp.full((1024, 128), masked_score, f32)
    w.sums[...] = jnp.zeros((1024, 128), f32)
    w.mixed[...] = jnp.zeros((1024, LAT), f32)
    contract_last = (((1,), (1,)), ((), ()))
    query_pos = c * 128 + lax.broadcasted_iota(jnp.int32, (128, 256), 0)

    def attend_to(s):
        key_doc = w.keys[s, KV:, :].astype(f32)[0:1]
        key_pos = lax.rem(z + 8 - s, 8) * 256 + lax.broadcasted_iota(jnp.int32, (128, 256), 1)
        query_doc = jnp.concatenate([w.query_doc[...]] * 2, axis=1)
        hidden = jnp.where((key_pos <= query_pos) & (query_doc == key_doc), 0.0, masked_score)
        hidden = jnp.concatenate([hidden] * 4, axis=0)

        def some(j, carry):
            at = pl.ds(pl.multiple_of(j * 512, 512), 512)
            scores = jnp.dot(w.queries[at], w.keys[s, 0:KV, :], preferred_element_type=f32) * score_scale + hidden
            before = w.top[at]
            highest = jnp.maximum(before, jnp.max(scores, axis=1, keepdims=True))
            shrink = jnp.exp(before - highest)
            weights = jnp.exp(scores - jnp.concatenate([highest, highest], axis=1))
            w.top[at] = highest
            w.sums[at] = w.sums[at] * shrink + jnp.sum(weights, axis=1, keepdims=True)
            update = lax.dot_general(weights.astype(bf), w.keys[s, 0:LAT, :], contract_last, preferred_element_type=f32)
            w.mixed[at] = w.mixed[at] * jnp.concatenate([shrink] * 4, axis=1) + update
            return carry

        lax.fori_loop(0, 2, some, 0)

    def visit(s, carry):
        def pass_keys(pieces):
            for q in pieces:
                chain(s, q).wait_recv()

                @pl.when(s < 4)
                def _(q=q):
                    chain(s + 1, q).start()

        pass_keys((0, 1))
        share_in(s - 1).wait_recv()
        attend_to(s - 1)
        pass_keys((2, 3))
        share(s).start()
        return carry

    lax.fori_loop(1, 5, visit, 0)
    share_in(4).wait_recv()
    attend_to(4)

    take(w.value_up, w.load.at[0])

    def gather(d, q, r):
        piece = pl.ds(q * 64, 64)
        if d == 0:
            return remote(w.heads.at[r - 1, piece], w.heads.at[r, piece], w.head_s.at[0], w.head_r.at[d, q, r - 1], ctx=right)
        return remote(
            w.heads.at[lax.rem(9 - r, 8), piece], w.heads.at[8 - r, piece], w.head_s.at[0], w.head_r.at[d, q, r - 1], ctx=left
        )

    for h in range(8):
        at = slice(h * 128, (h + 1) * 128)
        latent_out = (w.mixed[at] / jnp.concatenate([w.sums[at]] * 4, axis=1)).astype(bf)
        w.heads[0, :, at] = jnp.dot(latent_out, w.value_up[h], preferred_element_type=f32).astype(bf)
    for q in range(2):
        for d in range(2):
            gather(d, q, 1).start()

    own_proj.wait()
    pair_proj.wait_recv()
    w.proj_all[...] = jnp.transpose(w.proj[...])

    y_mine = pl.multiple_of(y * 64, 64)
    y_theirs = pl.multiple_of((1 - y) * 64, 64)
    x_mine = pl.multiple_of(x * 16, 16)

    def fold(slot):
        return remote(w.fold_out.at[slot], w.fold_in.at[slot], w.fold_s.at[0], w.fold_r.at[slot], exp=lax.rem(e + 4, 8))

    def cross(slot, i):
        to = lax.rem(x + i, 4)
        return remote(
            w.cross_out.at[slot, pl.ds(pl.multiple_of(to * 16, 16), 16)], w.cross_in.at[slot, i - 1],
            w.cross_s.at[0], w.cross_r.at[slot], exp=4 * y + to,
        )

    def deliver(slot):
        return remote(
            w.part_out.at[slot], w.parts.at[z], w.part_s.at[0], w.part_r.at[0], ctx=2 * lax.rem(z + 8 - slot, 8) + k
        )

    def project(slot):
        w.product[slot] = jnp.dot(w.heads[slot], w.proj_all[...], preferred_element_type=f32)
        w.fold_out[slot] = w.product[slot, pl.ds(y_theirs, 64), :].astype(bf)
        fold(slot).start()

    def direct(i):
        to = lax.rem(e + i, 8)
        return remote(
            w.direct_out.at[pl.ds(pl.multiple_of(to * 16, 16), 16)], w.direct_in.at[i - 1], w.direct_s.at[0], w.direct_r.at[0], exp=to
        )

    def project_last():
        w.product[4] = jnp.dot(w.heads[4], w.proj_all[...], preferred_element_type=f32)
        w.direct_out[...] = w.product[4].astype(bf)
        for i in range(1, 8):
            direct(i).start()

    def sum_last():
        whole = w.product[4, pl.ds(pl.multiple_of(e * 16, 16), 16), :]
        take(w.direct_in, w.direct_r.at[0])
        for i in range(7):
            whole = whole + w.direct_in[i].astype(f32)
        w.part_out[4] = whole.astype(bf)
        deliver(4).start()

    def over_y(slot):
        fold(slot).wait_recv()
        both = w.product[slot, pl.ds(y_mine, 64), :] + w.fold_in[slot].astype(f32)
        w.product[slot, pl.ds(y_mine, 64), :] = both
        w.cross_out[slot] = both.astype(bf)
        for i in range(1, 4):
            cross(slot, i).start()

    def over_x(slot):
        whole = w.product[slot, pl.ds(pl.multiple_of(y_mine + x_mine, 16), 16), :]
        take(w.cross_in.at[slot], w.cross_r.at[slot])
        for i in range(3):
            whole = whole + w.cross_in[slot, i].astype(f32)
        w.part_out[slot] = whole.astype(bf)

        @pl.when(slot >= 1)
        def _():
            deliver(slot).start()

    def turn(r, carry):
        @pl.when((r >= 1) & (r <= 4))
        def _():
            for q in range(2):
                for d in range(2):
                    @pl.when(r <= reach(d, q))
                    def _(d=d, q=q):
                        gather(d, q, r).wait_recv()

                    @pl.when(r + 1 <= reach(d, q))
                    def _(d=d, q=q):
                        gather(d, q, r + 1).start()

        @pl.when(r == 4)
        def _():
            project_last()

        for stage, act in enumerate((project, over_y, over_x)):
            now = r - stage

            @pl.when((now >= 0) & (now <= 3))
            def _(act=act, now=now):
                act(now)

            @pl.when((now >= 1) & (now <= 3))
            def _(act=act, now=now):
                act(8 - now)

        @pl.when(r == 5)
        def _():
            sum_last()

        make_tables(r)
        return carry

    lax.fori_loop(0, 7, turn, 0)
    w.parts[pl.ds(z, 1)] = w.part_out[0:1]
    take(w.parts.at[pl.ds(0, 7)], w.part_r.at[0])
    for other_z in range(8):
        columns = slice(other_z * 896, (other_z + 1) * 896)
        w.stream[:, columns] = (residual_ref[:, columns].astype(f32) + w.parts[other_z].astype(f32)).astype(bf)

    def settle():
        pair_proj.wait_send()
        take(w.keys.at[pl.ds(1, 4), :, my_lanes], w.chain_s.at[0])
        take(w.keys.at[:, :, my_lanes], w.share_s.at[0])
        take(w.heads.at[pl.ds(1, 7)], w.head_s.at[0])
        take(w.fold_out.at[pl.ds(0, 7)], w.fold_s.at[0])
        take(w.cross_in.at[pl.ds(0, 7)], w.cross_s.at[0])
        take(w.part_out.at[pl.ds(0, 7)], w.part_s.at[0])
        take(w.direct_in, w.direct_s.at[0])

    return settle


def column_of(rows):
    diagonal = lax.broadcasted_iota(jnp.int32, rows.shape, 0) == lax.broadcasted_iota(jnp.int32, rows.shape, 1)
    return jnp.sum(jnp.where(diagonal, rows, 0.0), axis=1, keepdims=True)


def tables(w, ids_ref, weights_ref, k):
    f32 = jnp.float32
    ids = [column_of(jnp.broadcast_to(ids_ref[i : i + 1, :].astype(f32), (16, 16))) for i in range(2)]
    weights = [column_of(jnp.broadcast_to(weights_ref[i : i + 1, :], (16, 16))) for i in range(2)]
    lane = lax.broadcasted_iota(jnp.int32, (16, 128), 1)
    expert = lane.astype(f32)
    first, second = (jnp.where(ids[i] == expert, 1.0, 0.0) for i in range(2))
    earlier = lax.broadcasted_iota(jnp.int32, (16, 16), 1) < lax.broadcasted_iota(jnp.int32, (16, 16), 0)
    counts = jnp.dot(jnp.where(earlier, 1.0, 0.0), first + second, preferred_element_type=f32)
    ranks = (
        jnp.sum(first * counts, axis=1, keepdims=True),
        jnp.sum(second * (counts + first), axis=1, keepdims=True),
    )
    table = jnp.zeros((16, 128), f32)
    for i in range(2):
        table = jnp.where(lane == i, ids[i] * 8.0 + ranks[i], table)
        table = jnp.where(lane == i + 2, weights[i], table)
    w.table[pl.ds(k, 1)] = table[None]


def decode(shape, axis, groups, height):
    row = lax.broadcasted_iota(jnp.int32, shape, axis).astype(jnp.float32)
    expert = jnp.floor((row + 0.5) * (1.0 / height))
    inner = row - expert * height
    group = jnp.floor((inner + 0.5) * 0.1)
    within = inner - group * 10.0
    block = jnp.where(within >= 5.0, 1.0, 0.0)
    slot = jnp.where(group < groups, expert * 8.0 + within - block * 5.0, -1.0)
    return slot, group * 2.0 + block


def choose_matrix(columns, sel, groups, height):
    span, count = groups * 32, 8 * height
    lanes = jnp.transpose(columns)
    slot, owner = decode((count, 1), 0, groups, height)
    token = lax.shift_right_logical(lax.broadcasted_iota(jnp.int32, (count, span), 1), 4).astype(jnp.float32)
    hit = (owner == token) & ((slot == lanes[0:1, :span]) | (slot == lanes[1:2, :span]))
    sel[...] = jnp.where(hit, 1.0, 0.0).astype(jnp.bfloat16)


def weigh_matrix(columns, mix, groups, height):
    span, count = groups * 32, 8 * height
    slot, owner = decode((1, count), 1, groups, height)
    token = lax.shift_right_logical(lax.broadcasted_iota(jnp.int32, (span, count), 0), 4).astype(jnp.float32)
    slot = jnp.where(owner == token, slot, -1.0)
    weight = jnp.zeros((span, count), jnp.float32)
    for i in range(2):
        weight = weight + jnp.where(slot == columns[:span, i : i + 1], columns[:span, i + 2 : i + 3], 0.0)
    high = weight.astype(jnp.bfloat16)
    mix[0:span, :] = high
    mix[span : 2 * span, :] = (weight - high.astype(jnp.float32)).astype(jnp.bfloat16)


def layer_kernel(
    q_ref, lat_ref, doc_ref, ids_ref, weights_ref, residual_ref, gain_ref, vu_ref, op_ref, gate_ref, up_ref, down_ref,
    out_ref, *scratch
):
    w = types.SimpleNamespace(**dict(zip(SCRATCH, scratch, strict=True)))
    p, c, e = lax.axis_index("pipe"), lax.axis_index("ctx"), lax.axis_index("exp")
    k = lax.rem(c, 2)
    z = lax.div(c, 2)
    kk = 1 - k
    other = 2 * z + kk
    right = 2 * lax.rem(z + 1, 8) + k
    left = 2 * lax.rem(z + 7, 8) + k
    over = 1 - p
    mine = pl.multiple_of(k * HALF, 128)
    theirs = pl.multiple_of(kk * HALF, 128)
    my_lane = pl.multiple_of(k * 128, 128)
    up_lane = pl.multiple_of(256 + k * 128, 128)

    bf, f32 = jnp.bfloat16, jnp.float32

    w.keys[0, 0:KV, pl.ds(my_lane, 128)] = lat_ref[...]
    doc_row = jnp.broadcast_to(doc_ref[...].astype(f32), (128, 128))
    w.keys[0, KV:, pl.ds(my_lane, 128)] = doc_row[0:16].astype(bf)
    w.query_doc[...] = jnp.broadcast_to(column_of(doc_row), (128, 128))
    meet(
        [{"ctx": other}, {"pipe": over}, {"pipe": over, "ctx": other}]
        + [{"ctx": 2 * lax.rem(z + i, 8) + k} for i in range(1, 8)]
        + [{"exp": lax.rem(e + i, 8)} for i in range(1, 8)]
    )
    local = [
        pltpu.make_async_copy(gate_ref.at[pl.ds(mine, HALF), :], w.w_in.at[:, pl.ds(my_lane, 128)], w.loc.at[0]),
        pltpu.make_async_copy(up_ref.at[pl.ds(mine, HALF), :], w.w_in.at[:, pl.ds(up_lane, 128)], w.loc.at[1]),
        pltpu.make_async_copy(down_ref.at[:, pl.ds(mine, HALF)], w.w_down.at[pl.ds(my_lane, 128), :], w.loc.at[2]),
    ]
    pair = [
        remote(w.normed.at[:, pl.ds(theirs, HALF)], w.pn, w.pair_s.at[0], w.pair_r.at[0], ctx=other),
        remote(w.stream.at[:, pl.ds(theirs, HALF)], w.ps, w.pair_s.at[1], w.pair_r.at[1], ctx=other),
        remote(gate_ref.at[pl.ds(theirs, HALF), :], w.w_in.at[:, pl.ds(my_lane, 128)], w.pair_s.at[2], w.pair_r.at[2], ctx=other),
        remote(up_ref.at[pl.ds(theirs, HALF), :], w.w_in.at[:, pl.ds(up_lane, 128)], w.pair_s.at[3], w.pair_r.at[3], ctx=other),
        remote(down_ref.at[:, pl.ds(theirs, HALF)], w.w_down.at[pl.ds(my_lane, 128), :], w.pair_s.at[4], w.pair_r.at[4], ctx=other),
    ]
    pair.append(remote(w.table.at[k], w.table.at[k], w.pair_s.at[5], w.pair_r.at[5], ctx=other))

    def start_rest():
        tables(w, ids_ref, weights_ref, k)
        pair[5].start()
        for copy in local:
            copy.start()
        for copy in pair[2:5]:
            copy.start()

    def spread_table(i):
        return remote(w.brief.at[0], w.brief.at[i], w.table_s.at[0], w.table_r.at[0], ctx=2 * lax.rem(z + i, 8) + k)

    def chip_table():
        return jnp.concatenate([w.table[...].reshape(32, 128)] * 4, axis=0)

    def make_tables(r):
        @pl.when(r == 3)
        def _():
            pair[5].wait_recv()
            w.brief[0] = jnp.transpose(chip_table())[0:8]
            for i in range(1, 8):
                spread_table(i).start()

        @pl.when(r == 4)
        def _():
            choose_matrix(chip_table(), w.sel, 3, 32)

        @pl.when(r == 6)
        def _():
            take(w.brief.at[pl.ds(0, 7)], w.table_r.at[0])
            for i in range(8):
                w.column[i * 32 : (i + 1) * 32, :] = jnp.transpose(jnp.concatenate([w.brief[i]] * 16, axis=0))[0:32]
            choose_matrix(w.column[...], w.plane_sel, 8, 80)

    settle = attend(w, q_ref, lat_ref, doc_ref, vu_ref, op_ref, residual_ref, start_rest, make_tables)
    wide = w.stream[...].astype(f32)
    mean_square = jnp.mean(wide * wide, axis=1, keepdims=True)
    w.normed[...] = (wide * lax.rsqrt(mean_square + epsilon) * gain_ref[...]).astype(bf)
    for copy in pair[:2]:
        copy.start()

    def place(target, plane_target, source, start, core):
        for g in range(PIECES):
            lanes = pl.ds(start + g * GROUP if isinstance(start, int) else pl.multiple_of(start + g * GROUP, 128), GROUP)
            target[g // 3, pl.ds(pl.multiple_of(g % 3 * 32 + core * 16, 16), 16), :] = source[:, lanes]
        lanes = pl.ds(start + RING if isinstance(start, int) else pl.multiple_of(start + RING, 128), PLANE)
        plane_target[pl.ds(pl.multiple_of(core * 16, 16), 16), :] = source[:, lanes]

    place(w.xg, w.tokens.at[0], w.normed, mine, k)
    place(w.sg, w.plane_stream, w.stream, mine, k)
    pair[0].wait_recv()
    place(w.xg, w.tokens.at[0], w.pn, 0, kk)

    def relay(d, q, r):
        columns = pl.ds(q * (PLANE // 2), PLANE // 2)
        src, dst, to = (r - 1, r, right) if d == 0 else (lax.rem(9 - r, 8), 8 - r, left)
        return remote(w.tokens.at[src, :, columns], w.tokens.at[dst, :, columns], w.relay_s.at[0], w.relay_r.at[d, q, r - 1], ctx=to)

    def relay_round(r):
        for q in range(2):
            for d in range(2):
                if r <= reach(d, q):
                    relay(d, q, r).wait_recv()
                if r + 1 <= reach(d, q):
                    relay(d, q, r + 1).start()

    for q in range(2):
        for d in range(2):
            relay(d, q, 1).start()

    def box(part, i):
        to = lax.rem(e + i, 8)
        return remote(w.outbox.at[part, to], w.inbox.at[part, e], w.box_s.at[0], w.box_r.at[part], exp=to)

    for part in range(2):
        chosen = jnp.dot(w.sel[...], w.xg[part], preferred_element_type=f32).astype(bf)
        w.outbox[part] = chosen.reshape(8, 32, GROUP)
        for i in range(1, 8):
            box(part, i).start()
        w.inbox[part, pl.ds(e, 1)] = w.outbox[part, pl.ds(e, 1)]
    relay_round(1)

    def gather(d, q, r):
        columns = pl.ds(q * GROUP, GROUP)
        src, dst, to = (r - 1, r, right) if d == 0 else (lax.rem(9 - r, 8), 8 - r, left)
        return remote(w.rows.at[src, :, columns], w.rows.at[dst, :, columns], w.ag_s.at[0], w.ag_r.at[d, q, r - 1], ctx=to)

    for part in range(2):
        take(w.inbox.at[part, pl.ds(0, 7)], w.box_r.at[part])
        landed_rows = w.inbox[part].reshape(256, GROUP)
        for g in range(3):
            q = part * 3 + g
            w.rows[0, :, q * GROUP : (q + 1) * GROUP] = jnp.dot(
                squeeze_map(32, 3, g), landed_rows, preferred_element_type=f32
            ).astype(bf)
            for d in range(2):
                gather(d, q, 1).start()
        relay_round(2 + part)
    relay_round(4)

    plane_out, plane_in = (w.plane_out0, w.plane_out1), (w.plane_in0, w.plane_in1)
    plane_ret, plane_back = (w.plane_ret0, w.plane_ret1), (w.plane_back0, w.plane_back1)

    def plane_box(h, i):
        to = lax.rem(e + i, 8)
        return remote(plane_out[h].at[to], plane_in[h].at[e], w.plane_s.at[h], w.plane_r.at[h], exp=to)

    for h, (start, width) in enumerate(SHARES):
        tokens = w.tokens[:, :, start : start + width].reshape(256, width)
        chosen = jnp.dot(w.plane_sel[...], tokens, preferred_element_type=f32).astype(bf)
        plane_out[h][...] = chosen.reshape(8, 80, width)
        for i in range(1, 8):
            plane_box(h, i).start()
        plane_in[h][pl.ds(e, 1)] = plane_out[h][pl.ds(e, 1)]
    pair[1].wait_recv()
    place(w.sg, w.plane_stream, w.ps, 0, kk)
    for copy in local:
        copy.wait()
    for copy in pair[2:5]:
        copy.wait_recv()

    BATCHES = ((0, 4), (5, 3), (4, 1))

    def swap(n):
        slots = pl.ds(*BATCHES[n])
        return remote(w.half.at[slots], w.half_other.at[slots], w.half_s.at[0], w.half_r.at[n], ctx=other)

    def ring_half(slot):
        w.half[slot] = w.half[slot] + jnp.dot(w.rows[slot], w.w_in[0:RING, :], preferred_element_type=f32)

    def second_half(n):
        first, count = BATCHES[n]
        swap(n).wait_recv()
        slots = slice(first, first + count)
        both = (w.half[slots] + w.half_other[slots]).reshape(count * 80, 512)
        gate = both[:, :256]
        hidden = (gate / (1.0 + jnp.exp(-gate)) * both[:, 256:]).astype(bf)
        w.hidden[first * 80 : (first + count) * 80, :] = hidden
        for part in range(2):
            columns = slice(part * 3 * GROUP, (part + 1) * 3 * GROUP)
            out = jnp.dot(hidden, w.w_down[:, columns], preferred_element_type=f32).astype(bf)
            w.total[slots, :, columns] = out.reshape(count, 80, 3 * GROUP)

    def scatter(d, q, j):
        far = reach(d, q) + 1 - j
        slot, to = (far, left) if d == 0 else (8 - far, right)
        columns = pl.ds(q * GROUP, GROUP)
        return remote(w.total.at[slot, :, columns], w.arrived.at[d, q, j - 1], w.rs_s.at[0], w.rs_r.at[d, q, j - 1], ctx=to)

    w.half[...] = jnp.zeros((8, 80, 512), f32)
    ring_half(0)
    for r in range(1, 5):
        for q in range(PIECES):
            for d in range(2):
                if r <= reach(d, q):
                    gather(d, q, r).wait_recv()
                if r + 1 <= reach(d, q):
                    gather(d, q, r + 1).start()
        ring_half(r)
        if r < 4:
            ring_half(8 - r)
        if r == 1:
            weigh_matrix(chip_table(), w.mix, 3, 32)
            for slot in range(8):
                w.turn[slot * 80 : (slot + 1) * 80, :] = squeeze_map(80, 8, slot)
        if r == 2:
            weigh_matrix(w.column[...], w.plane_mix, 8, 80)
        if r == 3:
            for h, (start, width) in enumerate(SHARES):
                take(plane_in[h].at[pl.ds(0, 7)], w.plane_r.at[h])
                turned = jnp.dot(w.turn[...], plane_in[h][...].reshape(640, width), preferred_element_type=f32).astype(bf)
                lanes = slice(RING + start, RING + start + width)
                more = jnp.dot(turned, w.w_in[lanes, :], preferred_element_type=f32)
                w.half[...] = w.half[...] + more.reshape(8, 80, 512)
            swap(0).start()
            swap(1).start()
            second_half(0)
            second_half(1)
            for q in range(PIECES):
                for d in range(2):
                    if reach(d, q) == 3:
                        scatter(d, q, 1).start()
    swap(2).start()
    second_half(2)

    def scatter_on(j):
        for q in range(PIECES):
            for d in range(2):
                if j + 1 <= reach(d, q):
                    far = reach(d, q) - j
                    slot = far if d == 0 else 8 - far
                    columns = slice(q * GROUP, (q + 1) * GROUP)
                    scatter(d, q, j).wait_recv()
                    w.total[slot, :, columns] = (
                        w.total[slot, :, columns].astype(f32) + w.arrived[d, q, j - 1].astype(f32)
                    ).astype(bf)
                    scatter(d, q, j + 1).start()

    for q in range(PIECES):
        for d in range(2):
            if reach(d, q) == 4:
                scatter(d, q, 1).start()

    def plane_give(h, i):
        to = lax.rem(e + i, 8)
        return remote(plane_ret[h].at[to], plane_back[h].at[e], w.give_s.at[h], w.give_r.at[h], exp=to)

    hidden = jnp.dot(w.turn[...], w.hidden[...], preferred_element_type=f32).astype(bf)
    for h, (start, width) in enumerate(SHARES):
        out = jnp.dot(hidden, w.w_down[:, RING + start : RING + start + width], preferred_element_type=f32).astype(bf)
        plane_ret[h][...] = out.reshape(8, 80, width)
        for i in range(1, 8):
            plane_give(h, i).start()
        plane_back[h][pl.ds(e, 1)] = plane_ret[h][pl.ds(e, 1)]

    def reduce(d, q, j):
        far = reach(d, q) + 1 - j
        slot, to = (far, left) if d == 0 else (8 - far, right)
        start, width = SUMS[q]
        return remote(
            w.partial.at[slot, :, pl.ds(start, width)], w.plane_arrived.at[d, q, j - 1, :, pl.ds(0, width)],
            w.red_s.at[0], w.red_r.at[d, q, j - 1], ctx=to,
        )

    def straight(slot):
        start, width = SHARES[1]
        return remote(
            w.partial.at[slot, :, pl.ds(start, width)], w.straight_in.at[slot], w.straight_s.at[0], w.straight_r.at[0],
            ctx=2 * lax.rem(z + 8 - slot, 8) + k,
        )

    def reduce_start(h):
        start, width = SHARES[h]
        take(plane_back[h].at[pl.ds(0, 7)], w.give_r.at[h])
        mixed = jnp.dot(w.plane_mix[...], plane_back[h][...].reshape(640, width), preferred_element_type=f32)
        mixed = mixed[:256] + mixed[256:]
        w.plane_own[:, start : start + width] = mixed[:32]
        w.partial[:, :, start : start + width] = mixed.astype(bf).reshape(8, 32, width)
        if h == 0:
            for q in range(2):
                for d in range(2):
                    reduce(d, q, 1).start()
        else:
            for slot in (4, 3, 5, 2, 6, 1, 7):
                straight(slot).start()

    def reduce_on(j):
        for q, (start, width) in enumerate(SUMS):
            for d in range(2):
                if j + 1 <= reach(d, q):
                    far = reach(d, q) - j
                    slot = far if d == 0 else 8 - far
                    columns = slice(start, start + width)
                    reduce(d, q, j).wait_recv()
                    w.partial[slot, :, columns] = (
                        w.partial[slot, :, columns].astype(f32) + w.plane_arrived[d, q, j - 1, :, 0:width].astype(f32)
                    ).astype(bf)
                    reduce(d, q, j + 1).start()

    def keep(whole, start, width):
        whole = whole.astype(bf)
        for b in range(2):
            w.ready[b, :, RING + start : RING + start + width] = whole[b * 16 : (b + 1) * 16]

    def reduce_end():
        for q, (start, width) in enumerate(SUMS):
            columns = slice(start, start + width)
            whole = w.plane_own[:, columns] + w.plane_stream[:, columns].astype(f32)
            for d in range(2):
                reduce(d, q, reach(d, q)).wait_recv()
                whole = whole + w.plane_arrived[d, q, reach(d, q) - 1, :, 0:width].astype(f32)
            keep(whole, start, width)
        for b in range(2):
            hand(2, b, k).start()

    def straight_end():
        start, width = SHARES[1]
        columns = slice(start, start + width)
        whole = w.plane_own[:, columns] + w.plane_stream[:, columns].astype(f32)
        take(w.straight_in.at[pl.ds(0, 7)], w.straight_r.at[0])
        for slot in range(1, 8):
            whole = whole + w.straight_in[slot].astype(f32)
        keep(whole, start, width)
        for b in range(2):
            hand(3, b, k).start()

    def give(part, i):
        to = lax.rem(e + i, 8)
        return remote(w.ret.at[part, to], w.back.at[part, e], w.back_s.at[0], w.back_r.at[part], exp=to)

    def send_back(part):
        spread = jnp.zeros((256, GROUP), f32)
        for g in range(3):
            q = part * 3 + g
            columns = slice(q * GROUP, (q + 1) * GROUP)
            whole = w.total[0, :, columns].astype(f32)
            for d in range(2):
                scatter(d, q, reach(d, q)).wait_recv()
                whole = whole + w.arrived[d, q, reach(d, q) - 1].astype(f32)
            spread = spread + jnp.dot(spread_map(32, 3, g), whole.astype(bf), preferred_element_type=f32)
        w.ret[part] = spread.astype(bf).reshape(8, 32, GROUP)
        for i in range(1, 8):
            give(part, i).start()
        w.back[part, pl.ds(e, 1)] = w.ret[part, pl.ds(e, 1)]

    def hand(part, b, core):
        start, width = HANDS[part]
        columns = pl.ds(start, width)
        return remote(
            w.ready.at[b, :, columns], w.landed.at[core, :, columns], w.fin_s.at[0], w.fin_r.at[0],
            pipe=over, ctx=2 * z + b,
        )

    def finish_ring(part):
        take(w.back.at[part, pl.ds(0, 7)], w.back_r.at[part])
        mixed = jnp.dot(w.mix[...], w.back[part].reshape(256, GROUP), preferred_element_type=f32)
        layer_out = (w.sg[part].astype(f32) + (mixed[:96] + mixed[96:])).astype(bf)
        for g in range(3):
            start = (part * 3 + g) * GROUP
            for b in range(2):
                w.ready[b, :, start : start + GROUP] = layer_out[g * 32 + b * 16 : g * 32 + b * 16 + 16]
        for b in range(2):
            hand(part, b, k).start()

    scatter_on(1)
    scatter_on(2)
    reduce_start(0)
    scatter_on(3)
    reduce_on(1)
    send_back(0)
    send_back(1)
    reduce_on(2)
    reduce_start(1)
    reduce_on(3)
    finish_ring(0)
    reduce_end()
    finish_ring(1)
    straight_end()
    take(w.landed, w.fin_r.at[0])
    for b in range(2):
        out_ref[:, b * HALF : (b + 1) * HALF] = w.landed[b]

    take(w.ready, w.fin_s.at[0])
    for copy in pair:
        copy.wait_send()
    take(w.brief.at[pl.ds(0, 7)], w.table_s.at[0])
    take(w.tokens.at[pl.ds(1, 7)], w.relay_s.at[0])
    take(w.inbox.at[:, pl.ds(0, 7)], w.box_s.at[0])
    take(w.back.at[:, pl.ds(0, 7)], w.back_s.at[0])
    for h in range(2):
        take(plane_out[h].at[pl.ds(0, 7)], w.plane_s.at[h])
        take(plane_ret[h].at[pl.ds(0, 7)], w.give_s.at[h])
    take(w.rows.at[pl.ds(1, 7)], w.ag_s.at[0])
    take(w.total.at[pl.ds(1, 7)], w.rs_s.at[0])
    take(w.half, w.half_s.at[0])
    take(w.partial.at[pl.ds(1, 7), :, pl.ds(0, 896)], w.red_s.at[0])
    take(w.straight_in.at[pl.ds(0, 7)], w.straight_s.at[0])
    settle()


BF, F32 = jnp.bfloat16, jnp.float32
SCRATCH = {
    "keys": ((5, KV + 16, 256), BF), "queries": ((1024, KV), BF), "query_doc": ((128, 128), F32), "top": ((1024, 128), F32),
    "sums": ((1024, 128), F32), "mixed": ((1024, LAT), F32), "value_up": ((8, LAT, 128), BF), "heads": ((8, 128, 1024), BF),
    "proj": ((896, 1024), BF), "proj_all": ((1024, 896), BF), "product": ((8, 128, 896), F32),
    "fold_out": ((8, 64, 896), BF), "fold_in": ((8, 64, 896), BF), "cross_out": ((8, 64, 896), BF),
    "cross_in": ((8, 3, 16, 896), BF), "direct_out": ((128, 896), BF), "direct_in": ((7, 16, 896), BF), "part_out": ((8, 16, 896), BF), "parts": ((8, 16, 896), BF), "stream": ((16, D), BF),
    "table": ((2, 16, 128), F32), "brief": ((8, 8, 128), F32), "column": ((256, 128), F32), "sel": ((256, 96), BF), "mix": ((192, 256), BF), "turn": ((640, 640), BF),
    "plane_sel": ((640, 256), BF), "plane_mix": ((512, 640), BF),
    "normed": ((16, D), BF), "pn": ((16, HALF), BF), "ps": ((16, HALF), BF), "tokens": ((8, 32, PLANE), BF),
    "xg": ((2, 96, GROUP), BF), "sg": ((2, 96, GROUP), BF), "plane_stream": ((32, PLANE), BF),
    "outbox": ((2, 8, 32, GROUP), BF), "inbox": ((2, 8, 32, GROUP), BF), "ret": ((2, 8, 32, GROUP), BF),
    "back": ((2, 8, 32, GROUP), BF), "plane_out0": ((8, 80, 896), BF), "plane_in0": ((8, 80, 896), BF),
    "plane_ret0": ((8, 80, 896), BF), "plane_back0": ((8, 80, 896), BF), "plane_out1": ((8, 80, 384), BF),
    "plane_in1": ((8, 80, 384), BF), "plane_ret1": ((8, 80, 384), BF), "plane_back1": ((8, 80, 384), BF),
    "straight_in": ((8, 32, 384), BF),
    "w_in": ((HALF, 512), BF), "w_down": ((256, HALF), BF), "rows": ((8, 80, RING), BF),
    "half": ((8, 80, 512), F32), "half_other": ((8, 80, 512), F32), "hidden": ((640, 256), BF), "total": ((8, 80, RING), BF),
    "arrived": ((2, PIECES, 4, 80, GROUP), BF), "partial": ((8, 32, PLANE), BF), "plane_own": ((32, PLANE), F32),
    "plane_arrived": ((2, 2, 4, 32, 512), BF), "ready": ((2, 16, HALF), BF), "landed": ((2, 16, HALF), BF),
    "load": ((2,), None), "chain_s": ((1,), None), "chain_r": ((4, 4), None), "share_s": ((1,), None), "share_r": ((5,), None),
    "proj_s": ((1,), None), "proj_r": ((1,), None), "head_s": ((1,), None), "head_r": ((2, 2, 4), None),
    "fold_s": ((1,), None), "fold_r": ((8,), None), "cross_s": ((1,), None), "cross_r": ((8,), None),
    "part_s": ((1,), None), "part_r": ((1,), None), "direct_s": ((1,), None), "direct_r": ((1,), None),
    "pair_s": ((6,), None), "pair_r": ((6,), None), "loc": ((3,), None), "table_s": ((1,), None), "table_r": ((1,), None),
    "box_s": ((1,), None), "box_r": ((2,), None), "relay_s": ((1,), None), "relay_r": ((2, 2, 4), None),
    "plane_s": ((2,), None), "plane_r": ((2,), None), "give_s": ((2,), None), "give_r": ((2,), None),
    "ag_s": ((1,), None), "ag_r": ((2, PIECES, 4), None), "half_s": ((1,), None), "half_r": ((3,), None),
    "rs_s": ((1,), None), "rs_r": ((2, PIECES, 4), None), "red_s": ((1,), None), "red_r": ((2, 2, 4), None),
    "straight_s": ((1,), None), "straight_r": ((1,), None), "back_s": ((1,), None), "back_r": ((2,), None),
    "fin_s": ((1,), None), "fin_r": ((1,), None),
}


def on_device(
    queries, latent_rows, doc_ids, value_up, out_proj, residual_in, norm_gain, expert_ids, gate_weights, gate_proj, up_proj,
    down_proj,
):
    vmem, any_space = pl.BlockSpec(memory_space=pltpu.VMEM), pl.BlockSpec(memory_space=pl.ANY)
    return pl.pallas_call(
        layer_kernel,
        out_shape=jax.ShapeDtypeStruct((16, D), BF),
        in_specs=[vmem] * 7 + [any_space] * 5,
        out_specs=vmem,
        scratch_shapes=[
            pltpu.SemaphoreType.DMA(shape) if kind is None else pltpu.VMEM(shape, kind) for shape, kind in SCRATCH.values()
        ],
        compiler_params=pltpu.CompilerParams(collective_id=1, has_side_effects=True, vmem_limit_bytes=60 << 20),
        cost_estimate=pl.CostEstimate(flops=8_000_000_000, bytes_accessed=10_000_000, transcendentals=2_000_000),
        name="layer",
    )(
        queries[0].transpose(1, 2, 0), latent_rows[0].T, doc_ids, expert_ids[0].T, gate_weights[0].T, residual_in[0], norm_gain,
        value_up[0], out_proj[0].T, gate_proj[0, 0], up_proj[0, 0], down_proj[0, 0],
    )[None]


def solution(mesh):
    return jax.shard_map(
        on_device,
        mesh=mesh,
        in_specs=(
            P("pipe", "ctx", "exp", None),
            P("pipe", "ctx", None),
            P("pipe", "ctx"),
            P("pipe", "exp", None, None),
            P("pipe", "exp", "ctx"),
            P("pipe", ("ctx", "exp"), None),
            P("pipe", None),
            P("pipe", ("ctx", "exp"), None),
            P("pipe", ("ctx", "exp"), None),
            P("pipe", "exp", None, "ctx"),
            P("pipe", "exp", None, "ctx"),
            P("pipe", "exp", "ctx", None),
        ),
        out_specs=P("pipe", ("ctx", "exp"), None),
        check_vma=False,
    )
```

```python
import math
import types

import jax
import jax.numpy as jnp
from jax import lax
from jax.experimental import pallas as pl
from jax.experimental.pallas import tpu as pltpu
from jax.sharding import PartitionSpec as P

D = 7168
HALF = D // 2
HD = 128
ROPE = 64
LAT = 512
KV = LAT + ROPE
MESH = pl.DeviceIdType.MESH

epsilon = 1e-06
masked_score = -1e30
score_scale = 1.0 / math.sqrt(HD + ROPE)
KEY_PIECES = ((0, 144), (144, 144), (288, 144), (432, 160))


def remote(src, dst, send_sem, recv_sem, **device):
    return pltpu.make_async_remote_copy(
        src_ref=src,
        dst_ref=dst,
        send_sem=send_sem,
        recv_sem=recv_sem,
        device_id=device,
        device_id_type=MESH,
    )


def take(ref, sem):
    pltpu.make_async_copy(ref, ref, sem).wait()


def meet(peers):
    barrier = pltpu.get_barrier_semaphore()
    for device in peers:
        pl.semaphore_signal(barrier, 1, device_id=device, device_id_type=MESH)
    pl.semaphore_wait(barrier, len(peers))


def squeeze_map(rows, groups, group, dtype=jnp.bfloat16):
    row = lax.broadcasted_iota(jnp.int32, (80, 8 * rows), 0).astype(jnp.float32)
    col = lax.broadcasted_iota(jnp.int32, (80, 8 * rows), 1).astype(jnp.float32)
    source = jnp.floor((row + 0.5) * 0.1)
    want = source * rows + (row - source * 10) + group * 10
    return jnp.where(col == want, 1.0, 0.0).astype(dtype)


def spread_map(rows, groups, group, dtype=jnp.bfloat16):
    row = lax.broadcasted_iota(jnp.int32, (8 * rows, 80), 0).astype(jnp.float32)
    col = lax.broadcasted_iota(jnp.int32, (8 * rows, 80), 1).astype(jnp.float32)
    source = jnp.floor((col + 0.5) * 0.1)
    want = source * rows + (col - source * 10) + group * 10
    return jnp.where(row == want, 1.0, 0.0).astype(dtype)


RING = 2304
GROUP = 384
PIECES = RING // GROUP
PLANE = HALF - RING
SHARES = ((0, 896), (896, 384))
HANDS = ((0, 3 * GROUP), (3 * GROUP, 3 * GROUP), (RING, 896), (RING + 896, 384))
SUMS = ((0, 512), (512, 384))


def reach(d, q):
    return 4 if q % 2 == d else 3


def attend(w, q_ref, lat_ref, doc_ref, vu_ref, op_ref, residual_ref, start_rest, make_tables):
    p, c, e = lax.axis_index("pipe"), lax.axis_index("ctx"), lax.axis_index("exp")
    k = lax.rem(c, 2)
    z = lax.div(c, 2)
    kk = 1 - k
    other = 2 * z + kk
    right = 2 * lax.rem(z + 1, 8) + k
    left = 2 * lax.rem(z + 7, 8) + k
    y = lax.div(e, 4)
    x = lax.rem(e, 4)
    bf, f32 = jnp.bfloat16, jnp.float32
    my_lanes = pl.ds(pl.multiple_of(k * 128, 128), 128)
    their_lanes = pl.ds(pl.multiple_of(kk * 128, 128), 128)
    my_columns = pl.ds(pl.multiple_of(k * 448, 16), 448)

    def chain(s, q):
        piece = pl.ds(*KEY_PIECES[q])
        return remote(
            w.keys.at[s - 1, piece, my_lanes], w.keys.at[s, piece, my_lanes], w.chain_s.at[0], w.chain_r.at[s - 1, q], ctx=right
        )

    def share(s):
        return remote(w.keys.at[s, :, my_lanes], w.keys.at[s, :, my_lanes], w.share_s.at[0], w.share_r.at[s], ctx=other)

    def share_in(s):
        return remote(w.keys.at[s, :, their_lanes], w.keys.at[s, :, their_lanes], w.share_s.at[0], w.share_r.at[s], ctx=other)

    for q in range(4):
        chain(1, q).start()
    share(0).start()
    own_proj = pltpu.make_async_copy(op_ref, w.proj.at[my_columns], w.load.at[1])
    own_proj.start()
    pair_proj = remote(op_ref, w.proj.at[my_columns], w.proj_s.at[0], w.proj_r.at[0], ctx=other)
    pair_proj.start()
    up_loads = [
        pltpu.make_async_copy(vu_ref.at[h], w.value_up.at[h], w.load.at[0]) for h in range(8)
    ]
    for copy in up_loads:
        copy.start()
    start_rest()

    for h in range(8):
        w.queries[h * 128 : (h + 1) * 128, :] = jnp.transpose(q_ref[h])
    w.top[...] = jnp.full((1024, 128), masked_score, f32)
    w.sums[...] = jnp.zeros((1024, 128), f32)
    w.mixed[...] = jnp.zeros((1024, LAT), f32)
    contract_last = (((1,), (1,)), ((), ()))
    query_pos = c * 128 + lax.broadcasted_iota(jnp.int32, (128, 256), 0)

    def attend_to(s):
        key_doc = w.keys[s, KV:, :].astype(f32)[0:1]
        key_pos = lax.rem(z + 8 - s, 8) * 256 + lax.broadcasted_iota(jnp.int32, (128, 256), 1)
        query_doc = jnp.concatenate([w.query_doc[...]] * 2, axis=1)
        hidden = jnp.where((key_pos <= query_pos) & (query_doc == key_doc), 0.0, masked_score)
        hidden = jnp.concatenate([hidden] * 4, axis=0)

        def some(j, carry):
            at = pl.ds(pl.multiple_of(j * 512, 512), 512)
            scores = jnp.dot(w.queries[at], w.keys[s, 0:KV, :], preferred_element_type=f32) * score_scale + hidden
            before = w.top[at]
            highest = jnp.maximum(before, jnp.max(scores, axis=1, keepdims=True))
            shrink = jnp.exp(before - highest)
            weights = jnp.exp(scores - jnp.concatenate([highest, highest], axis=1))
            w.top[at] = highest
            w.sums[at] = w.sums[at] * shrink + jnp.sum(weights, axis=1, keepdims=True)
            update = lax.dot_general(weights.astype(bf), w.keys[s, 0:LAT, :], contract_last, preferred_element_type=f32)
            w.mixed[at] = w.mixed[at] * jnp.concatenate([shrink] * 4, axis=1) + update
            return carry

        lax.fori_loop(0, 2, some, 0)

    def visit(s, carry):
        def pass_keys(pieces):
            for q in pieces:
                chain(s, q).wait_recv()

                @pl.when(s < 4)
                def _(q=q):
                    chain(s + 1, q).start()

        pass_keys((0, 1))
        share_in(s - 1).wait_recv()
        attend_to(s - 1)
        pass_keys((2, 3))
        share(s).start()
        return carry

    lax.fori_loop(1, 5, visit, 0)
    share_in(4).wait_recv()
    attend_to(4)

    take(w.value_up, w.load.at[0])

    def gather(d, q, r):
        piece = pl.ds(q * 64, 64)
        if d == 0:
            return remote(w.heads.at[r - 1, piece], w.heads.at[r, piece], w.head_s.at[0], w.head_r.at[d, q, r - 1], ctx=right)
        return remote(
            w.heads.at[lax.rem(9 - r, 8), piece], w.heads.at[8 - r, piece], w.head_s.at[0], w.head_r.at[d, q, r - 1], ctx=left
        )

    for h in range(8):
        at = slice(h * 128, (h + 1) * 128)
        latent_out = (w.mixed[at] / jnp.concatenate([w.sums[at]] * 4, axis=1)).astype(bf)
        w.heads[0, :, at] = jnp.dot(latent_out, w.value_up[h], preferred_element_type=f32).astype(bf)
    for q in range(2):
        for d in range(2):
            gather(d, q, 1).start()

    own_proj.wait()
    pair_proj.wait_recv()
    w.proj_all[...] = jnp.transpose(w.proj[...])

    y_mine = pl.multiple_of(y * 64, 64)
    y_theirs = pl.multiple_of((1 - y) * 64, 64)
    x_mine = pl.multiple_of(x * 16, 16)

    def fold(slot):
        return remote(w.fold_out.at[slot], w.fold_in.at[slot], w.fold_s.at[0], w.fold_r.at[slot], exp=lax.rem(e + 4, 8))

    def cross(slot, i):
        to = lax.rem(x + i, 4)
        return remote(
            w.cross_out.at[slot, pl.ds(pl.multiple_of(to * 16, 16), 16)], w.cross_in.at[slot, i - 1],
            w.cross_s.at[0], w.cross_r.at[slot], exp=4 * y + to,
        )

    def deliver(slot):
        return remote(
            w.part_out.at[slot], w.parts.at[z], w.part_s.at[0], w.part_r.at[0], ctx=2 * lax.rem(z + 8 - slot, 8) + k
        )

    def project(slot):
        w.product[slot] = jnp.dot(w.heads[slot], w.proj_all[...], preferred_element_type=f32)
        w.fold_out[slot] = w.product[slot, pl.ds(y_theirs, 64), :].astype(bf)
        fold(slot).start()

    def direct(i):
        to = lax.rem(e + i, 8)
        return remote(
            w.direct_out.at[pl.ds(pl.multiple_of(to * 16, 16), 16)], w.direct_in.at[i - 1], w.direct_s.at[0], w.direct_r.at[0], exp=to
        )

    def project_last():
        w.product[4] = jnp.dot(w.heads[4], w.proj_all[...], preferred_element_type=f32)
        w.direct_out[...] = w.product[4].astype(bf)
        for i in range(1, 8):
            direct(i).start()

    def sum_last():
        whole = w.product[4, pl.ds(pl.multiple_of(e * 16, 16), 16), :]
        take(w.direct_in, w.direct_r.at[0])
        for i in range(7):
            whole = whole + w.direct_in[i].astype(f32)
        w.part_out[4] = whole.astype(bf)
        deliver(4).start()

    def over_y(slot):
        fold(slot).wait_recv()
        both = w.product[slot, pl.ds(y_mine, 64), :] + w.fold_in[slot].astype(f32)
        w.product[slot, pl.ds(y_mine, 64), :] = both
        w.cross_out[slot] = both.astype(bf)
        for i in range(1, 4):
            cross(slot, i).start()

    def over_x(slot):
        whole = w.product[slot, pl.ds(pl.multiple_of(y_mine + x_mine, 16), 16), :]
        take(w.cross_in.at[slot], w.cross_r.at[slot])
        for i in range(3):
            whole = whole + w.cross_in[slot, i].astype(f32)
        w.part_out[slot] = whole.astype(bf)

        @pl.when(slot >= 1)
        def _():
            deliver(slot).start()

    def turn(r, carry):
        @pl.when((r >= 1) & (r <= 4))
        def _():
            for q in range(2):
                for d in range(2):
                    @pl.when(r <= reach(d, q))
                    def _(d=d, q=q):
                        gather(d, q, r).wait_recv()

                    @pl.when(r + 1 <= reach(d, q))
                    def _(d=d, q=q):
                        gather(d, q, r + 1).start()

        @pl.when(r == 4)
        def _():
            project_last()

        for stage, act in enumerate((project, over_y, over_x)):
            now = r - stage

            @pl.when((now >= 0) & (now <= 3))
            def _(act=act, now=now):
                act(now)

            @pl.when((now >= 1) & (now <= 3))
            def _(act=act, now=now):
                act(8 - now)

        @pl.when(r == 5)
        def _():
            sum_last()

        make_tables(r)
        return carry

    lax.fori_loop(0, 7, turn, 0)
    w.parts[pl.ds(z, 1)] = w.part_out[0:1]
    take(w.parts.at[pl.ds(0, 7)], w.part_r.at[0])
    for other_z in range(8):
        columns = slice(other_z * 896, (other_z + 1) * 896)
        w.stream[:, columns] = (residual_ref[:, columns].astype(f32) + w.parts[other_z].astype(f32)).astype(bf)

    def settle():
        pair_proj.wait_send()
        take(w.keys.at[pl.ds(1, 4), :, my_lanes], w.chain_s.at[0])
        take(w.keys.at[:, :, my_lanes], w.share_s.at[0])
        take(w.heads.at[pl.ds(1, 7)], w.head_s.at[0])
        take(w.fold_out.at[pl.ds(0, 7)], w.fold_s.at[0])
        take(w.cross_in.at[pl.ds(0, 7)], w.cross_s.at[0])
        take(w.part_out.at[pl.ds(0, 7)], w.part_s.at[0])
        take(w.direct_in, w.direct_s.at[0])

    return settle


def column_of(rows):
    diagonal = lax.broadcasted_iota(jnp.int32, rows.shape, 0) == lax.broadcasted_iota(jnp.int32, rows.shape, 1)
    return jnp.sum(jnp.where(diagonal, rows, 0.0), axis=1, keepdims=True)


def tables(w, ids_ref, weights_ref, k):
    f32 = jnp.float32
    ids = [column_of(jnp.broadcast_to(ids_ref[i : i + 1, :].astype(f32), (16, 16))) for i in range(2)]
    weights = [column_of(jnp.broadcast_to(weights_ref[i : i + 1, :], (16, 16))) for i in range(2)]
    lane = lax.broadcasted_iota(jnp.int32, (16, 128), 1)
    expert = lane.astype(f32)
    first, second = (jnp.where(ids[i] == expert, 1.0, 0.0) for i in range(2))
    earlier = lax.broadcasted_iota(jnp.int32, (16, 16), 1) < lax.broadcasted_iota(jnp.int32, (16, 16), 0)
    counts = jnp.dot(jnp.where(earlier, 1.0, 0.0), first + second, preferred_element_type=f32)
    ranks = (
        jnp.sum(first * counts, axis=1, keepdims=True),
        jnp.sum(second * (counts + first), axis=1, keepdims=True),
    )
    table = jnp.zeros((16, 128), f32)
    for i in range(2):
        table = jnp.where(lane == i, ids[i] * 8.0 + ranks[i], table)
        table = jnp.where(lane == i + 2, weights[i], table)
    w.table[pl.ds(k, 1)] = table[None]


def decode(shape, axis, groups, height):
    row = lax.broadcasted_iota(jnp.int32, shape, axis).astype(jnp.float32)
    expert = jnp.floor((row + 0.5) * (1.0 / height))
    inner = row - expert * height
    group = jnp.floor((inner + 0.5) * 0.1)
    within = inner - group * 10.0
    block = jnp.where(within >= 5.0, 1.0, 0.0)
    slot = jnp.where(group < groups, expert * 8.0 + within - block * 5.0, -1.0)
    return slot, group * 2.0 + block


def choose_matrix(columns, sel, groups, height):
    span, count = groups * 32, 8 * height
    lanes = jnp.transpose(columns)
    slot, owner = decode((count, 1), 0, groups, height)
    token = lax.shift_right_logical(lax.broadcasted_iota(jnp.int32, (count, span), 1), 4).astype(jnp.float32)
    hit = (owner == token) & ((slot == lanes[0:1, :span]) | (slot == lanes[1:2, :span]))
    sel[...] = jnp.where(hit, 1.0, 0.0).astype(jnp.bfloat16)


def weigh_matrix(columns, mix, groups, height):
    span, count = groups * 32, 8 * height
    slot, owner = decode((1, count), 1, groups, height)
    token = lax.shift_right_logical(lax.broadcasted_iota(jnp.int32, (span, count), 0), 4).astype(jnp.float32)
    slot = jnp.where(owner == token, slot, -1.0)
    weight = jnp.zeros((span, count), jnp.float32)
    for i in range(2):
        weight = weight + jnp.where(slot == columns[:span, i : i + 1], columns[:span, i + 2 : i + 3], 0.0)
    high = weight.astype(jnp.bfloat16)
    mix[0:span, :] = high
    mix[span : 2 * span, :] = (weight - high.astype(jnp.float32)).astype(jnp.bfloat16)


def layer_kernel(
    q_ref, lat_ref, doc_ref, ids_ref, weights_ref, residual_ref, gain_ref, vu_ref, op_ref, gate_ref, up_ref, down_ref,
    out_ref, *scratch
):
    w = types.SimpleNamespace(**dict(zip(SCRATCH, scratch, strict=True)))
    p, c, e = lax.axis_index("pipe"), lax.axis_index("ctx"), lax.axis_index("exp")
    k = lax.rem(c, 2)
    z = lax.div(c, 2)
    kk = 1 - k
    other = 2 * z + kk
    right = 2 * lax.rem(z + 1, 8) + k
    left = 2 * lax.rem(z + 7, 8) + k
    over = 1 - p
    mine = pl.multiple_of(k * HALF, 128)
    theirs = pl.multiple_of(kk * HALF, 128)
    my_lane = pl.multiple_of(k * 128, 128)
    up_lane = pl.multiple_of(256 + k * 128, 128)

    bf, f32 = jnp.bfloat16, jnp.float32

    w.keys[0, 0:KV, pl.ds(my_lane, 128)] = lat_ref[...]
    doc_row = jnp.broadcast_to(doc_ref[...].astype(f32), (128, 128))
    w.keys[0, KV:, pl.ds(my_lane, 128)] = doc_row[0:16].astype(bf)
    w.query_doc[...] = jnp.broadcast_to(column_of(doc_row), (128, 128))
    meet(
        [{"ctx": other}, {"pipe": over}, {"pipe": over, "ctx": other}, {"pipe": over, "exp": lax.rem(e + 4, 8)}]
        + [{"ctx": 2 * lax.rem(z + i, 8) + k} for i in range(1, 8)]
        + [{"exp": lax.rem(e + i, 8)} for i in range(1, 8)]
    )
    local = [
        pltpu.make_async_copy(gate_ref.at[pl.ds(mine, HALF), :], w.w_in.at[:, pl.ds(my_lane, 128)], w.loc.at[0]),
        pltpu.make_async_copy(up_ref.at[pl.ds(mine, HALF), :], w.w_in.at[:, pl.ds(up_lane, 128)], w.loc.at[1]),
        pltpu.make_async_copy(down_ref.at[:, pl.ds(mine, HALF)], w.w_down.at[pl.ds(my_lane, 128), :], w.loc.at[2]),
    ]
    pair = [
        remote(w.normed.at[:, pl.ds(theirs, HALF)], w.pn, w.pair_s.at[0], w.pair_r.at[0], ctx=other),
        remote(w.stream.at[:, pl.ds(theirs, HALF)], w.ps, w.pair_s.at[1], w.pair_r.at[1], ctx=other),
        remote(gate_ref.at[pl.ds(theirs, HALF), :], w.w_in.at[:, pl.ds(my_lane, 128)], w.pair_s.at[2], w.pair_r.at[2], ctx=other),
        remote(up_ref.at[pl.ds(theirs, HALF), :], w.w_in.at[:, pl.ds(up_lane, 128)], w.pair_s.at[3], w.pair_r.at[3], ctx=other),
        remote(down_ref.at[:, pl.ds(theirs, HALF)], w.w_down.at[pl.ds(my_lane, 128), :], w.pair_s.at[4], w.pair_r.at[4], ctx=other),
    ]
    pair.append(remote(w.table.at[k], w.table.at[k], w.pair_s.at[5], w.pair_r.at[5], ctx=other))

    def start_rest():
        tables(w, ids_ref, weights_ref, k)
        pair[5].start()
        for copy in local:
            copy.start()
        for copy in pair[2:5]:
            copy.start()

    def spread_table(i):
        return remote(w.brief.at[0], w.brief.at[i], w.table_s.at[0], w.table_r.at[0], ctx=2 * lax.rem(z + i, 8) + k)

    def chip_table():
        return jnp.concatenate([w.table[...].reshape(32, 128)] * 4, axis=0)

    def make_tables(r):
        @pl.when(r == 3)
        def _():
            pair[5].wait_recv()
            w.brief[0] = jnp.transpose(chip_table())[0:8]
            for i in range(1, 8):
                spread_table(i).start()

        @pl.when(r == 4)
        def _():
            choose_matrix(chip_table(), w.sel, 3, 32)

        @pl.when(r == 6)
        def _():
            take(w.brief.at[pl.ds(0, 7)], w.table_r.at[0])
            for i in range(8):
                w.column[i * 32 : (i + 1) * 32, :] = jnp.transpose(jnp.concatenate([w.brief[i]] * 16, axis=0))[0:32]
            choose_matrix(w.column[...], w.plane_sel, 8, 80)

    settle = attend(w, q_ref, lat_ref, doc_ref, vu_ref, op_ref, residual_ref, start_rest, make_tables)
    wide = w.stream[...].astype(f32)
    mean_square = jnp.mean(wide * wide, axis=1, keepdims=True)
    w.normed[...] = (wide * lax.rsqrt(mean_square + epsilon) * gain_ref[...]).astype(bf)
    for copy in pair[:2]:
        copy.start()

    def place(target, plane_target, source, start, core):
        for g in range(PIECES):
            lanes = pl.ds(start + g * GROUP if isinstance(start, int) else pl.multiple_of(start + g * GROUP, 128), GROUP)
            target[g // 3, pl.ds(pl.multiple_of(g % 3 * 32 + core * 16, 16), 16), :] = source[:, lanes]
        lanes = pl.ds(start + RING if isinstance(start, int) else pl.multiple_of(start + RING, 128), PLANE)
        plane_target[pl.ds(pl.multiple_of(core * 16, 16), 16), :] = source[:, lanes]

    place(w.xg, w.tokens.at[0], w.normed, mine, k)
    place(w.sg, w.plane_stream, w.stream, mine, k)
    pair[0].wait_recv()
    place(w.xg, w.tokens.at[0], w.pn, 0, kk)

    def relay(d, q, r):
        columns = pl.ds(q * (PLANE // 2), PLANE // 2)
        src, dst, to = (r - 1, r, right) if d == 0 else (lax.rem(9 - r, 8), 8 - r, left)
        return remote(w.tokens.at[src, :, columns], w.tokens.at[dst, :, columns], w.relay_s.at[0], w.relay_r.at[d, q, r - 1], ctx=to)

    def relay_round(r):
        for q in range(2):
            for d in range(2):
                if r <= reach(d, q):
                    relay(d, q, r).wait_recv()
                if r + 1 <= reach(d, q):
                    relay(d, q, r + 1).start()

    for q in range(2):
        for d in range(2):
            relay(d, q, 1).start()

    def box(part, i):
        to = lax.rem(e + i, 8)
        return remote(w.outbox.at[part, to], w.inbox.at[part, e], w.box_s.at[0], w.box_r.at[part], exp=to)

    for part in range(2):
        chosen = jnp.dot(w.sel[...], w.xg[part], preferred_element_type=f32).astype(bf)
        w.outbox[part] = chosen.reshape(8, 32, GROUP)
        for i in range(1, 8):
            box(part, i).start()
        w.inbox[part, pl.ds(e, 1)] = w.outbox[part, pl.ds(e, 1)]
    relay_round(1)

    def gather(d, q, r):
        columns = pl.ds(q * GROUP, GROUP)
        src, dst, to = (r - 1, r, right) if d == 0 else (lax.rem(9 - r, 8), 8 - r, left)
        return remote(w.rows.at[src, :, columns], w.rows.at[dst, :, columns], w.ag_s.at[0], w.ag_r.at[d, q, r - 1], ctx=to)

    for part in range(2):
        take(w.inbox.at[part, pl.ds(0, 7)], w.box_r.at[part])
        landed_rows = w.inbox[part].reshape(256, GROUP)
        for g in range(3):
            q = part * 3 + g
            w.rows[0, :, q * GROUP : (q + 1) * GROUP] = jnp.dot(
                squeeze_map(32, 3, g), landed_rows, preferred_element_type=f32
            ).astype(bf)
            for d in range(2):
                gather(d, q, 1).start()
        relay_round(2 + part)
    relay_round(4)

    plane_out, plane_in = (w.plane_out0, w.plane_out1), (w.plane_in0, w.plane_in1)
    plane_ret, plane_back = (w.plane_ret0, w.plane_ret1), (w.plane_back0, w.plane_back1)

    def plane_box(h, i):
        to = lax.rem(e + i, 8)
        return remote(plane_out[h].at[to], plane_in[h].at[e], w.plane_s.at[h], w.plane_r.at[h], exp=to)

    for h, (start, width) in enumerate(SHARES):
        tokens = w.tokens[:, :, start : start + width].reshape(256, width)
        chosen = jnp.dot(w.plane_sel[...], tokens, preferred_element_type=f32).astype(bf)
        plane_out[h][...] = chosen.reshape(8, 80, width)
        for i in range(1, 8):
            plane_box(h, i).start()
        plane_in[h][pl.ds(e, 1)] = plane_out[h][pl.ds(e, 1)]
    pair[1].wait_recv()
    place(w.sg, w.plane_stream, w.ps, 0, kk)
    for copy in local:
        copy.wait()
    for copy in pair[2:5]:
        copy.wait_recv()

    BATCHES = ((0, 4), (5, 3), (4, 1))

    def swap(n):
        slots = pl.ds(*BATCHES[n])
        return remote(w.half.at[slots], w.half_other.at[slots], w.half_s.at[0], w.half_r.at[n], ctx=other)

    def ring_half(slot):
        w.half[slot] = w.half[slot] + jnp.dot(w.rows[slot], w.w_in[0:RING, :], preferred_element_type=f32)

    def second_half(n):
        first, count = BATCHES[n]
        swap(n).wait_recv()
        slots = slice(first, first + count)
        both = (w.half[slots] + w.half_other[slots]).reshape(count * 80, 512)
        gate = both[:, :256]
        hidden = (gate / (1.0 + jnp.exp(-gate)) * both[:, 256:]).astype(bf)
        w.hidden[first * 80 : (first + count) * 80, :] = hidden
        for part in range(2):
            columns = slice(part * 3 * GROUP, (part + 1) * 3 * GROUP)
            out = jnp.dot(hidden, w.w_down[:, columns], preferred_element_type=f32).astype(bf)
            w.total[slots, :, columns] = out.reshape(count, 80, 3 * GROUP)

    def scatter(d, q, j):
        far = reach(d, q) + 1 - j
        slot, to = (far, left) if d == 0 else (8 - far, right)
        columns = pl.ds(q * GROUP, GROUP)
        return remote(w.total.at[slot, :, columns], w.arrived.at[d, q, j - 1], w.rs_s.at[0], w.rs_r.at[d, q, j - 1], ctx=to)

    w.half[...] = jnp.zeros((8, 80, 512), f32)
    ring_half(0)
    def turn_rows(slots):
        for slot in slots:
            w.turn[slot * 80 : (slot + 1) * 80, :] = squeeze_map(80, 8, slot)

    between = {
        (1, 0): lambda: turn_rows((0, 1, 2)),
        (1, 1): lambda: turn_rows((3, 4, 5)),
        (1, 2): lambda: turn_rows((6, 7)),
        (1, 3): lambda: weigh_matrix(chip_table(), w.mix, 3, 32),
        (2, 0): lambda: ring_half(1),
        (2, 1): lambda: ring_half(7),
        (2, 3): lambda: weigh_matrix(w.column[...], w.plane_mix, 8, 80),
        (3, 0): lambda: ring_half(2),
        (3, 1): lambda: ring_half(6),
    }
    for r in range(1, 5):
        for q in range(PIECES):
            for d in range(2):
                if r <= reach(d, q):
                    gather(d, q, r).wait_recv()
                if r + 1 <= reach(d, q):
                    gather(d, q, r + 1).start()
            if (r, q) in between:
                between[r, q]()
        if r == 4:
            ring_half(4)
        if r == 3:
            ring_half(3)
            ring_half(5)
            for h, (start, width) in enumerate(SHARES):
                take(plane_in[h].at[pl.ds(0, 7)], w.plane_r.at[h])
                turned = jnp.dot(w.turn[...], plane_in[h][...].reshape(640, width), preferred_element_type=f32).astype(bf)
                lanes = slice(RING + start, RING + start + width)
                more = jnp.dot(turned, w.w_in[lanes, :], preferred_element_type=f32)
                w.half[...] = w.half[...] + more.reshape(8, 80, 512)
            swap(0).start()
            swap(1).start()
            second_half(0)
            second_half(1)
            for q in range(PIECES):
                for d in range(2):
                    if reach(d, q) == 3:
                        scatter(d, q, 1).start()
    swap(2).start()
    second_half(2)

    def scatter_on(j):
        for q in range(PIECES):
            for d in range(2):
                if j + 1 <= reach(d, q):
                    far = reach(d, q) - j
                    slot = far if d == 0 else 8 - far
                    columns = slice(q * GROUP, (q + 1) * GROUP)
                    scatter(d, q, j).wait_recv()
                    w.total[slot, :, columns] = (
                        w.total[slot, :, columns].astype(f32) + w.arrived[d, q, j - 1].astype(f32)
                    ).astype(bf)
                    scatter(d, q, j + 1).start()

    for q in range(PIECES):
        for d in range(2):
            if reach(d, q) == 4:
                scatter(d, q, 1).start()

    def plane_give(h, i):
        to = lax.rem(e + i, 8)
        return remote(plane_ret[h].at[to], plane_back[h].at[e], w.give_s.at[h], w.give_r.at[h], exp=to)

    hidden = jnp.dot(w.turn[...], w.hidden[...], preferred_element_type=f32).astype(bf)
    for h, (start, width) in enumerate(SHARES):
        out = jnp.dot(hidden, w.w_down[:, RING + start : RING + start + width], preferred_element_type=f32).astype(bf)
        plane_ret[h][...] = out.reshape(8, 80, width)
        for i in range(1, 8):
            plane_give(h, i).start()
        plane_back[h][pl.ds(e, 1)] = plane_ret[h][pl.ds(e, 1)]

    def reduce(d, q, j):
        far = reach(d, q) + 1 - j
        slot, to = (far, left) if d == 0 else (8 - far, right)
        start, width = SUMS[q]
        return remote(
            w.partial.at[slot, :, pl.ds(start, width)], w.plane_arrived.at[d, q, j - 1, :, pl.ds(0, width)],
            w.red_s.at[0], w.red_r.at[d, q, j - 1], ctx=to,
        )

    def straight(slot):
        start, width = SHARES[1]
        return remote(
            w.partial.at[slot, :, pl.ds(start, width)], w.straight_in.at[slot], w.straight_s.at[0], w.straight_r.at[0],
            ctx=2 * lax.rem(z + 8 - slot, 8) + k,
        )

    def reduce_start(h):
        start, width = SHARES[h]
        take(plane_back[h].at[pl.ds(0, 7)], w.give_r.at[h])
        mixed = jnp.dot(w.plane_mix[...], plane_back[h][...].reshape(640, width), preferred_element_type=f32)
        mixed = mixed[:256] + mixed[256:]
        w.plane_own[:, start : start + width] = mixed[:32]
        w.partial[:, :, start : start + width] = mixed.astype(bf).reshape(8, 32, width)
        if h == 0:
            for q in range(2):
                for d in range(2):
                    reduce(d, q, 1).start()
        else:
            for slot in (4, 3, 5, 2, 6, 1, 7):
                straight(slot).start()

    def reduce_on(j):
        for q, (start, width) in enumerate(SUMS):
            for d in range(2):
                if j + 1 <= reach(d, q):
                    far = reach(d, q) - j
                    slot = far if d == 0 else 8 - far
                    columns = slice(start, start + width)
                    reduce(d, q, j).wait_recv()
                    w.partial[slot, :, columns] = (
                        w.partial[slot, :, columns].astype(f32) + w.plane_arrived[d, q, j - 1, :, 0:width].astype(f32)
                    ).astype(bf)
                    reduce(d, q, j + 1).start()

    def keep(whole, start, width):
        whole = whole.astype(bf)
        for b in range(2):
            w.ready[b, :, RING + start : RING + start + width] = whole[b * 16 : (b + 1) * 16]

    def reduce_end():
        for q, (start, width) in enumerate(SUMS):
            columns = slice(start, start + width)
            whole = w.plane_own[:, columns] + w.plane_stream[:, columns].astype(f32)
            for d in range(2):
                reduce(d, q, reach(d, q)).wait_recv()
                whole = whole + w.plane_arrived[d, q, reach(d, q) - 1, :, 0:width].astype(f32)
            keep(whole, start, width)
        hand(2)

    def straight_end():
        start, width = SHARES[1]
        columns = slice(start, start + width)
        whole = w.plane_own[:, columns] + w.plane_stream[:, columns].astype(f32)
        take(w.straight_in.at[pl.ds(0, 7)], w.straight_r.at[0])
        for slot in range(1, 8):
            whole = whole + w.straight_in[slot].astype(f32)
        keep(whole, start, width)
        hand(3)

    def give(part, i):
        to = lax.rem(e + i, 8)
        return remote(w.ret.at[part, to], w.back.at[part, e], w.back_s.at[0], w.back_r.at[part], exp=to)

    def send_back(part):
        spread = jnp.zeros((256, GROUP), f32)
        for g in range(3):
            q = part * 3 + g
            columns = slice(q * GROUP, (q + 1) * GROUP)
            whole = w.total[0, :, columns].astype(f32)
            for d in range(2):
                scatter(d, q, reach(d, q)).wait_recv()
                whole = whole + w.arrived[d, q, reach(d, q) - 1].astype(f32)
            spread = spread + jnp.dot(spread_map(32, 3, g), whole.astype(bf), preferred_element_type=f32)
        w.ret[part] = spread.astype(bf).reshape(8, 32, GROUP)
        for i in range(1, 8):
            give(part, i).start()
        w.back[part, pl.ds(e, 1)] = w.ret[part, pl.ds(e, 1)]

    y_low = lax.div(e, 4)
    before = {"pipe": jnp.where(y_low == 1, p, over), "exp": lax.rem(e + 4, 8)}

    def hand(part):
        start, width = HANDS[part]
        columns = pl.ds(start, width)
        remote(
            w.ready.at[kk, :, columns], w.landed.at[k, :, columns], w.fin_s.at[0], w.fin_r.at[0], pipe=over, ctx=other
        ).start()
        remote(w.ready.at[k, :, columns], w.transit.at[:, columns], w.fin_s.at[0], w.hop_r.at[part], **before).start()

    def hand_on(part):
        start, width = HANDS[part]
        columns = pl.ds(start, width)
        take(w.transit.at[:, columns], w.hop_r.at[part])
        remote(w.transit.at[:, columns], w.landed.at[k, :, columns], w.hop_s.at[0], w.fin_r.at[0], **before).start()

    def finish_ring(part):
        take(w.back.at[part, pl.ds(0, 7)], w.back_r.at[part])
        mixed = jnp.dot(w.mix[...], w.back[part].reshape(256, GROUP), preferred_element_type=f32)
        layer_out = (w.sg[part].astype(f32) + (mixed[:96] + mixed[96:])).astype(bf)
        for g in range(3):
            start = (part * 3 + g) * GROUP
            for b in range(2):
                w.ready[b, :, start : start + GROUP] = layer_out[g * 32 + b * 16 : g * 32 + b * 16 + 16]
        hand(part)

    scatter_on(1)
    scatter_on(2)
    reduce_start(0)
    scatter_on(3)
    reduce_on(1)
    send_back(0)
    send_back(1)
    reduce_on(2)
    reduce_start(1)
    reduce_on(3)
    finish_ring(0)
    reduce_end()
    hand_on(0)
    finish_ring(1)
    hand_on(2)
    straight_end()
    hand_on(1)
    hand_on(3)
    take(w.landed, w.fin_r.at[0])
    for b in range(2):
        out_ref[:, b * HALF : (b + 1) * HALF] = w.landed[b]

    take(w.ready, w.fin_s.at[0])
    take(w.transit, w.hop_s.at[0])
    for copy in pair:
        copy.wait_send()
    take(w.brief.at[pl.ds(0, 7)], w.table_s.at[0])
    take(w.tokens.at[pl.ds(1, 7)], w.relay_s.at[0])
    take(w.inbox.at[:, pl.ds(0, 7)], w.box_s.at[0])
    take(w.back.at[:, pl.ds(0, 7)], w.back_s.at[0])
    for h in range(2):
        take(plane_out[h].at[pl.ds(0, 7)], w.plane_s.at[h])
        take(plane_ret[h].at[pl.ds(0, 7)], w.give_s.at[h])
    take(w.rows.at[pl.ds(1, 7)], w.ag_s.at[0])
    take(w.total.at[pl.ds(1, 7)], w.rs_s.at[0])
    take(w.half, w.half_s.at[0])
    take(w.partial.at[pl.ds(1, 7), :, pl.ds(0, 896)], w.red_s.at[0])
    take(w.straight_in.at[pl.ds(0, 7)], w.straight_s.at[0])
    settle()


BF, F32 = jnp.bfloat16, jnp.float32
SCRATCH = {
    "keys": ((5, KV + 16, 256), BF), "queries": ((1024, KV), BF), "query_doc": ((128, 128), F32), "top": ((1024, 128), F32),
    "sums": ((1024, 128), F32), "mixed": ((1024, LAT), F32), "value_up": ((8, LAT, 128), BF), "heads": ((8, 128, 1024), BF),
    "proj": ((896, 1024), BF), "proj_all": ((1024, 896), BF), "product": ((8, 128, 896), F32),
    "fold_out": ((8, 64, 896), BF), "fold_in": ((8, 64, 896), BF), "cross_out": ((8, 64, 896), BF),
    "cross_in": ((8, 3, 16, 896), BF), "direct_out": ((128, 896), BF), "direct_in": ((7, 16, 896), BF), "part_out": ((8, 16, 896), BF), "parts": ((8, 16, 896), BF), "stream": ((16, D), BF),
    "table": ((2, 16, 128), F32), "brief": ((8, 8, 128), F32), "column": ((256, 128), F32), "sel": ((256, 96), BF), "mix": ((192, 256), BF), "turn": ((640, 640), BF),
    "plane_sel": ((640, 256), BF), "plane_mix": ((512, 640), BF),
    "normed": ((16, D), BF), "pn": ((16, HALF), BF), "ps": ((16, HALF), BF), "tokens": ((8, 32, PLANE), BF),
    "xg": ((2, 96, GROUP), BF), "sg": ((2, 96, GROUP), BF), "plane_stream": ((32, PLANE), BF),
    "outbox": ((2, 8, 32, GROUP), BF), "inbox": ((2, 8, 32, GROUP), BF), "ret": ((2, 8, 32, GROUP), BF),
    "back": ((2, 8, 32, GROUP), BF), "plane_out0": ((8, 80, 896), BF), "plane_in0": ((8, 80, 896), BF),
    "plane_ret0": ((8, 80, 896), BF), "plane_back0": ((8, 80, 896), BF), "plane_out1": ((8, 80, 384), BF),
    "plane_in1": ((8, 80, 384), BF), "plane_ret1": ((8, 80, 384), BF), "plane_back1": ((8, 80, 384), BF),
    "straight_in": ((8, 32, 384), BF),
    "w_in": ((HALF, 512), BF), "w_down": ((256, HALF), BF), "rows": ((8, 80, RING), BF),
    "half": ((8, 80, 512), F32), "half_other": ((8, 80, 512), F32), "hidden": ((640, 256), BF), "total": ((8, 80, RING), BF),
    "arrived": ((2, PIECES, 4, 80, GROUP), BF), "partial": ((8, 32, PLANE), BF), "plane_own": ((32, PLANE), F32),
    "plane_arrived": ((2, 2, 4, 32, 512), BF), "ready": ((2, 16, HALF), BF), "landed": ((2, 16, HALF), BF), "transit": ((16, HALF), BF),
    "load": ((2,), None), "chain_s": ((1,), None), "chain_r": ((4, 4), None), "share_s": ((1,), None), "share_r": ((5,), None),
    "proj_s": ((1,), None), "proj_r": ((1,), None), "head_s": ((1,), None), "head_r": ((2, 2, 4), None),
    "fold_s": ((1,), None), "fold_r": ((8,), None), "cross_s": ((1,), None), "cross_r": ((8,), None),
    "part_s": ((1,), None), "part_r": ((1,), None), "direct_s": ((1,), None), "direct_r": ((1,), None),
    "pair_s": ((6,), None), "pair_r": ((6,), None), "loc": ((3,), None), "table_s": ((1,), None), "table_r": ((1,), None),
    "box_s": ((1,), None), "box_r": ((2,), None), "relay_s": ((1,), None), "relay_r": ((2, 2, 4), None),
    "plane_s": ((2,), None), "plane_r": ((2,), None), "give_s": ((2,), None), "give_r": ((2,), None),
    "ag_s": ((1,), None), "ag_r": ((2, PIECES, 4), None), "half_s": ((1,), None), "half_r": ((3,), None),
    "rs_s": ((1,), None), "rs_r": ((2, PIECES, 4), None), "red_s": ((1,), None), "red_r": ((2, 2, 4), None),
    "straight_s": ((1,), None), "straight_r": ((1,), None), "back_s": ((1,), None), "back_r": ((2,), None),
    "fin_s": ((1,), None), "fin_r": ((1,), None), "hop_s": ((1,), None), "hop_r": ((4,), None),
}


def on_device(
    queries, latent_rows, doc_ids, value_up, out_proj, residual_in, norm_gain, expert_ids, gate_weights, gate_proj, up_proj,
    down_proj,
):
    vmem, any_space = pl.BlockSpec(memory_space=pltpu.VMEM), pl.BlockSpec(memory_space=pl.ANY)
    return pl.pallas_call(
        layer_kernel,
        out_shape=jax.ShapeDtypeStruct((16, D), BF),
        in_specs=[vmem] * 7 + [any_space] * 5,
        out_specs=vmem,
        scratch_shapes=[
            pltpu.SemaphoreType.DMA(shape) if kind is None else pltpu.VMEM(shape, kind) for shape, kind in SCRATCH.values()
        ],
        compiler_params=pltpu.CompilerParams(collective_id=1, has_side_effects=True, vmem_limit_bytes=60 << 20),
        cost_estimate=pl.CostEstimate(flops=8_000_000_000, bytes_accessed=10_000_000, transcendentals=2_000_000),
        name="layer",
    )(
        queries[0].transpose(1, 2, 0), latent_rows[0].T, doc_ids, expert_ids[0].T, gate_weights[0].T, residual_in[0], norm_gain,
        value_up[0], out_proj[0].T, gate_proj[0, 0], up_proj[0, 0], down_proj[0, 0],
    )[None]


def solution(mesh):
    return jax.shard_map(
        on_device,
        mesh=mesh,
        in_specs=(
            P("pipe", "ctx", "exp", None),
            P("pipe", "ctx", None),
            P("pipe", "ctx"),
            P("pipe", "exp", None, None),
            P("pipe", "exp", "ctx"),
            P("pipe", ("ctx", "exp"), None),
            P("pipe", None),
            P("pipe", ("ctx", "exp"), None),
            P("pipe", ("ctx", "exp"), None),
            P("pipe", "exp", None, "ctx"),
            P("pipe", "exp", None, "ctx"),
            P("pipe", "exp", "ctx", None),
        ),
        out_specs=P("pipe", ("ctx", "exp"), None),
        check_vma=False,
    )
```

```python
import math
import types

import jax
import jax.numpy as jnp
from jax import lax
from jax.experimental import pallas as pl
from jax.experimental.pallas import tpu as pltpu
from jax.sharding import PartitionSpec as P

D = 7168
HALF = D // 2
HD = 128
ROPE = 64
LAT = 512
KV = LAT + ROPE
MESH = pl.DeviceIdType.MESH

epsilon = 1e-06
masked_score = -1e30
score_scale = 1.0 / math.sqrt(HD + ROPE)
KEY_PIECES = ((0, 144), (144, 144), (288, 144), (432, 160))


def remote(src, dst, send_sem, recv_sem, **device):
    return pltpu.make_async_remote_copy(
        src_ref=src,
        dst_ref=dst,
        send_sem=send_sem,
        recv_sem=recv_sem,
        device_id=device,
        device_id_type=MESH,
    )


def take(ref, sem):
    pltpu.make_async_copy(ref, ref, sem).wait()


def meet(peers):
    barrier = pltpu.get_barrier_semaphore()
    for device in peers:
        pl.semaphore_signal(barrier, 1, device_id=device, device_id_type=MESH)
    pl.semaphore_wait(barrier, len(peers))


def squeeze_map(rows, groups, group, dtype=jnp.bfloat16):
    row = lax.broadcasted_iota(jnp.int32, (80, 8 * rows), 0).astype(jnp.float32)
    col = lax.broadcasted_iota(jnp.int32, (80, 8 * rows), 1).astype(jnp.float32)
    source = jnp.floor((row + 0.5) * 0.1)
    want = source * rows + (row - source * 10) + group * 10
    return jnp.where(col == want, 1.0, 0.0).astype(dtype)


def spread_map(rows, groups, group, dtype=jnp.bfloat16):
    row = lax.broadcasted_iota(jnp.int32, (8 * rows, 80), 0).astype(jnp.float32)
    col = lax.broadcasted_iota(jnp.int32, (8 * rows, 80), 1).astype(jnp.float32)
    source = jnp.floor((col + 0.5) * 0.1)
    want = source * rows + (col - source * 10) + group * 10
    return jnp.where(row == want, 1.0, 0.0).astype(dtype)


RING = 2304
GROUP = 384
PIECES = RING // GROUP
PLANE = HALF - RING
SHARES = ((0, 896), (896, 384))
HANDS = ((0, 3 * GROUP), (3 * GROUP, 3 * GROUP), (RING, 896), (RING + 896, 384))
SUMS = ((0, 512), (512, 384))


def reach(d, q):
    return 4 if q % 2 == d else 3


def attend(w, q_ref, lat_ref, doc_ref, vu_ref, op_ref, residual_ref, start_rest, make_tables):
    p, c, e = lax.axis_index("pipe"), lax.axis_index("ctx"), lax.axis_index("exp")
    k = lax.rem(c, 2)
    z = lax.div(c, 2)
    kk = 1 - k
    other = 2 * z + kk
    right = 2 * lax.rem(z + 1, 8) + k
    left = 2 * lax.rem(z + 7, 8) + k
    y = lax.div(e, 4)
    x = lax.rem(e, 4)
    bf, f32 = jnp.bfloat16, jnp.float32
    my_lanes = pl.ds(pl.multiple_of(k * 128, 128), 128)
    their_lanes = pl.ds(pl.multiple_of(kk * 128, 128), 128)
    my_columns = pl.ds(pl.multiple_of(k * 448, 16), 448)

    def chain(s, q):
        piece = pl.ds(*KEY_PIECES[q])
        return remote(
            w.keys.at[s - 1, piece, my_lanes], w.keys.at[s, piece, my_lanes], w.chain_s.at[0], w.chain_r.at[s - 1, q], ctx=right
        )

    def share(s):
        return remote(w.keys.at[s, :, my_lanes], w.keys.at[s, :, my_lanes], w.share_s.at[0], w.share_r.at[s], ctx=other)

    def share_in(s):
        return remote(w.keys.at[s, :, their_lanes], w.keys.at[s, :, their_lanes], w.share_s.at[0], w.share_r.at[s], ctx=other)

    for q in range(4):
        chain(1, q).start()
    share(0).start()
    own_proj = pltpu.make_async_copy(op_ref, w.proj.at[my_columns], w.load.at[1])
    own_proj.start()
    pair_proj = remote(op_ref, w.proj.at[my_columns], w.proj_s.at[0], w.proj_r.at[0], ctx=other)
    pair_proj.start()
    up_loads = [
        pltpu.make_async_copy(vu_ref.at[h], w.value_up.at[h], w.load.at[0]) for h in range(8)
    ]
    for copy in up_loads:
        copy.start()
    start_rest()

    for h in range(8):
        w.queries[h * 128 : (h + 1) * 128, :] = jnp.transpose(q_ref[h])
    w.top[...] = jnp.full((1024, 128), masked_score, f32)
    w.sums[...] = jnp.zeros((1024, 128), f32)
    w.mixed[...] = jnp.zeros((1024, LAT), f32)
    contract_last = (((1,), (1,)), ((), ()))
    query_pos = c * 128 + lax.broadcasted_iota(jnp.int32, (128, 256), 0)

    def attend_to(s):
        key_doc = w.keys[s, KV:, :].astype(f32)[0:1]
        key_pos = lax.rem(z + 8 - s, 8) * 256 + lax.broadcasted_iota(jnp.int32, (128, 256), 1)
        query_doc = jnp.concatenate([w.query_doc[...]] * 2, axis=1)
        hidden = jnp.where((key_pos <= query_pos) & (query_doc == key_doc), 0.0, masked_score)
        hidden = jnp.concatenate([hidden] * 4, axis=0)

        def some(j, carry):
            at = pl.ds(pl.multiple_of(j * 512, 512), 512)
            scores = jnp.dot(w.queries[at], w.keys[s, 0:KV, :], preferred_element_type=f32) * score_scale + hidden
            before = w.top[at]
            highest = jnp.maximum(before, jnp.max(scores, axis=1, keepdims=True))
            shrink = jnp.exp(before - highest)
            weights = jnp.exp(scores - jnp.concatenate([highest, highest], axis=1))
            w.top[at] = highest
            w.sums[at] = w.sums[at] * shrink + jnp.sum(weights, axis=1, keepdims=True)
            update = lax.dot_general(weights.astype(bf), w.keys[s, 0:LAT, :], contract_last, preferred_element_type=f32)
            w.mixed[at] = w.mixed[at] * jnp.concatenate([shrink] * 4, axis=1) + update
            return carry

        lax.fori_loop(0, 2, some, 0)

    def visit(s, carry):
        def pass_keys(pieces):
            for q in pieces:
                chain(s, q).wait_recv()

                @pl.when(s < 4)
                def _(q=q):
                    chain(s + 1, q).start()

        pass_keys((0, 1))
        share_in(s - 1).wait_recv()
        attend_to(s - 1)
        pass_keys((2, 3))
        share(s).start()
        return carry

    lax.fori_loop(1, 5, visit, 0)
    share_in(4).wait_recv()
    attend_to(4)

    take(w.value_up, w.load.at[0])

    def gather(d, q, r):
        piece = pl.ds(q * 64, 64)
        if d == 0:
            return remote(w.heads.at[r - 1, piece], w.heads.at[r, piece], w.head_s.at[0], w.head_r.at[d, q, r - 1], ctx=right)
        return remote(
            w.heads.at[lax.rem(9 - r, 8), piece], w.heads.at[8 - r, piece], w.head_s.at[0], w.head_r.at[d, q, r - 1], ctx=left
        )

    for h in range(8):
        at = slice(h * 128, (h + 1) * 128)
        latent_out = (w.mixed[at] / jnp.concatenate([w.sums[at]] * 4, axis=1)).astype(bf)
        w.heads[0, :, at] = jnp.dot(latent_out, w.value_up[h], preferred_element_type=f32).astype(bf)
    for q in range(2):
        for d in range(2):
            gather(d, q, 1).start()

    own_proj.wait()
    pair_proj.wait_recv()
    w.proj_all[...] = jnp.transpose(w.proj[...])

    y_mine = pl.multiple_of(y * 64, 64)
    y_theirs = pl.multiple_of((1 - y) * 64, 64)
    x_mine = pl.multiple_of(x * 16, 16)

    def fold(slot):
        return remote(w.fold_out.at[slot], w.fold_in.at[slot], w.fold_s.at[0], w.fold_r.at[slot], exp=lax.rem(e + 4, 8))

    def cross(slot, i):
        to = lax.rem(x + i, 4)
        return remote(
            w.cross_out.at[slot, pl.ds(pl.multiple_of(to * 16, 16), 16)], w.cross_in.at[slot, i - 1],
            w.cross_s.at[0], w.cross_r.at[slot], exp=4 * y + to,
        )

    def deliver(slot):
        return remote(
            w.part_out.at[slot], w.parts.at[z], w.part_s.at[0], w.part_r.at[0], ctx=2 * lax.rem(z + 8 - slot, 8) + k
        )

    def project(slot):
        w.product[slot] = jnp.dot(w.heads[slot], w.proj_all[...], preferred_element_type=f32)
        w.fold_out[slot] = w.product[slot, pl.ds(y_theirs, 64), :].astype(bf)
        fold(slot).start()

    def direct(i):
        to = lax.rem(e + i, 8)
        return remote(
            w.direct_out.at[pl.ds(pl.multiple_of(to * 16, 16), 16)], w.direct_in.at[i - 1], w.direct_s.at[0], w.direct_r.at[0], exp=to
        )

    def project_last():
        w.product[4] = jnp.dot(w.heads[4], w.proj_all[...], preferred_element_type=f32)
        w.direct_out[...] = w.product[4].astype(bf)
        for i in range(1, 8):
            direct(i).start()

    def sum_last():
        whole = w.product[4, pl.ds(pl.multiple_of(e * 16, 16), 16), :]
        take(w.direct_in, w.direct_r.at[0])
        for i in range(7):
            whole = whole + w.direct_in[i].astype(f32)
        w.part_out[4] = whole.astype(bf)
        deliver(4).start()

    def over_y(slot):
        fold(slot).wait_recv()
        both = w.product[slot, pl.ds(y_mine, 64), :] + w.fold_in[slot].astype(f32)
        w.product[slot, pl.ds(y_mine, 64), :] = both
        w.cross_out[slot] = both.astype(bf)
        for i in range(1, 4):
            cross(slot, i).start()

    def over_x(slot):
        whole = w.product[slot, pl.ds(pl.multiple_of(y_mine + x_mine, 16), 16), :]
        take(w.cross_in.at[slot], w.cross_r.at[slot])
        for i in range(3):
            whole = whole + w.cross_in[slot, i].astype(f32)
        w.part_out[slot] = whole.astype(bf)

        @pl.when(slot >= 1)
        def _():
            deliver(slot).start()

    def turn(r, carry):
        @pl.when((r >= 1) & (r <= 4))
        def _():
            for q in range(2):
                for d in range(2):
                    @pl.when(r <= reach(d, q))
                    def _(d=d, q=q):
                        gather(d, q, r).wait_recv()

                    @pl.when(r + 1 <= reach(d, q))
                    def _(d=d, q=q):
                        gather(d, q, r + 1).start()

        @pl.when(r == 4)
        def _():
            project_last()

        for stage, act in enumerate((project, over_y, over_x)):
            now = r - stage

            @pl.when((now >= 0) & (now <= 3))
            def _(act=act, now=now):
                act(now)

            @pl.when((now >= 1) & (now <= 3))
            def _(act=act, now=now):
                act(8 - now)

        @pl.when(r == 5)
        def _():
            sum_last()

        make_tables(r)
        return carry

    lax.fori_loop(0, 7, turn, 0)
    w.parts[pl.ds(z, 1)] = w.part_out[0:1]
    take(w.parts.at[pl.ds(0, 7)], w.part_r.at[0])
    for other_z in range(8):
        columns = slice(other_z * 896, (other_z + 1) * 896)
        w.stream[:, columns] = (residual_ref[:, columns].astype(f32) + w.parts[other_z].astype(f32)).astype(bf)

    def settle():
        pair_proj.wait_send()
        take(w.keys.at[pl.ds(1, 4), :, my_lanes], w.chain_s.at[0])
        take(w.keys.at[:, :, my_lanes], w.share_s.at[0])
        take(w.heads.at[pl.ds(1, 7)], w.head_s.at[0])
        take(w.fold_out.at[pl.ds(0, 7)], w.fold_s.at[0])
        take(w.cross_in.at[pl.ds(0, 7)], w.cross_s.at[0])
        take(w.part_out.at[pl.ds(0, 7)], w.part_s.at[0])
        take(w.direct_in, w.direct_s.at[0])

    return settle


def column_of(rows):
    diagonal = lax.broadcasted_iota(jnp.int32, rows.shape, 0) == lax.broadcasted_iota(jnp.int32, rows.shape, 1)
    return jnp.sum(jnp.where(diagonal, rows, 0.0), axis=1, keepdims=True)


def tables(w, ids_ref, weights_ref, k):
    f32 = jnp.float32
    ids = [column_of(jnp.broadcast_to(ids_ref[i : i + 1, :].astype(f32), (16, 16))) for i in range(2)]
    weights = [column_of(jnp.broadcast_to(weights_ref[i : i + 1, :], (16, 16))) for i in range(2)]
    lane = lax.broadcasted_iota(jnp.int32, (16, 128), 1)
    expert = lane.astype(f32)
    first, second = (jnp.where(ids[i] == expert, 1.0, 0.0) for i in range(2))
    earlier = lax.broadcasted_iota(jnp.int32, (16, 16), 1) < lax.broadcasted_iota(jnp.int32, (16, 16), 0)
    counts = jnp.dot(jnp.where(earlier, 1.0, 0.0), first + second, preferred_element_type=f32)
    ranks = (
        jnp.sum(first * counts, axis=1, keepdims=True),
        jnp.sum(second * (counts + first), axis=1, keepdims=True),
    )
    table = jnp.zeros((16, 128), f32)
    for i in range(2):
        table = jnp.where(lane == i, ids[i] * 8.0 + ranks[i], table)
        table = jnp.where(lane == i + 2, weights[i], table)
    w.table[pl.ds(k, 1)] = table[None]


def decode(shape, axis, groups, height):
    row = lax.broadcasted_iota(jnp.int32, shape, axis).astype(jnp.float32)
    expert = jnp.floor((row + 0.5) * (1.0 / height))
    inner = row - expert * height
    group = jnp.floor((inner + 0.5) * 0.1)
    within = inner - group * 10.0
    block = jnp.where(within >= 5.0, 1.0, 0.0)
    slot = jnp.where(group < groups, expert * 8.0 + within - block * 5.0, -1.0)
    return slot, group * 2.0 + block


def choose_matrix(columns, sel, groups, height):
    span, count = groups * 32, 8 * height
    lanes = jnp.transpose(columns)
    slot, owner = decode((count, 1), 0, groups, height)
    token = lax.shift_right_logical(lax.broadcasted_iota(jnp.int32, (count, span), 1), 4).astype(jnp.float32)
    hit = (owner == token) & ((slot == lanes[0:1, :span]) | (slot == lanes[1:2, :span]))
    sel[...] = jnp.where(hit, 1.0, 0.0).astype(jnp.bfloat16)


def weigh_matrix(columns, mix, groups, height):
    span, count = groups * 32, 8 * height
    slot, owner = decode((1, count), 1, groups, height)
    token = lax.shift_right_logical(lax.broadcasted_iota(jnp.int32, (span, count), 0), 4).astype(jnp.float32)
    slot = jnp.where(owner == token, slot, -1.0)
    weight = jnp.zeros((span, count), jnp.float32)
    for i in range(2):
        weight = weight + jnp.where(slot == columns[:span, i : i + 1], columns[:span, i + 2 : i + 3], 0.0)
    high = weight.astype(jnp.bfloat16)
    mix[0:span, :] = high
    mix[span : 2 * span, :] = (weight - high.astype(jnp.float32)).astype(jnp.bfloat16)


def layer_kernel(
    q_ref, lat_ref, doc_ref, ids_ref, weights_ref, residual_ref, gain_ref, vu_ref, op_ref, gate_ref, up_ref, down_ref,
    out_ref, *scratch
):
    w = types.SimpleNamespace(**dict(zip(SCRATCH, scratch, strict=True)))
    p, c, e = lax.axis_index("pipe"), lax.axis_index("ctx"), lax.axis_index("exp")
    k = lax.rem(c, 2)
    z = lax.div(c, 2)
    kk = 1 - k
    other = 2 * z + kk
    right = 2 * lax.rem(z + 1, 8) + k
    left = 2 * lax.rem(z + 7, 8) + k
    over = 1 - p
    mine = pl.multiple_of(k * HALF, 128)
    theirs = pl.multiple_of(kk * HALF, 128)
    my_lane = pl.multiple_of(k * 128, 128)
    up_lane = pl.multiple_of(256 + k * 128, 128)

    bf, f32 = jnp.bfloat16, jnp.float32

    w.keys[0, 0:KV, pl.ds(my_lane, 128)] = lat_ref[...]
    doc_row = jnp.broadcast_to(doc_ref[...].astype(f32), (128, 128))
    w.keys[0, KV:, pl.ds(my_lane, 128)] = doc_row[0:16].astype(bf)
    w.query_doc[...] = jnp.broadcast_to(column_of(doc_row), (128, 128))
    meet(
        [{"ctx": other}, {"pipe": over}, {"pipe": over, "ctx": other}]
        + [{"ctx": 2 * lax.rem(z + i, 8) + k} for i in range(1, 8)]
        + [{"exp": lax.rem(e + i, 8)} for i in range(1, 8)]
    )
    local = [
        pltpu.make_async_copy(gate_ref.at[pl.ds(mine, HALF), :], w.w_in.at[:, pl.ds(my_lane, 128)], w.loc.at[0]),
        pltpu.make_async_copy(up_ref.at[pl.ds(mine, HALF), :], w.w_in.at[:, pl.ds(up_lane, 128)], w.loc.at[1]),
        pltpu.make_async_copy(down_ref.at[:, pl.ds(mine, HALF)], w.w_down.at[pl.ds(my_lane, 128), :], w.loc.at[2]),
    ]
    pair = [
        remote(w.normed.at[:, pl.ds(theirs, HALF)], w.pn, w.pair_s.at[0], w.pair_r.at[0], ctx=other),
        remote(w.stream.at[:, pl.ds(theirs, HALF)], w.ps, w.pair_s.at[1], w.pair_r.at[1], ctx=other),
        remote(gate_ref.at[pl.ds(theirs, HALF), :], w.w_in.at[:, pl.ds(my_lane, 128)], w.pair_s.at[2], w.pair_r.at[2], ctx=other),
        remote(up_ref.at[pl.ds(theirs, HALF), :], w.w_in.at[:, pl.ds(up_lane, 128)], w.pair_s.at[3], w.pair_r.at[3], ctx=other),
        remote(down_ref.at[:, pl.ds(theirs, HALF)], w.w_down.at[pl.ds(my_lane, 128), :], w.pair_s.at[4], w.pair_r.at[4], ctx=other),
    ]
    pair.append(remote(w.table.at[k], w.table.at[k], w.pair_s.at[5], w.pair_r.at[5], ctx=other))

    def start_rest():
        tables(w, ids_ref, weights_ref, k)
        pair[5].start()
        for copy in local:
            copy.start()
        for copy in pair[2:5]:
            copy.start()

    def spread_table(i):
        return remote(w.brief.at[0], w.brief.at[i], w.table_s.at[0], w.table_r.at[0], ctx=2 * lax.rem(z + i, 8) + k)

    def chip_table():
        return jnp.concatenate([w.table[...].reshape(32, 128)] * 4, axis=0)

    def make_tables(r):
        @pl.when(r == 3)
        def _():
            pair[5].wait_recv()
            w.brief[0] = jnp.transpose(chip_table())[0:8]
            for i in range(1, 8):
                spread_table(i).start()

        @pl.when(r == 4)
        def _():
            choose_matrix(chip_table(), w.sel, 3, 32)

        @pl.when(r == 6)
        def _():
            take(w.brief.at[pl.ds(0, 7)], w.table_r.at[0])
            for i in range(8):
                w.column[i * 32 : (i + 1) * 32, :] = jnp.transpose(jnp.concatenate([w.brief[i]] * 16, axis=0))[0:32]
            choose_matrix(w.column[...], w.plane_sel, 8, 80)

    settle = attend(w, q_ref, lat_ref, doc_ref, vu_ref, op_ref, residual_ref, start_rest, make_tables)
    wide = w.stream[...].astype(f32)
    mean_square = jnp.mean(wide * wide, axis=1, keepdims=True)
    w.normed[...] = (wide * lax.rsqrt(mean_square + epsilon) * gain_ref[...]).astype(bf)
    for copy in pair[:2]:
        copy.start()

    def place(target, plane_target, source, start, core):
        for g in range(PIECES):
            lanes = pl.ds(start + g * GROUP if isinstance(start, int) else pl.multiple_of(start + g * GROUP, 128), GROUP)
            target[g // 3, pl.ds(pl.multiple_of(g % 3 * 32 + core * 16, 16), 16), :] = source[:, lanes]
        lanes = pl.ds(start + RING if isinstance(start, int) else pl.multiple_of(start + RING, 128), PLANE)
        plane_target[pl.ds(pl.multiple_of(core * 16, 16), 16), :] = source[:, lanes]

    place(w.xg, w.tokens.at[0], w.normed, mine, k)
    place(w.sg, w.plane_stream, w.stream, mine, k)
    pair[0].wait_recv()
    place(w.xg, w.tokens.at[0], w.pn, 0, kk)

    def relay(d, q, r):
        columns = pl.ds(q * (PLANE // 2), PLANE // 2)
        src, dst, to = (r - 1, r, right) if d == 0 else (lax.rem(9 - r, 8), 8 - r, left)
        return remote(w.tokens.at[src, :, columns], w.tokens.at[dst, :, columns], w.relay_s.at[0], w.relay_r.at[d, q, r - 1], ctx=to)

    def relay_round(r):
        for q in range(2):
            for d in range(2):
                if r <= reach(d, q):
                    relay(d, q, r).wait_recv()
                if r + 1 <= reach(d, q):
                    relay(d, q, r + 1).start()

    for q in range(2):
        for d in range(2):
            relay(d, q, 1).start()

    def box(part, i):
        to = lax.rem(e + i, 8)
        return remote(w.outbox.at[part, to], w.inbox.at[part, e], w.box_s.at[0], w.box_r.at[part], exp=to)

    for part in range(2):
        chosen = jnp.dot(w.sel[...], w.xg[part], preferred_element_type=f32).astype(bf)
        w.outbox[part] = chosen.reshape(8, 32, GROUP)
        for i in range(1, 8):
            box(part, i).start()
        w.inbox[part, pl.ds(e, 1)] = w.outbox[part, pl.ds(e, 1)]
    relay_round(1)

    def gather(d, q, r):
        columns = pl.ds(q * GROUP, GROUP)
        src, dst, to = (r - 1, r, right) if d == 0 else (lax.rem(9 - r, 8), 8 - r, left)
        return remote(w.rows.at[src, :, columns], w.rows.at[dst, :, columns], w.ag_s.at[0], w.ag_r.at[d, q, r - 1], ctx=to)

    for part in range(2):
        take(w.inbox.at[part, pl.ds(0, 7)], w.box_r.at[part])
        landed_rows = w.inbox[part].reshape(256, GROUP)
        for g in range(3):
            q = part * 3 + g
            w.rows[0, :, q * GROUP : (q + 1) * GROUP] = jnp.dot(
                squeeze_map(32, 3, g), landed_rows, preferred_element_type=f32
            ).astype(bf)
            for d in range(2):
                gather(d, q, 1).start()
        relay_round(2 + part)
    relay_round(4)

    plane_out, plane_in = (w.plane_out0, w.plane_out1), (w.plane_in0, w.plane_in1)
    plane_ret, plane_back = (w.plane_ret0, w.plane_ret1), (w.plane_back0, w.plane_back1)

    def plane_box(h, i):
        to = lax.rem(e + i, 8)
        return remote(plane_out[h].at[to], plane_in[h].at[e], w.plane_s.at[h], w.plane_r.at[h], exp=to)

    for h, (start, width) in enumerate(SHARES):
        tokens = w.tokens[:, :, start : start + width].reshape(256, width)
        chosen = jnp.dot(w.plane_sel[...], tokens, preferred_element_type=f32).astype(bf)
        plane_out[h][...] = chosen.reshape(8, 80, width)
        for i in range(1, 8):
            plane_box(h, i).start()
        plane_in[h][pl.ds(e, 1)] = plane_out[h][pl.ds(e, 1)]
    pair[1].wait_recv()
    place(w.sg, w.plane_stream, w.ps, 0, kk)
    for copy in local:
        copy.wait()
    for copy in pair[2:5]:
        copy.wait_recv()

    BATCHES = ((0, 4), (5, 3), (4, 1))

    def swap(n):
        slots = pl.ds(*BATCHES[n])
        return remote(w.half.at[slots], w.half_other.at[slots], w.half_s.at[0], w.half_r.at[n], ctx=other)

    def ring_half(slot):
        w.half[slot] = w.half[slot] + jnp.dot(w.rows[slot], w.w_in[0:RING, :], preferred_element_type=f32)

    def second_half(n):
        first, count = BATCHES[n]
        swap(n).wait_recv()
        slots = slice(first, first + count)
        both = (w.half[slots] + w.half_other[slots]).reshape(count * 80, 512)
        gate = both[:, :256]
        hidden = (gate / (1.0 + jnp.exp(-gate)) * both[:, 256:]).astype(bf)
        w.hidden[first * 80 : (first + count) * 80, :] = hidden
        for part in range(2):
            columns = slice(part * 3 * GROUP, (part + 1) * 3 * GROUP)
            out = jnp.dot(hidden, w.w_down[:, columns], preferred_element_type=f32).astype(bf)
            w.total[slots, :, columns] = out.reshape(count, 80, 3 * GROUP)

    def scatter(d, q, j):
        far = reach(d, q) + 1 - j
        slot, to = (far, left) if d == 0 else (8 - far, right)
        columns = pl.ds(q * GROUP, GROUP)
        return remote(w.total.at[slot, :, columns], w.arrived.at[d, q, j - 1], w.rs_s.at[0], w.rs_r.at[d, q, j - 1], ctx=to)

    w.half[...] = jnp.zeros((8, 80, 512), f32)
    ring_half(0)
    def turn_rows(slots):
        for slot in slots:
            w.turn[slot * 80 : (slot + 1) * 80, :] = squeeze_map(80, 8, slot)

    between = {
        (1, 0): lambda: turn_rows((0, 1, 2)),
        (1, 1): lambda: turn_rows((3, 4, 5)),
        (1, 2): lambda: turn_rows((6, 7)),
        (1, 5): lambda: weigh_matrix(chip_table(), w.mix, 3, 32),
        (2, 0): lambda: ring_half(1),
        (2, 1): lambda: ring_half(7),
        (2, 5): lambda: weigh_matrix(w.column[...], w.plane_mix, 8, 80),
        (3, 0): lambda: ring_half(2),
        (3, 1): lambda: ring_half(6),
    }
    for r in range(1, 5):
        for q in range(PIECES):
            for d in range(2):
                if r <= reach(d, q):
                    gather(d, q, r).wait_recv()
                if r + 1 <= reach(d, q):
                    gather(d, q, r + 1).start()
            if (r, q) in between:
                between[r, q]()
        if r == 4:
            ring_half(4)
        if r == 3:
            ring_half(3)
            ring_half(5)
            for h, (start, width) in enumerate(SHARES):
                take(plane_in[h].at[pl.ds(0, 7)], w.plane_r.at[h])
                turned = jnp.dot(w.turn[...], plane_in[h][...].reshape(640, width), preferred_element_type=f32).astype(bf)
                lanes = slice(RING + start, RING + start + width)
                more = jnp.dot(turned, w.w_in[lanes, :], preferred_element_type=f32)
                w.half[...] = w.half[...] + more.reshape(8, 80, 512)
            swap(0).start()
            swap(1).start()
            second_half(0)
            second_half(1)
            for q in range(PIECES):
                for d in range(2):
                    if reach(d, q) == 3:
                        scatter(d, q, 1).start()
    swap(2).start()
    second_half(2)

    def scatter_on(j):
        for q in range(PIECES):
            for d in range(2):
                if j + 1 <= reach(d, q):
                    far = reach(d, q) - j
                    slot = far if d == 0 else 8 - far
                    columns = slice(q * GROUP, (q + 1) * GROUP)
                    scatter(d, q, j).wait_recv()
                    w.total[slot, :, columns] = (
                        w.total[slot, :, columns].astype(f32) + w.arrived[d, q, j - 1].astype(f32)
                    ).astype(bf)
                    scatter(d, q, j + 1).start()

    for q in range(PIECES):
        for d in range(2):
            if reach(d, q) == 4:
                scatter(d, q, 1).start()

    def plane_give(h, i):
        to = lax.rem(e + i, 8)
        return remote(plane_ret[h].at[to], plane_back[h].at[e], w.give_s.at[h], w.give_r.at[h], exp=to)

    hidden = jnp.dot(w.turn[...], w.hidden[...], preferred_element_type=f32).astype(bf)
    for h, (start, width) in enumerate(SHARES):
        out = jnp.dot(hidden, w.w_down[:, RING + start : RING + start + width], preferred_element_type=f32).astype(bf)
        plane_ret[h][...] = out.reshape(8, 80, width)
        for i in range(1, 8):
            plane_give(h, i).start()
        plane_back[h][pl.ds(e, 1)] = plane_ret[h][pl.ds(e, 1)]

    def reduce(d, q, j):
        far = reach(d, q) + 1 - j
        slot, to = (far, left) if d == 0 else (8 - far, right)
        start, width = SUMS[q]
        return remote(
            w.partial.at[slot, :, pl.ds(start, width)], w.plane_arrived.at[d, q, j - 1, :, pl.ds(0, width)],
            w.red_s.at[0], w.red_r.at[d, q, j - 1], ctx=to,
        )

    def straight(slot):
        start, width = SHARES[1]
        return remote(
            w.partial.at[slot, :, pl.ds(start, width)], w.straight_in.at[slot], w.straight_s.at[0], w.straight_r.at[0],
            ctx=2 * lax.rem(z + 8 - slot, 8) + k,
        )

    def reduce_start(h):
        start, width = SHARES[h]
        take(plane_back[h].at[pl.ds(0, 7)], w.give_r.at[h])
        mixed = jnp.dot(w.plane_mix[...], plane_back[h][...].reshape(640, width), preferred_element_type=f32)
        mixed = mixed[:256] + mixed[256:]
        w.plane_own[:, start : start + width] = mixed[:32]
        w.partial[:, :, start : start + width] = mixed.astype(bf).reshape(8, 32, width)
        if h == 0:
            for q in range(2):
                for d in range(2):
                    reduce(d, q, 1).start()
        else:
            for slot in (4, 3, 5, 2, 6, 1, 7):
                straight(slot).start()

    def reduce_on(j):
        for q, (start, width) in enumerate(SUMS):
            for d in range(2):
                if j + 1 <= reach(d, q):
                    far = reach(d, q) - j
                    slot = far if d == 0 else 8 - far
                    columns = slice(start, start + width)
                    reduce(d, q, j).wait_recv()
                    w.partial[slot, :, columns] = (
                        w.partial[slot, :, columns].astype(f32) + w.plane_arrived[d, q, j - 1, :, 0:width].astype(f32)
                    ).astype(bf)
                    reduce(d, q, j + 1).start()

    def keep(whole, start, width):
        whole = whole.astype(bf)
        for b in range(2):
            w.ready[b, :, RING + start : RING + start + width] = whole[b * 16 : (b + 1) * 16]

    def reduce_end():
        for q, (start, width) in enumerate(SUMS):
            columns = slice(start, start + width)
            whole = w.plane_own[:, columns] + w.plane_stream[:, columns].astype(f32)
            for d in range(2):
                reduce(d, q, reach(d, q)).wait_recv()
                whole = whole + w.plane_arrived[d, q, reach(d, q) - 1, :, 0:width].astype(f32)
            keep(whole, start, width)
        for b in range(2):
            hand(2, b, k).start()

    def straight_end():
        start, width = SHARES[1]
        columns = slice(start, start + width)
        whole = w.plane_own[:, columns] + w.plane_stream[:, columns].astype(f32)
        take(w.straight_in.at[pl.ds(0, 7)], w.straight_r.at[0])
        for slot in range(1, 8):
            whole = whole + w.straight_in[slot].astype(f32)
        keep(whole, start, width)
        for b in range(2):
            hand(3, b, k).start()

    def give(part, i):
        to = lax.rem(e + i, 8)
        return remote(w.ret.at[part, to], w.back.at[part, e], w.back_s.at[0], w.back_r.at[part], exp=to)

    def send_back(part):
        spread = jnp.zeros((256, GROUP), f32)
        for g in range(3):
            q = part * 3 + g
            columns = slice(q * GROUP, (q + 1) * GROUP)
            whole = w.total[0, :, columns].astype(f32)
            for d in range(2):
                scatter(d, q, reach(d, q)).wait_recv()
                whole = whole + w.arrived[d, q, reach(d, q) - 1].astype(f32)
            spread = spread + jnp.dot(spread_map(32, 3, g), whole.astype(bf), preferred_element_type=f32)
        w.ret[part] = spread.astype(bf).reshape(8, 32, GROUP)
        for i in range(1, 8):
            give(part, i).start()
        w.back[part, pl.ds(e, 1)] = w.ret[part, pl.ds(e, 1)]

    def hand(part, b, core):
        start, width = HANDS[part]
        columns = pl.ds(start, width)
        return remote(
            w.ready.at[b, :, columns], w.landed.at[core, :, columns], w.fin_s.at[0], w.fin_r.at[0],
            pipe=over, ctx=2 * z + b,
        )

    def finish_ring(part):
        take(w.back.at[part, pl.ds(0, 7)], w.back_r.at[part])
        mixed = jnp.dot(w.mix[...], w.back[part].reshape(256, GROUP), preferred_element_type=f32)
        layer_out = (w.sg[part].astype(f32) + (mixed[:96] + mixed[96:])).astype(bf)
        for g in range(3):
            start = (part * 3 + g) * GROUP
            for b in range(2):
                w.ready[b, :, start : start + GROUP] = layer_out[g * 32 + b * 16 : g * 32 + b * 16 + 16]
        for b in range(2):
            hand(part, b, k).start()

    scatter_on(1)
    scatter_on(2)
    reduce_start(0)
    scatter_on(3)
    reduce_on(1)
    send_back(0)
    send_back(1)
    reduce_on(2)
    reduce_start(1)
    reduce_on(3)
    finish_ring(0)
    reduce_end()
    finish_ring(1)
    straight_end()
    take(w.landed, w.fin_r.at[0])
    for b in range(2):
        out_ref[:, b * HALF : (b + 1) * HALF] = w.landed[b]

    take(w.ready, w.fin_s.at[0])
    for copy in pair:
        copy.wait_send()
    take(w.brief.at[pl.ds(0, 7)], w.table_s.at[0])
    take(w.tokens.at[pl.ds(1, 7)], w.relay_s.at[0])
    take(w.inbox.at[:, pl.ds(0, 7)], w.box_s.at[0])
    take(w.back.at[:, pl.ds(0, 7)], w.back_s.at[0])
    for h in range(2):
        take(plane_out[h].at[pl.ds(0, 7)], w.plane_s.at[h])
        take(plane_ret[h].at[pl.ds(0, 7)], w.give_s.at[h])
    take(w.rows.at[pl.ds(1, 7)], w.ag_s.at[0])
    take(w.total.at[pl.ds(1, 7)], w.rs_s.at[0])
    take(w.half, w.half_s.at[0])
    take(w.partial.at[pl.ds(1, 7), :, pl.ds(0, 896)], w.red_s.at[0])
    take(w.straight_in.at[pl.ds(0, 7)], w.straight_s.at[0])
    settle()


BF, F32 = jnp.bfloat16, jnp.float32
SCRATCH = {
    "keys": ((5, KV + 16, 256), BF), "queries": ((1024, KV), BF), "query_doc": ((128, 128), F32), "top": ((1024, 128), F32),
    "sums": ((1024, 128), F32), "mixed": ((1024, LAT), F32), "value_up": ((8, LAT, 128), BF), "heads": ((8, 128, 1024), BF),
    "proj": ((896, 1024), BF), "proj_all": ((1024, 896), BF), "product": ((8, 128, 896), F32),
    "fold_out": ((8, 64, 896), BF), "fold_in": ((8, 64, 896), BF), "cross_out": ((8, 64, 896), BF),
    "cross_in": ((8, 3, 16, 896), BF), "direct_out": ((128, 896), BF), "direct_in": ((7, 16, 896), BF), "part_out": ((8, 16, 896), BF), "parts": ((8, 16, 896), BF), "stream": ((16, D), BF),
    "table": ((2, 16, 128), F32), "brief": ((8, 8, 128), F32), "column": ((256, 128), F32), "sel": ((256, 96), BF), "mix": ((192, 256), BF), "turn": ((640, 640), BF),
    "plane_sel": ((640, 256), BF), "plane_mix": ((512, 640), BF),
    "normed": ((16, D), BF), "pn": ((16, HALF), BF), "ps": ((16, HALF), BF), "tokens": ((8, 32, PLANE), BF),
    "xg": ((2, 96, GROUP), BF), "sg": ((2, 96, GROUP), BF), "plane_stream": ((32, PLANE), BF),
    "outbox": ((2, 8, 32, GROUP), BF), "inbox": ((2, 8, 32, GROUP), BF), "ret": ((2, 8, 32, GROUP), BF),
    "back": ((2, 8, 32, GROUP), BF), "plane_out0": ((8, 80, 896), BF), "plane_in0": ((8, 80, 896), BF),
    "plane_ret0": ((8, 80, 896), BF), "plane_back0": ((8, 80, 896), BF), "plane_out1": ((8, 80, 384), BF),
    "plane_in1": ((8, 80, 384), BF), "plane_ret1": ((8, 80, 384), BF), "plane_back1": ((8, 80, 384), BF),
    "straight_in": ((8, 32, 384), BF),
    "w_in": ((HALF, 512), BF), "w_down": ((256, HALF), BF), "rows": ((8, 80, RING), BF),
    "half": ((8, 80, 512), F32), "half_other": ((8, 80, 512), F32), "hidden": ((640, 256), BF), "total": ((8, 80, RING), BF),
    "arrived": ((2, PIECES, 4, 80, GROUP), BF), "partial": ((8, 32, PLANE), BF), "plane_own": ((32, PLANE), F32),
    "plane_arrived": ((2, 2, 4, 32, 512), BF), "ready": ((2, 16, HALF), BF), "landed": ((2, 16, HALF), BF),
    "load": ((2,), None), "chain_s": ((1,), None), "chain_r": ((4, 4), None), "share_s": ((1,), None), "share_r": ((5,), None),
    "proj_s": ((1,), None), "proj_r": ((1,), None), "head_s": ((1,), None), "head_r": ((2, 2, 4), None),
    "fold_s": ((1,), None), "fold_r": ((8,), None), "cross_s": ((1,), None), "cross_r": ((8,), None),
    "part_s": ((1,), None), "part_r": ((1,), None), "direct_s": ((1,), None), "direct_r": ((1,), None),
    "pair_s": ((6,), None), "pair_r": ((6,), None), "loc": ((3,), None), "table_s": ((1,), None), "table_r": ((1,), None),
    "box_s": ((1,), None), "box_r": ((2,), None), "relay_s": ((1,), None), "relay_r": ((2, 2, 4), None),
    "plane_s": ((2,), None), "plane_r": ((2,), None), "give_s": ((2,), None), "give_r": ((2,), None),
    "ag_s": ((1,), None), "ag_r": ((2, PIECES, 4), None), "half_s": ((1,), None), "half_r": ((3,), None),
    "rs_s": ((1,), None), "rs_r": ((2, PIECES, 4), None), "red_s": ((1,), None), "red_r": ((2, 2, 4), None),
    "straight_s": ((1,), None), "straight_r": ((1,), None), "back_s": ((1,), None), "back_r": ((2,), None),
    "fin_s": ((1,), None), "fin_r": ((1,), None),
}


def on_device(
    queries, latent_rows, doc_ids, value_up, out_proj, residual_in, norm_gain, expert_ids, gate_weights, gate_proj, up_proj,
    down_proj,
):
    vmem, any_space = pl.BlockSpec(memory_space=pltpu.VMEM), pl.BlockSpec(memory_space=pl.ANY)
    return pl.pallas_call(
        layer_kernel,
        out_shape=jax.ShapeDtypeStruct((16, D), BF),
        in_specs=[vmem] * 7 + [any_space] * 5,
        out_specs=vmem,
        scratch_shapes=[
            pltpu.SemaphoreType.DMA(shape) if kind is None else pltpu.VMEM(shape, kind) for shape, kind in SCRATCH.values()
        ],
        compiler_params=pltpu.CompilerParams(collective_id=1, has_side_effects=True, vmem_limit_bytes=60 << 20),
        cost_estimate=pl.CostEstimate(flops=8_000_000_000, bytes_accessed=10_000_000, transcendentals=2_000_000),
        name="layer",
    )(
        queries[0].transpose(1, 2, 0), latent_rows[0].T, doc_ids, expert_ids[0].T, gate_weights[0].T, residual_in[0], norm_gain,
        value_up[0], out_proj[0].T, gate_proj[0, 0], up_proj[0, 0], down_proj[0, 0],
    )[None]


def solution(mesh):
    return jax.shard_map(
        on_device,
        mesh=mesh,
        in_specs=(
            P("pipe", "ctx", "exp", None),
            P("pipe", "ctx", None),
            P("pipe", "ctx"),
            P("pipe", "exp", None, None),
            P("pipe", "exp", "ctx"),
            P("pipe", ("ctx", "exp"), None),
            P("pipe", None),
            P("pipe", ("ctx", "exp"), None),
            P("pipe", ("ctx", "exp"), None),
            P("pipe", "exp", None, "ctx"),
            P("pipe", "exp", None, "ctx"),
            P("pipe", "exp", "ctx", None),
        ),
        out_specs=P("pipe", ("ctx", "exp"), None),
        check_vma=False,
    )
```
